128 devices in a mesh: rows: 16 (over z, y_hi, core), seq: 8 (over y_lo, x).
Axes of the slice: x: 4, y: 4 (y_hi: 2, y_lo: 2; y = y_hi * 2 + y_lo), z: 4, core: 2. Of those that a mesh axis runs over, the one named last changes fastest.
Arguments:
- inputs: bfloat16 [32, 1024, 768], P('rows', 'seq'), may hold values from -6 to 6
- lengths: int32 [32], P('rows'), may hold values from 128 to 1024, as said below
- qkv_weight: float32 [768, 3, 768], P(('rows', 'seq')), may hold values from -0.3125 to 0.3125
- out_weight: float32 [768, 768], P(('rows', 'seq')), may hold values from -0.875 to 0.875
- up_weight: float32 [768, 3072], P(('rows', 'seq')), may hold values from -0.21875 to 0.21875
- down_weight: float32 [3072, 768], P(('rows', 'seq')), may hold values from -0.21875 to 0.21875
- ln1_gain: float32 [768], P(('rows', 'seq')), may hold values from 0.25 to 1.75
- ln1_bias: float32 [768], P(('rows', 'seq')), may hold values from -1.5 to 1.5
- ln2_gain: float32 [768], P(('rows', 'seq')), may hold values from 0.25 to 1.75
- ln2_bias: float32 [768], P(('rows', 'seq')), may hold values from -1.5 to 1.5
- cotangent: bfloat16 [32, 1024, 768], P('rows', 'seq'), may hold values from -6 to 6
Outputs:
- output: bfloat16 [32, 1024, 768], P('rows', 'seq')
- input_grad: float32 [32, 1024, 768], P('rows', 'seq')
- qkv_grad: float32 [768, 3, 768], P(('rows', 'seq'))
- out_grad: float32 [768, 768], P(('rows', 'seq'))
- up_grad: float32 [768, 3072], P(('rows', 'seq'))
- down_grad: float32 [3072, 768], P(('rows', 'seq'))
- ln1_gain_grad: float32 [768], P(('rows', 'seq'))
- ln1_bias_grad: float32 [768], P(('rows', 'seq'))
- ln2_gain_grad: float32 [768], P(('rows', 'seq'))
- ln2_bias_grad: float32 [768], P(('rows', 'seq'))
The draws below stay inside these ranges and needn't reach their ends.
Inputs may be any that keep to these rules, and one draw needn't show every extreme that they name: `lengths`: each row's count of valid tokens: keys at or past it are padding; in every draw one row holds exactly 1024 and another exactly 128.
All inputs are finite; a program needn't handle non-finite values.
Results may differ from the reference program's by a relative error of at most 0.017.
The reference program's roundings to bfloat16 on the way count: a program that leaves them out, or rounds other values in their place, can miss the bound.
Values may be sent and summed in bfloat16 or wider, within the bound.
A program may use at most 128 MiB of HBM per device.

```python
import math
import jax
import jax.numpy as jnp
from jax import lax

D = 768
HEADS = 24
HEAD_DIM = 32
FF = 3072
SEQ_LEN = 1024
BATCH_ROWS = 32


def draw_lengths(key, part):
    first, second, third = jax.random.split(jax.random.fold_in(key, 11), 3)
    valid = jax.random.randint(first, (BATCH_ROWS,), SEQ_LEN // 8, SEQ_LEN + 1)
    longest = jax.random.randint(second, (), 0, BATCH_ROWS)
    shortest = (longest + jax.random.randint(third, (), 1, BATCH_ROWS)) % BATCH_ROWS
    valid = valid.at[longest].set(SEQ_LEN).at[shortest].set(SEQ_LEN // 8)
    return valid.astype(jnp.int32)


def level_of(key, shape, pieces, least, high):
    factor_of = 1.0
    for dim, blocks in pieces:
        steps = jax.random.uniform(jax.random.fold_in(jax.random.fold_in(key, 6), dim), (blocks,), jnp.float32, least / len(pieces), high / len(pieces))
        factor_of = factor_of * jnp.repeat(jnp.exp(steps), shape[dim] // blocks).reshape((-1,) + (1,) * (len(shape) - 1 - dim))
    return factor_of


def noise(own_key, dims, width, limit, cuts=(), kind=jnp.bfloat16):
    values = width * jax.random.normal(own_key, dims, jnp.float32)
    if cuts:
        values = values * level_of(own_key, dims, cuts, -0.22, 0.18)
    return jnp.clip(values, -limit, limit).astype(kind)


def setup_inputs(seed: int = 0) -> dict:
    key_list = jax.random.split(jax.random.key(seed), 12)
    return {
        "inputs": noise(key_list[0], (BATCH_ROWS, SEQ_LEN, D), 1.0, 6.0, ((0, 16), (1, 8))),
        "lengths": draw_lengths(jax.random.fold_in(key_list[11], 71), 0),
        "qkv_weight": noise(key_list[2], (D, 3, D), (D // 2) ** -0.5, 0.3125, ((0, 128),), jnp.float32),
        "out_weight": noise(key_list[3], (D, D), (D // 16) ** -0.5, 0.875, ((0, 128),), jnp.float32),
        "up_weight": noise(key_list[4], (D, FF), D ** -0.5, 0.21875, ((0, 128),), jnp.float32),
        "down_weight": noise(key_list[5], (FF, D), (FF // 4) ** -0.5, 0.21875, ((0, 128),), jnp.float32),
        "ln1_gain": jnp.clip(1.0 + 0.15 * jax.random.normal(key_list[6], (D,), jnp.float32), 0.25, 1.75),
        "ln1_bias": noise(key_list[7], (D,), 0.3, 1.5, ((0, 128),), jnp.float32),
        "ln2_gain": jnp.clip(1.0 + 0.15 * jax.random.normal(key_list[8], (D,), jnp.float32), 0.25, 1.75),
        "ln2_bias": noise(key_list[9], (D,), 0.3, 1.5, ((0, 128),), jnp.float32),
        "cotangent": noise(key_list[10], (BATCH_ROWS, SEQ_LEN, D), 1.0, 6.0, ((0, 16), (1, 8))),
    }


EPS = 1e-05
HIGH = lax.Precision.HIGHEST

@jax.custom_vjp
def low(v):
    return lax.optimization_barrier(v.astype(jnp.bfloat16)).astype(jnp.float32)

@jax.custom_vjp
def low_back(v):
    return v

def low_keep(v):
    return (low(v), None)

def low_pass(kept, grad):
    return (grad,)

def back_keep(v):
    return (v, None)

def back_low(kept, grad):
    return (low(grad),)
low.defvjp(low_keep, low_pass)
low_back.defvjp(back_keep, back_low)

def layer_norm(value, gain, bias):
    mean = lax.optimization_barrier(jnp.mean(value, axis=-1, keepdims=True))
    centred = value - mean
    var = lax.optimization_barrier(jnp.mean(centred * centred, axis=-1, keepdims=True))
    return centred * lax.rsqrt(var + EPS) * gain + bias

def attend_row(query, keys, values, length):
    scores = jnp.einsum('qhe,khe->hqk', query, keys, precision=HIGH) * HEAD_DIM ** (-0.5)
    scores = low_back(scores)
    places = jnp.arange(SEQ_LEN, dtype=jnp.int32)
    allowed = (places[None, :] <= places[:, None]) & (places[None, :] < length)
    scores = jnp.where(allowed[None], scores, -1e+30)
    probs = jax.nn.softmax(scores, axis=-1)
    return jnp.einsum('hqk,khe->qhe', low(probs), values, precision=HIGH)
attend_checked = jax.checkpoint(attend_row)

def forward(x, lens, qkv_w, out_w, up_w, down_w, g1, b1, g2, b2):
    count = x.shape[0]
    h1 = low(layer_norm(x, low(g1), low(b1)))
    qkv = low(low_back(jnp.einsum('rsd,dcf->rscf', h1, low(qkv_w), precision=HIGH)))
    shape = (count, SEQ_LEN, HEADS, HEAD_DIM)
    query = qkv[:, :, 0].reshape(shape)
    keys = qkv[:, :, 1].reshape(shape)
    values = qkv[:, :, 2].reshape(shape)
    mixed = lax.map(lambda args: attend_checked(*args), (query, keys, values, lens))
    mixed = low(low_back(mixed.reshape(count, SEQ_LEN, D)))
    attn = low_back(jnp.einsum('rsd,df->rsf', mixed, low(out_w), precision=HIGH))
    x1 = x + attn
    h2 = low(layer_norm(x1, low(g2), low(b2)))
    pre = low_back(jnp.einsum('rsd,df->rsf', h2, low(up_w), precision=HIGH))
    act = low(jax.nn.gelu(pre, approximate=False))
    branch = low_back(jnp.einsum('rsf,fd->rsd', act, low(down_w), precision=HIGH))
    return x1 + branch

def reference(inputs, lengths, qkv_weight, out_weight, up_weight, down_weight, ln1_gain, ln1_bias, ln2_gain, ln2_bias, cotangent):
    per_block = math.gcd(BATCH_ROWS, max(1, 4096 // SEQ_LEN))
    blocks = BATCH_ROWS // per_block
    xs = inputs.astype(jnp.float32).reshape(blocks, per_block, SEQ_LEN, D)
    dys = cotangent.astype(jnp.float32).reshape(blocks, per_block, SEQ_LEN, D)
    lens = lengths.astype(jnp.int32).reshape(blocks, per_block)
    params = (qkv_weight, out_weight, up_weight, down_weight, ln1_gain, ln1_bias, ln2_gain, ln2_bias)

    def step(totals, block):
        x, lens_block, dy = block
        result, pull = jax.vjp(lambda xx, *p: forward(xx, lens_block, *p), x, *params)
        grads = pull(dy)
        totals = tuple((t + g for t, g in zip(totals, grads[1:])))
        return (totals, (result, grads[0]))
    start = tuple((jnp.zeros_like(p) for p in params))
    totals, (results, dxs) = lax.scan(step, start, (xs, lens, dys))
    output = results.reshape(BATCH_ROWS, SEQ_LEN, D).astype(jnp.bfloat16)
    input_grad = dxs.reshape(BATCH_ROWS, SEQ_LEN, D)
    return (output, input_grad, totals[0], totals[1], totals[2], totals[3], totals[4], totals[5], totals[6], totals[7])
```

```python
import functools
import math

import jax
import jax.numpy as jnp
import numpy as np
from jax import lax
from jax.experimental import pallas as pl
from jax.experimental.pallas import tpu as pltpu
from jax.sharding import PartitionSpec as P

MESH = pl.DeviceIdType.MESH
BF = jnp.bfloat16
F32 = jnp.float32
HEAD_DIM = 32
EPS = 1e-05
ROWS_A = 208
ROWS_B = 384
VM = pl.BlockSpec(memory_space=pltpu.VMEM)
SM = pl.BlockSpec(memory_space=pltpu.SMEM)


def perm_a():
    m = np.zeros((ROWS_A, 256), np.float32)
    for c in range(4):
        for s in range(8):
            for i in range(6):
                m[c * 48 + s * 6 + i, s * 32 + c * 6 + i] = 1
    for s in range(8):
        m[192 + s, s * 32 + 24] = 1
    return m


def perm_b():
    m = np.zeros((ROWS_B, 384), np.float32)
    for s in range(8):
        for j in range(4):
            for i in range(6):
                m[j * 48 + s * 6 + i, s * 48 + j * 6 + i] = 1
        for i in range(24):
            m[192 + s * 24 + i, s * 48 + 24 + i] = 1
    return m


def spread_m():
    m = np.zeros((256, 768), np.float32)
    for r in range(16):
        for s in range(8):
            m[r * 16 + s, (r * 8 + s) * 6 : (r * 8 + s) * 6 + 6] = 1
    return m


def spread_e():
    m = np.zeros((128, 768), np.float32)
    for j in range(768):
        m[j % 6, j] = 1
    return m


def const(m):
    return jnp.asarray(m, BF)


def nn(a, b):
    return lax.dot_general(a, b, (((1,), (0,)), ((), ())), preferred_element_type=F32)


def nt(a, b):
    return lax.dot_general(a, b, (((1,), (1,)), ((), ())), preferred_element_type=F32)


def tn(a, b):
    return lax.dot_general(a, b, (((0,), (0,)), ((), ())), preferred_element_type=F32)


class Place:
    def __init__(self):
        self.r = lax.axis_index("rows")
        self.s = lax.axis_index("seq")
        self.z = self.r // 4
        self.y = (self.r // 2) % 2
        self.c = self.r % 2

    def slot(self, dz, dy, dc):
        z = (self.z + dz) % 4
        y = (self.y + dy) % 2
        c = (self.c + dc) % 2
        return z * 4 + y * 2 + c

    def row_dev(self, dz, dy, dc):
        return {"rows": self.slot(dz, dy, dc)}

    def seq_at(self, d):
        return (self.s + d) % 8

    def seq_dev(self, d):
        return {"seq": self.seq_at(d)}


ROW_PEERS = ((0, 0, 1), (0, 1, 0), (1, 0, 0), (3, 0, 0))


def barrier(me):
    sem = pltpu.get_barrier_semaphore()
    for p in ROW_PEERS:
        pl.semaphore_signal(sem, inc=1, device_id=me.row_dev(*p), device_id_type=MESH)
    for d in range(1, 8):
        pl.semaphore_signal(sem, inc=1, device_id=me.seq_dev(d), device_id_type=MESH)
    pl.semaphore_wait(sem, len(ROW_PEERS) + 7)


def remote(src, dst, ss, rs, dev):
    return pltpu.make_async_remote_copy(
        src_ref=src, dst_ref=dst, send_sem=ss, recv_sem=rs, device_id=dev, device_id_type=MESH
    )


class Exchange:
    def __init__(self, me, src, dst, land, ss, rs, base):
        self.me, self.src, self.dst, self.land = me, src, dst, land
        self.ss, self.rs, self.base = ss, rs, base

    def _copy(self, d):
        return remote(
            self.src(d),
            self.dst(d),
            self.ss.at[self.base + d - 1],
            self.rs.at[self.base + d - 1],
            self.me.seq_dev(d),
        )

    def start(self):
        for d in range(1, 8):
            self._copy(d).start()

    def wait_recv(self):
        for d in range(1, 8):
            here = self.land(d)
            remote(
                here, here, self.ss.at[self.base + d - 1], self.rs.at[self.base + d - 1], self.me.seq_dev(d)
            ).wait_recv()

    def wait_send(self):
        for d in range(1, 8):
            self._copy(d).wait_send()


GATHER_SEMS = 17


class RowsGather:
    def __init__(self, me, buf, cut, ss, rs, base):
        self.me, self.buf, self.cut = me, buf, cut
        self.ss, self.rs, self.base = ss, rs, base
        self.sent = []

    def _part(self, rel, part):
        slot = self.me.slot(*rel)
        full = self.buf.shape[1]
        if part == 0:
            return self.buf.at[slot]
        if part == 1:
            return self.buf.at[slot, pl.ds(0, self.cut)]
        return self.buf.at[slot, pl.ds(self.cut, full - self.cut)]

    PLAN = {
        "y": (0, (0, 1, 0), (0, 0, 0), 0),
        "p0": (1, (1, 0, 0), (0, 0, 0), 0),
        "m0": (2, (3, 0, 0), (0, 0, 0), 0),
        "p1": (3, (1, 0, 0), (0, 1, 0), 0),
        "m1": (4, (3, 0, 0), (0, 1, 0), 0),
        "fp0": (5, (1, 0, 0), (3, 0, 0), 1),
        "fm0": (6, (3, 0, 0), (1, 0, 0), 2),
        "fp1": (7, (1, 0, 0), (3, 1, 0), 1),
        "fm1": (8, (3, 0, 0), (1, 1, 0), 2),
        "c00": (9, (0, 0, 1), (0, 0, 0), 0),
        "c01": (10, (0, 0, 1), (0, 1, 0), 0),
        "c10": (11, (0, 0, 1), (1, 0, 0), 0),
        "c11": (12, (0, 0, 1), (1, 1, 0), 0),
        "c20": (13, (0, 0, 1), (2, 0, 0), 0),
        "c21": (14, (0, 0, 1), (2, 1, 0), 0),
        "c30": (15, (0, 0, 1), (3, 0, 0), 0),
        "c31": (16, (0, 0, 1), (3, 1, 0), 0),
    }

    def _send(self, name):
        i, to, block, part = self.PLAN[name]
        ref = self._part(block, part)
        return remote(ref, ref, self.ss.at[self.base + i], self.rs.at[self.base + i], self.me.row_dev(*to))

    def send(self, *names):
        for name in names:
            self._send(name).start()
            self.sent.append(name)

    def recv(self, *names):
        for name in names:
            i, to, block, part = self.PLAN[name]
            rel = ((block[0] - to[0]) % 4, (block[1] - to[1]) % 2, (block[2] - to[2]) % 2)
            ref = self._part(rel, part)
            remote(ref, ref, self.ss.at[self.base + i], self.rs.at[self.base + i], self.me.row_dev(*to)).wait_recv()

    def step0(self):
        self.send("y", "p0", "m0", "c00")

    def step1(self):
        self.recv("y")
        self.send("p1", "m1", "c01")

    def step2(self):
        self.recv("p0")
        self.send("fp0", "c30")
        self.recv("m0")
        self.send("fm0", "c10")

    def step3(self):
        self.recv("p1")
        self.send("fp1", "c31")
        self.recv("m1")
        self.send("fm1", "c11")

    def step4(self):
        self.recv("fp0", "fm0")
        self.send("c20")

    def step5(self):
        self.recv("fp1", "fm1")
        self.send("c21")

    def step6(self):
        self.recv("c00", "c01", "c10", "c11", "c20", "c21", "c30", "c31")

    def finish(self):
        for name in self.sent:
            self._send(name).wait_send()

    def steps(self):
        return [self.step0, self.step1, self.step2, self.step3, self.step4, self.step5, self.step6]


SCATTER_SEMS = 15


class RowsScatter:
    def __init__(self, me, g, cr, zlo, zhi, zr, yr, cut, ss, rs, base):
        self.me, self.g, self.cr, self.zlo, self.zhi, self.zr, self.yr = me, g, cr, zlo, zhi, zr, yr
        self.cut, self.ss, self.rs, self.base = cut, ss, rs, base
        self.full = g.shape[1]
        self.open = []

    def _copy(self, i, src, dst, to):
        return remote(src, dst, self.ss.at[self.base + i], self.rs.at[self.base + i], self.me.row_dev(*to))

    def _start(self, i, src, dst, to):
        copy = self._copy(i, src, dst, to)
        copy.start()
        self.open.append(copy)

    def _landed(self, i, dst, to):
        self._copy(i, dst, dst, to).wait_recv()

    ORDER = ((2, 0), (2, 1), (1, 0), (1, 1), (3, 0), (3, 1), (0, 1), (0, 0))

    def start_core(self, which=None):
        for k, (dz, dy) in enumerate(self.ORDER):
            self._start(k, self.g.at[self.me.slot(dz, dy, 1)], self.cr.at[k], (0, 0, 1))

    def _add(self, k):
        dz, dy = self.ORDER[k]
        self._landed(k, self.cr.at[k], (0, 0, 1))
        slot = self.me.slot(dz, dy, 0)
        self.g[slot] = (self.g[slot].astype(F32) + self.cr[k].astype(F32)).astype(BF)

    def add_far(self):
        lo, hi = pl.ds(0, self.cut), pl.ds(self.cut, self.full - self.cut)
        for dy in (0, 1):
            self._add(dy)
            slot = self.me.slot(2, dy, 0)
            self._start(8 + dy, self.g.at[slot, lo], self.zlo.at[dy], (1, 0, 0))
            self._start(10 + dy, self.g.at[slot, hi], self.zhi.at[dy], (3, 0, 0))

    def add_near(self):
        for k in (2, 3, 4, 5):
            self._add(k)

    def pass_near(self):
        lo, hi = pl.ds(0, self.cut), pl.ds(self.cut, self.full - self.cut)
        for dy in (0, 1):
            self._landed(8 + dy, self.zlo.at[dy], (1, 0, 0))
            slot = self.me.slot(1, dy, 0)
            self.g[slot, lo] = (self.g[slot, lo].astype(F32) + self.zlo[dy].astype(F32)).astype(BF)
            self._landed(10 + dy, self.zhi.at[dy], (3, 0, 0))
            slot = self.me.slot(3, dy, 0)
            self.g[slot, hi] = (self.g[slot, hi].astype(F32) + self.zhi[dy].astype(F32)).astype(BF)
        both = self.me.y == 0
        p0, p1 = self.me.slot(1, 0, 0), self.me.slot(1, 1, 0)
        m0, m1 = self.me.slot(3, 0, 0), self.me.slot(3, 1, 0)
        self._start(12, self.g.at[p1], self.zr.at[0, 1], (1, 0, 0))
        self._start(13, self.g.at[m1], self.zr.at[1, 1], (3, 0, 0))
        self._start(14, self.g.at[p0], self.zr.at[0, 0], (1, 0, 0))
        self._start(15, self.g.at[m0], self.zr.at[1, 0], (3, 0, 0))

    def own_core(self):
        self._add(6)
        self._add(7)

    def cross(self):
        self._landed(12, self.zr.at[0, 1], (1, 0, 0))
        self._landed(13, self.zr.at[1, 1], (3, 0, 0))
        slot = self.me.slot(0, 1, 0)
        total = self.g[slot].astype(F32) + self.zr[0, 1].astype(F32) + self.zr[1, 1].astype(F32)
        self.g[slot] = total.astype(BF)
        self._start(16, self.g.at[slot], self.yr, (0, 1, 0))

    def last(self):
        self._landed(14, self.zr.at[0, 0], (1, 0, 0))
        self._landed(15, self.zr.at[1, 0], (3, 0, 0))
        self._landed(16, self.yr, (0, 1, 0))
        slot = self.me.slot(0, 0, 0)
        return (
            self.g[slot].astype(F32)
            + self.zr[0, 0].astype(F32)
            + self.zr[1, 0].astype(F32)
            + self.yr[...].astype(F32)
        )

    def finish(self):
        for copy in self.open:
            copy.wait_send()


SCATTER_SEMS = 17


def small_vec(ref, row):
    lane = lax.broadcasted_iota(jnp.int32, (1, 128), 1)
    out = jnp.zeros((1, 128), F32)
    for i in range(6):
        out = jnp.where(lane == i, ref[i], out)
    return out


def normalise(v):
    mean = jnp.mean(v, axis=-1, keepdims=True)
    centred = v - mean
    var = jnp.mean(centred * centred, axis=-1, keepdims=True)
    inverse = lax.rsqrt(var + EPS)
    return centred * inverse, inverse


def gather_kernel(
    x_ref, wqkv_ref, wo_ref, wu_ref, wd_ref, g1_ref, b1_ref, g2_ref, b2_ref,
    pa_ref, pb_ref, sm_ref, se_ref,
    ga_ref, gb_ref, lnp_ref, h1_ref, heads_ref,
    f_ref, ka_ref, kb_ref, xa_ref, xb_ref, out_ref,
    ss, rs,
):
    me = Place()
    f_ref[...] = jnp.zeros_like(f_ref)
    for c in range(3):
        for i in range(6):
            f_ref[pl.ds(c * 6 + i, 1), :] = wqkv_ref[i, pl.ds(c, 1), :]
    f_ref[pl.ds(18, 6), :] = wo_ref[...]
    for p, ref in enumerate((g1_ref, b1_ref, g2_ref, b2_ref)):
        f_ref[pl.ds(24, 1), pl.ds(p * 128, 128)] = small_vec(ref, p)
    for j in range(4):
        f_ref[pl.ds(32 + j * 6, 6), :] = wu_ref[:, pl.ds(j * 768, 768)]
    f_ref[pl.ds(56, 24), :] = wd_ref[...]
    ka_ref[...] = f_ref[pl.ds(0, 32), :].astype(BF)
    kb_ref[...] = f_ref[pl.ds(32, 48), :].astype(BF)

    barrier(me)
    xch_a = Exchange(me, lambda d: ka_ref, lambda d: xa_ref.at[me.s], lambda d: xa_ref.at[me.seq_at(8 - d)], ss, rs, 0)
    xch_b = Exchange(me, lambda d: kb_ref, lambda d: xb_ref.at[me.s], lambda d: xb_ref.at[me.seq_at(8 - d)], ss, rs, 7)
    xch_a.start()
    xch_b.start()
    xa_ref[me.s] = ka_ref[...]
    xb_ref[me.s] = kb_ref[...]
    x = x_ref[...].reshape(256, 768).astype(F32)
    xhat, _ = normalise(x)

    ag_a = RowsGather(me, ga_ref, 112, ss, rs, 14)
    ag_b = RowsGather(me, gb_ref, 192, ss, rs, 14 + GATHER_SEMS)
    xch_a.wait_recv()
    ga_ref[me.r] = nn(pa_ref[...], xa_ref[...].reshape(256, 768)).astype(BF)
    ag_a.step0()
    xch_b.wait_recv()
    gb_ref[me.r] = nn(pb_ref[...], xb_ref[...].reshape(384, 768)).astype(BF)
    for step in ag_a.steps()[1:4]:
        step()
    ag_b.step0()
    for step in ag_a.steps()[4:]:
        step()

    ln = ga_ref[:, pl.ds(192, 16), :].reshape(256, 768)
    for p in range(4):
        spread = nn(ln[:, p * 128 : (p + 1) * 128], se_ref[...])
        lnp_ref[pl.ds(p, 1), :] = jnp.sum(spread * sm_ref[...].astype(F32), axis=0, keepdims=True)
    lnp_ref[pl.ds(4, 4), :] = jnp.zeros((4, 768), F32)
    h1 = (xhat * lnp_ref[pl.ds(0, 1), :] + lnp_ref[pl.ds(1, 1), :]).astype(BF)
    h1_ref[...] = h1
    for c in range(3):
        w = ga_ref[:, pl.ds(c * 48, 48), :].reshape(768, 768)
        val = nn(h1, w).T.astype(BF)
        for k in range(8):
            for b in range(2):
                out_ref[k, b, c] = val[k * 96 : (k + 1) * 96, b * 128 : (b + 1) * 128]
    xq = [
        Exchange(
            me,
            lambda d, b=b: out_ref.at[me.seq_at(d), b],
            lambda d, b=b: heads_ref.at[b, me.s],
            lambda d, b=b: heads_ref.at[b, me.seq_at(8 - d)],
            ss,
            rs,
            14 + 2 * GATHER_SEMS + 7 * b,
        )
        for b in range(2)
    ]
    for b in range(2):
        xq[b].start()
        heads_ref[b, me.s] = out_ref[me.s, b]
    for step in ag_b.steps()[1:]:
        step()
    for b in range(2):
        xq[b].wait_recv()
    for each in (xch_a, xch_b, xq[0], xq[1]):
        each.wait_send()
    ag_a.finish()
    ag_b.finish()


def gather_call(x, wqkv, wo, wu, wd, g1, b1, g2, b2):
    n = 14 + 2 * GATHER_SEMS + 14
    return pl.pallas_call(
        gather_kernel,
        out_shape=(
            jax.ShapeDtypeStruct((16, ROWS_A, 768), BF),
            jax.ShapeDtypeStruct((16, ROWS_B, 768), BF),
            jax.ShapeDtypeStruct((8, 768), F32),
            jax.ShapeDtypeStruct((256, 768), BF),
            jax.ShapeDtypeStruct((2, 8, 3, 96, 128), BF),
        ),
        in_specs=[VM] * 5 + [SM] * 4 + [VM] * 4,
        out_specs=[VM] * 5,
        scratch_shapes=[
            pltpu.VMEM((80, 768), F32),
            pltpu.VMEM((32, 768), BF),
            pltpu.VMEM((48, 768), BF),
            pltpu.VMEM((8, 32, 768), BF),
            pltpu.VMEM((8, 48, 768), BF),
            pltpu.VMEM((8, 2, 3, 96, 128), BF),
            pltpu.SemaphoreType.DMA((n,)),
            pltpu.SemaphoreType.DMA((n,)),
        ],
        compiler_params=pltpu.CompilerParams(
            collective_id=0, has_side_effects=True, vmem_limit_bytes=48 * 1024 * 1024
        ),
        name="gather",
    )(x, wqkv, wo, wu, wd, g1, b1, g2, b2, const(perm_a()), const(perm_b()), const(spread_m()), const(spread_e()))


def scatter_kernel(
    grads_ref, pa_ref, pb_ref,
    dqkv_ref, dwo_ref, dwu_ref, dwd_ref, dln_ref,
    g_ref, cr_ref, zlo_ref, zhi_ref, zr_ref, yr_ref, pk_ref, xs_ref, f_ref,
    ss, rs, ls,
):
    me = Place()
    load = pltpu.make_async_copy(grads_ref, g_ref, ls)
    load.start()
    barrier(me)
    load.wait()
    sc = RowsScatter(me, g_ref, cr_ref, zlo_ref, zhi_ref, zr_ref, yr_ref, 304, ss, rs, 0)
    sc.start_core()
    sc.add_far()
    sc.add_near()
    sc.pass_near()
    sc.own_core()
    sc.cross()
    total = sc.last().astype(BF)
    pk_ref[:, pl.ds(0, 32), :] = tn(pa_ref[...], total[0:ROWS_A]).astype(BF).reshape(8, 32, 768)
    pk_ref[:, pl.ds(32, 48), :] = tn(pb_ref[...], total[ROWS_A:]).astype(BF).reshape(8, 48, 768)
    xch = Exchange(
        me, lambda d: pk_ref.at[me.seq_at(d)], lambda d: xs_ref.at[me.s], lambda d: xs_ref.at[me.seq_at(8 - d)],
        ss, rs, SCATTER_SEMS,
    )
    xch.start()
    xs_ref[me.s] = pk_ref[me.s]
    xch.wait_recv()
    f_ref[...] = jnp.sum(xs_ref[...].astype(F32), axis=0)
    for c in range(3):
        for i in range(6):
            dqkv_ref[i, pl.ds(c, 1), :] = f_ref[pl.ds(c * 6 + i, 1), :]
    dwo_ref[...] = f_ref[pl.ds(18, 6), :]
    dln_ref[...] = f_ref[pl.ds(24, 8), :]
    for j in range(4):
        dwu_ref[:, pl.ds(j * 768, 768)] = f_ref[pl.ds(32 + j * 6, 6), :]
    dwd_ref[...] = f_ref[pl.ds(56, 24), :]
    xch.wait_send()
    sc.finish()


def scatter_call(grads):
    n = SCATTER_SEMS + 7
    rows = ROWS_A + ROWS_B
    return pl.pallas_call(
        scatter_kernel,
        out_shape=(
            jax.ShapeDtypeStruct((6, 3, 768), F32),
            jax.ShapeDtypeStruct((6, 768), F32),
            jax.ShapeDtypeStruct((6, 3072), F32),
            jax.ShapeDtypeStruct((24, 768), F32),
            jax.ShapeDtypeStruct((8, 768), F32),
        ),
        in_specs=[pl.BlockSpec(memory_space=pl.ANY), VM, VM],
        out_specs=[VM] * 5,
        scratch_shapes=[
            pltpu.VMEM((16, rows, 768), BF),
            pltpu.VMEM((8, rows, 768), BF),
            pltpu.VMEM((2, 304, 768), BF),
            pltpu.VMEM((2, rows - 304, 768), BF),
            pltpu.VMEM((2, 2, rows, 768), BF),
            pltpu.VMEM((rows, 768), BF),
            pltpu.VMEM((8, 80, 768), BF),
            pltpu.VMEM((8, 80, 768), BF),
            pltpu.VMEM((80, 768), F32),
            pltpu.SemaphoreType.DMA((n,)),
            pltpu.SemaphoreType.DMA((n,)),
            pltpu.SemaphoreType.DMA,
        ],
        compiler_params=pltpu.CompilerParams(
            collective_id=1, has_side_effects=True, vmem_limit_bytes=56 * 1024 * 1024
        ),
        name="scatter",
    )(grads, const(perm_a()), const(perm_b()))


def row_scores(query, keys, length):
    scores = jnp.einsum("qhe,khe->hqk", query, keys, preferred_element_type=F32) * HEAD_DIM ** (-0.5)
    places = jnp.arange(query.shape[0], dtype=jnp.int32)
    allowed = (places[None, :] <= places[:, None]) & (places[None, :] < length)
    return jnp.where(allowed[None], scores, -1e30)


def attend_forward(args):
    query, keys, values, length = args
    scores = row_scores(query, keys, length)
    top = jnp.max(scores, axis=-1, keepdims=True)
    expo = jnp.exp(scores - top)
    total = jnp.sum(expo, axis=-1, keepdims=True)
    probs = (expo / total).astype(BF)
    mixed = jnp.einsum("hqk,khe->qhe", probs, values, preferred_element_type=F32).astype(BF)
    return (mixed, (top + jnp.log(total))[..., 0])


def attend_back(args):
    query, keys, values, length, logsum, grad_mixed = args
    scores = row_scores(query, keys, length)
    probs = jnp.exp(scores - logsum[..., None])
    grad_values = jnp.einsum("hqk,qhe->khe", probs.astype(BF), grad_mixed, preferred_element_type=F32)
    grad_probs = jnp.einsum("qhe,khe->hqk", grad_mixed, values, preferred_element_type=F32)
    delta = jnp.sum(grad_probs * probs, axis=-1, keepdims=True)
    grad_scores = (probs * (grad_probs - delta)).astype(BF)
    scale = HEAD_DIM ** (-0.5)
    grad_query = jnp.einsum("hqk,khe->qhe", grad_scores, keys, preferred_element_type=F32) * scale
    grad_keys = jnp.einsum("hqk,qhe->khe", grad_scores, query, preferred_element_type=F32) * scale
    return (grad_query.astype(BF), grad_keys.astype(BF), grad_values.astype(BF))


def gelu_slope(pre):
    normal_cdf = 0.5 * (1.0 + lax.erf(pre * (1.0 / math.sqrt(2.0))))
    density = jnp.exp(-0.5 * pre * pre) * (1.0 / math.sqrt(2.0 * math.pi))
    return normal_cdf + pre * density


def norm_back(grad, gain, scaled, inverse):
    weighted = grad * gain
    first = jnp.mean(weighted, axis=-1, keepdims=True)
    second = jnp.mean(weighted * scaled, axis=-1, keepdims=True)
    grad_in = inverse * (weighted - first - scaled * second)
    return (grad_in, jnp.sum(grad * scaled, axis=0), jnp.sum(grad, axis=0))


def on_device(inputs, lengths, qkv_weight, out_weight, up_weight, down_weight, ln1_gain, ln1_bias, ln2_gain, ln2_bias, cotangent):
    ga, gb, lnp, h1, heads = gather_call(
        inputs, qkv_weight, out_weight, up_weight, down_weight, ln1_gain, ln1_bias, ln2_gain, ln2_bias
    )
    mat = lambda i: ga[:, i * 48 : (i + 1) * 48, :].reshape(768, 768)
    wqkv = jnp.stack([mat(0), mat(1), mat(2)], axis=1)
    wo = mat(3)
    wu = jnp.concatenate([gb[:, j * 48 : (j + 1) * 48, :].reshape(768, 768) for j in range(4)], axis=1)
    wd = gb[:, 192:, :].reshape(3072, 768)
    g1, g2 = lnp[0], lnp[2]
    b2 = lnp[3]
    x = inputs.reshape(256, 768).astype(F32)
    scaled1, inverse1 = normalise(x)

    def split(v):
        return v.transpose(0, 1, 3, 2).reshape(2, 1024, 3, 32)

    q, k, v = (split(heads[:, :, c]) for c in range(3))
    head_out, logsum = lax.map(attend_forward, (q, k, v, lengths))
    mixed = lax.all_to_all(head_out.reshape(2, 1024, 96), "seq", split_axis=1, concat_axis=2, tiled=True).reshape(256, 768)
    x1 = x + nn(mixed, wo)
    scaled2, inverse2 = normalise(x1)
    h2 = (scaled2 * g2 + b2).astype(BF)
    pre = nn(h2, wu)
    act = jax.nn.gelu(pre, approximate=False).astype(BF)
    output = (x1 + nn(act, wd)).astype(BF)
    dy = cotangent.reshape(256, 768)
    grad_down = tn(act, dy)
    grad_pre = (nt(dy, wd) * gelu_slope(pre)).astype(BF)
    grad_up = tn(h2, grad_pre)
    grad_h2 = nt(grad_pre, wu)
    grad_norm2, gg2, gb2 = norm_back(grad_h2, g2, scaled2, inverse2)
    dx1 = dy.astype(F32) + grad_norm2
    low = dx1.astype(BF)
    grad_out = tn(mixed, low)
    do = nt(low, wo).astype(BF).reshape(2, 128, 768)
    do = lax.all_to_all(do, "seq", split_axis=2, concat_axis=1, tiled=True).reshape(2, 1024, 3, 32)
    dqkv = lax.map(attend_back, (q, k, v, lengths, logsum, do))
    dqkv = jnp.stack(
        [lax.all_to_all(t.reshape(2, 1024, 96), "seq", split_axis=1, concat_axis=2, tiled=True).reshape(256, 768) for t in dqkv]
    )
    grad_w = jnp.einsum("td,ctf->cdf", h1, dqkv, preferred_element_type=F32)
    grad_h1 = jnp.einsum("ctf,dcf->td", dqkv, wqkv, preferred_element_type=F32)
    grad_norm1, gg1, gb1 = norm_back(grad_h1, g1, scaled1, inverse1)
    input_grad = dx1 + grad_norm1
    lnb = jnp.stack([t.reshape(16, 8, 6) for t in (gg1, gb1, gg2, gb2)], axis=2)
    lnb = jnp.pad(lnb, ((0, 0), (0, 0), (0, 0), (0, 122))).reshape(16, 8, 512)
    lnb = jnp.pad(lnb, ((0, 0), (0, 8), (0, 256)))
    blocks = [grad_w[c].astype(BF).reshape(16, 48, 768) for c in range(3)]
    blocks += [grad_out.astype(BF).reshape(16, 48, 768), lnb.astype(BF)]
    blocks += [grad_up[:, j * 768 : (j + 1) * 768].astype(BF).reshape(16, 48, 768) for j in range(4)]
    blocks += [grad_down.astype(BF).reshape(16, 192, 768)]
    dqkv_w, dwo, dwu, dwd, dln = scatter_call(jnp.concatenate(blocks, axis=1))
    lns = [dln[0, p * 128 : p * 128 + 6] for p in range(4)]
    return (output.reshape(2, 128, 768), input_grad.reshape(2, 128, 768), dqkv_w, dwo, dwu, dwd, *lns)


def solution(mesh):
    both = ("rows", "seq")
    return jax.shard_map(
        on_device,
        mesh=mesh,
        in_specs=(P("rows", "seq", None), P("rows"), P(both, None, None), P(both, None), P(both, None), P(both, None),
                  P(both), P(both), P(both), P(both), P("rows", "seq", None)),
        out_specs=(P("rows", "seq", None), P("rows", "seq", None), P(both, None, None), P(both, None), P(both, None),
                   P(both, None), P(both), P(both), P(both), P(both)),
        check_vma=False,
    )
```

```python
import functools
import math

import jax
import jax.numpy as jnp
import numpy as np
from jax import lax
from jax.experimental import pallas as pl
from jax.experimental.pallas import tpu as pltpu
from jax.sharding import PartitionSpec as P

MESH = pl.DeviceIdType.MESH
BF = jnp.bfloat16
F32 = jnp.float32
HEAD_DIM = 32
EPS = 1e-05
ROWS_A = 208
ROWS_B = 384
VM = pl.BlockSpec(memory_space=pltpu.VMEM)
SM = pl.BlockSpec(memory_space=pltpu.SMEM)


def perm_a():
    m = np.zeros((ROWS_A, 256), np.float32)
    for c in range(4):
        for s in range(8):
            for i in range(6):
                m[c * 48 + s * 6 + i, s * 32 + c * 6 + i] = 1
    for s in range(8):
        m[192 + s, s * 32 + 24] = 1
    return m


def perm_b():
    m = np.zeros((ROWS_B, 384), np.float32)
    for s in range(8):
        for j in range(4):
            for i in range(6):
                m[j * 48 + s * 6 + i, s * 48 + j * 6 + i] = 1
        for i in range(24):
            m[192 + s * 24 + i, s * 48 + 24 + i] = 1
    return m


def spread_m():
    m = np.zeros((256, 768), np.float32)
    for r in range(16):
        for s in range(8):
            m[r * 16 + s, (r * 8 + s) * 6 : (r * 8 + s) * 6 + 6] = 1
    return m


def spread_e():
    m = np.zeros((128, 768), np.float32)
    for j in range(768):
        m[j % 6, j] = 1
    return m


def const(m):
    return jnp.asarray(m, BF)


def nn(a, b):
    return lax.dot_general(a, b, (((1,), (0,)), ((), ())), preferred_element_type=F32)


def nt(a, b):
    return lax.dot_general(a, b, (((1,), (1,)), ((), ())), preferred_element_type=F32)


def tn(a, b):
    return lax.dot_general(a, b, (((0,), (0,)), ((), ())), preferred_element_type=F32)


class Place:
    def __init__(self):
        self.r = lax.axis_index("rows")
        self.s = lax.axis_index("seq")
        self.z = self.r // 4
        self.y = (self.r // 2) % 2
        self.c = self.r % 2

    def slot(self, dz, dy, dc):
        z = (self.z + dz) % 4
        y = (self.y + dy) % 2
        c = (self.c + dc) % 2
        return z * 4 + y * 2 + c

    def row_dev(self, dz, dy, dc):
        return {"rows": self.slot(dz, dy, dc)}

    def seq_at(self, d):
        return (self.s + d) % 8

    def seq_dev(self, d):
        return {"seq": self.seq_at(d)}


ROW_PEERS = ((0, 0, 1), (0, 1, 0), (1, 0, 0), (3, 0, 0))


def barrier(me):
    sem = pltpu.get_barrier_semaphore()
    for p in ROW_PEERS:
        pl.semaphore_signal(sem, inc=1, device_id=me.row_dev(*p), device_id_type=MESH)
    for d in range(1, 8):
        pl.semaphore_signal(sem, inc=1, device_id=me.seq_dev(d), device_id_type=MESH)
    pl.semaphore_wait(sem, len(ROW_PEERS) + 7)


def remote(src, dst, ss, rs, dev):
    return pltpu.make_async_remote_copy(
        src_ref=src, dst_ref=dst, send_sem=ss, recv_sem=rs, device_id=dev, device_id_type=MESH
    )


class Exchange:
    def __init__(self, me, src, dst, land, ss, rs, base):
        self.me, self.src, self.dst, self.land = me, src, dst, land
        self.ss, self.rs, self.base = ss, rs, base

    def _copy(self, d):
        return remote(
            self.src(d),
            self.dst(d),
            self.ss.at[self.base + d - 1],
            self.rs.at[self.base + d - 1],
            self.me.seq_dev(d),
        )

    def start(self):
        for d in range(1, 8):
            self._copy(d).start()

    def wait_recv(self):
        for d in range(1, 8):
            here = self.land(d)
            remote(
                here, here, self.ss.at[self.base + d - 1], self.rs.at[self.base + d - 1], self.me.seq_dev(d)
            ).wait_recv()

    def wait_send(self):
        for d in range(1, 8):
            self._copy(d).wait_send()


GATHER_SEMS = 17


class RowsGather:
    def __init__(self, me, buf, cut, ss, rs, base):
        self.me, self.buf, self.cut = me, buf, cut
        self.ss, self.rs, self.base = ss, rs, base
        self.sent = []

    def _part(self, rel, part):
        slot = self.me.slot(*rel)
        full = self.buf.shape[1]
        if part == 0:
            return self.buf.at[slot]
        if part == 1:
            return self.buf.at[slot, pl.ds(0, self.cut)]
        return self.buf.at[slot, pl.ds(self.cut, full - self.cut)]

    PLAN = {
        "y": (0, (0, 1, 0), (0, 0, 0), 0),
        "p0": (1, (1, 0, 0), (0, 0, 0), 0),
        "m0": (2, (3, 0, 0), (0, 0, 0), 0),
        "p1": (3, (1, 0, 0), (0, 1, 0), 0),
        "m1": (4, (3, 0, 0), (0, 1, 0), 0),
        "fp0": (5, (1, 0, 0), (3, 0, 0), 1),
        "fm0": (6, (3, 0, 0), (1, 0, 0), 2),
        "fp1": (7, (1, 0, 0), (3, 1, 0), 1),
        "fm1": (8, (3, 0, 0), (1, 1, 0), 2),
        "c00": (9, (0, 0, 1), (0, 0, 0), 0),
        "c01": (10, (0, 0, 1), (0, 1, 0), 0),
        "c10": (11, (0, 0, 1), (1, 0, 0), 0),
        "c11": (12, (0, 0, 1), (1, 1, 0), 0),
        "c20": (13, (0, 0, 1), (2, 0, 0), 0),
        "c21": (14, (0, 0, 1), (2, 1, 0), 0),
        "c30": (15, (0, 0, 1), (3, 0, 0), 0),
        "c31": (16, (0, 0, 1), (3, 1, 0), 0),
    }

    def _send(self, name):
        i, to, block, part = self.PLAN[name]
        ref = self._part(block, part)
        return remote(ref, ref, self.ss.at[self.base + i], self.rs.at[self.base + i], self.me.row_dev(*to))

    def send(self, *names):
        for name in names:
            self._send(name).start()
            self.sent.append(name)

    def recv(self, *names):
        for name in names:
            i, to, block, part = self.PLAN[name]
            rel = ((block[0] - to[0]) % 4, (block[1] - to[1]) % 2, (block[2] - to[2]) % 2)
            ref = self._part(rel, part)
            remote(ref, ref, self.ss.at[self.base + i], self.rs.at[self.base + i], self.me.row_dev(*to)).wait_recv()

    def step0(self):
        self.send("y", "p0", "m0", "c00")

    def step1(self):
        self.recv("y")
        self.send("p1", "m1", "c01")

    def step2(self):
        self.recv("p0")
        self.send("fp0", "c30")
        self.recv("m0")
        self.send("fm0", "c10")

    def step3(self):
        self.recv("p1")
        self.send("fp1", "c31")
        self.recv("m1")
        self.send("fm1", "c11")

    def step4(self):
        self.recv("fp0", "fm0")
        self.send("c20")

    def step5(self):
        self.recv("fp1", "fm1")
        self.send("c21")

    def step6(self):
        self.recv("c00", "c01", "c10", "c11", "c20", "c21", "c30", "c31")

    def finish(self):
        for name in self.sent:
            self._send(name).wait_send()

    def steps(self):
        return [self.step0, self.step1, self.step2, self.step3, self.step4, self.step5, self.step6]


SCATTER_SEMS = 15


class RowsScatter:
    def __init__(self, me, g, cr, zlo, zhi, zr, yr, cut, ss, rs, base):
        self.me, self.g, self.cr, self.zlo, self.zhi, self.zr, self.yr = me, g, cr, zlo, zhi, zr, yr
        self.cut, self.ss, self.rs, self.base = cut, ss, rs, base
        self.full = g.shape[1]
        self.open = []

    def _copy(self, i, src, dst, to):
        return remote(src, dst, self.ss.at[self.base + i], self.rs.at[self.base + i], self.me.row_dev(*to))

    def _start(self, i, src, dst, to):
        copy = self._copy(i, src, dst, to)
        copy.start()
        self.open.append(copy)

    def _landed(self, i, dst, to):
        self._copy(i, dst, dst, to).wait_recv()

    ORDER = ((2, 0), (2, 1), (1, 0), (1, 1), (3, 0), (3, 1), (0, 1), (0, 0))

    def start_core(self, which=None):
        for k, (dz, dy) in enumerate(self.ORDER):
            self._start(k, self.g.at[self.me.slot(dz, dy, 1)], self.cr.at[k], (0, 0, 1))

    def _add(self, k):
        dz, dy = self.ORDER[k]
        self._landed(k, self.cr.at[k], (0, 0, 1))
        slot = self.me.slot(dz, dy, 0)
        self.g[slot] = (self.g[slot].astype(F32) + self.cr[k].astype(F32)).astype(BF)

    def add_far(self):
        lo, hi = pl.ds(0, self.cut), pl.ds(self.cut, self.full - self.cut)
        for dy in (0, 1):
            self._add(dy)
            slot = self.me.slot(2, dy, 0)
            self._start(8 + dy, self.g.at[slot, lo], self.zlo.at[dy], (1, 0, 0))
            self._start(10 + dy, self.g.at[slot, hi], self.zhi.at[dy], (3, 0, 0))

    def add_near(self):
        for k in (2, 3, 4, 5):
            self._add(k)

    def pass_near(self):
        lo, hi = pl.ds(0, self.cut), pl.ds(self.cut, self.full - self.cut)
        for dy in (0, 1):
            self._landed(8 + dy, self.zlo.at[dy], (1, 0, 0))
            slot = self.me.slot(1, dy, 0)
            self.g[slot, lo] = (self.g[slot, lo].astype(F32) + self.zlo[dy].astype(F32)).astype(BF)
            self._landed(10 + dy, self.zhi.at[dy], (3, 0, 0))
            slot = self.me.slot(3, dy, 0)
            self.g[slot, hi] = (self.g[slot, hi].astype(F32) + self.zhi[dy].astype(F32)).astype(BF)
        both = self.me.y == 0
        p0, p1 = self.me.slot(1, 0, 0), self.me.slot(1, 1, 0)
        m0, m1 = self.me.slot(3, 0, 0), self.me.slot(3, 1, 0)
        self._start(12, self.g.at[p1], self.zr.at[0, 1], (1, 0, 0))
        self._start(13, self.g.at[m1], self.zr.at[1, 1], (3, 0, 0))
        self._start(14, self.g.at[p0], self.zr.at[0, 0], (1, 0, 0))
        self._start(15, self.g.at[m0], self.zr.at[1, 0], (3, 0, 0))

    def own_core(self):
        self._add(6)
        self._add(7)

    def cross(self):
        self._landed(12, self.zr.at[0, 1], (1, 0, 0))
        self._landed(13, self.zr.at[1, 1], (3, 0, 0))
        slot = self.me.slot(0, 1, 0)
        total = self.g[slot].astype(F32) + self.zr[0, 1].astype(F32) + self.zr[1, 1].astype(F32)
        self.g[slot] = total.astype(BF)
        self._start(16, self.g.at[slot], self.yr, (0, 1, 0))

    def last(self):
        self._landed(14, self.zr.at[0, 0], (1, 0, 0))
        self._landed(15, self.zr.at[1, 0], (3, 0, 0))
        self._landed(16, self.yr, (0, 1, 0))
        slot = self.me.slot(0, 0, 0)
        return (
            self.g[slot].astype(F32)
            + self.zr[0, 0].astype(F32)
            + self.zr[1, 0].astype(F32)
            + self.yr[...].astype(F32)
        )

    def finish(self):
        for copy in self.open:
            copy.wait_send()


SCATTER_SEMS = 17


def small_vec(ref, row):
    lane = lax.broadcasted_iota(jnp.int32, (1, 128), 1)
    out = jnp.zeros((1, 128), F32)
    for i in range(6):
        out = jnp.where(lane == i, ref[i], out)
    return out


def normalise(v):
    mean = jnp.mean(v, axis=-1, keepdims=True)
    centred = v - mean
    var = jnp.mean(centred * centred, axis=-1, keepdims=True)
    inverse = lax.rsqrt(var + EPS)
    return centred * inverse, inverse


SCALE = HEAD_DIM**-0.5
LOG2E = 1.4426950408889634
BASE = (0, 256, 768, 1536)


def lanes(ref, b, c, h, first, count):
    rows = pl.ds(pl.multiple_of(h * 32, 32), 32)
    if c is None:
        parts = [ref[b, first + i, rows, :] for i in range(count)]
    else:
        parts = [ref[b, first + i, c, rows, :] for i in range(count)]
    return parts[0] if count == 1 else jnp.concatenate(parts, axis=1)


def allowed(nk, length):
    key = lax.broadcasted_iota(jnp.int32, (nk, 256), 0)
    query = lax.broadcasted_iota(jnp.int32, (nk, 256), 1) + (nk - 256)
    return (key <= query) & (key < length)


def attend_one(heads_ref, length, p_ref, l_ref, os_ref, b, h, i):
    rows = pl.ds(pl.multiple_of(h * 32, 32), 32)
    kt = lanes(heads_ref, b, 1, h, 0, 8)
    vt = lanes(heads_ref, b, 2, h, 0, 8)
    for qb in range(4):
        nk = (qb + 1) * 256
        qt = lanes(heads_ref, b, 0, h, 2 * qb, 2)
        s = tn(kt[:, :nk], qt)
        s = jnp.where(allowed(nk, length), s, -1e30)
        top = jnp.max(s, axis=0, keepdims=True)
        p = jnp.exp2((s - top) * (SCALE * LOG2E))
        inverse = 1.0 / jnp.sum(p, axis=0, keepdims=True)
        low = p.astype(BF)
        p_ref[i, pl.ds(BASE[qb], nk), :] = low
        l_ref[i, pl.ds(qb, 1), :] = inverse
        o = (nn(vt[:, :nk], low) * inverse).astype(BF)
        os_ref[b, 2 * qb, rows, :] = o[:, :128]
        os_ref[b, 2 * qb + 1, rows, :] = o[:, 128:]


def attend_one_back(heads_ref, p_ref, l_ref, os_ref, do_ref, dq_ref, acc_ref, b, h, i):
    rows = pl.ds(pl.multiple_of(h * 32, 32), 32)
    kt = lanes(heads_ref, b, 1, h, 0, 8)
    vt = lanes(heads_ref, b, 2, h, 0, 8)
    for qb in range(4):
        nk = (qb + 1) * 256
        qt = lanes(heads_ref, b, 0, h, 2 * qb, 2)
        do = lanes(do_ref, b, None, h, 2 * qb, 2).astype(F32) * l_ref[i, pl.ds(qb, 1), :]
        o = lanes(os_ref, b, None, h, 2 * qb, 2).astype(F32)
        delta = jnp.sum(do * o, axis=0, keepdims=True)
        low = do.astype(BF)
        p = p_ref[i, pl.ds(BASE[qb], nk), :]
        ds = (p.astype(F32) * (tn(vt[:, :nk], low) - delta)).astype(BF)
        dv = nt(low, p)
        dk = nt(qt, ds)
        if nk > 256:
            acc_ref[0, :, : nk - 256] += dk[:, : nk - 256]
            acc_ref[1, :, : nk - 256] += dv[:, : nk - 256]
        acc_ref[0, :, nk - 256 : nk] = dk[:, nk - 256 :]
        acc_ref[1, :, nk - 256 : nk] = dv[:, nk - 256 :]
        dq = (nn(kt[:, :nk], ds) * SCALE).astype(BF)
        dq_ref[b, 2 * qb, 0, rows, :] = dq[:, :128]
        dq_ref[b, 2 * qb + 1, 0, rows, :] = dq[:, 128:]
    for j in range(8):
        dq_ref[b, j, 1, rows, :] = (acc_ref[0, :, j * 128 : (j + 1) * 128] * SCALE).astype(BF)
        dq_ref[b, j, 2, rows, :] = acc_ref[1, :, j * 128 : (j + 1) * 128].astype(BF)


def feed_forward(gb_ref, h2_ref, dy_ref, y_ref, dh_ref):
    dh_ref[...] = jnp.zeros_like(dh_ref)

    def block(j, carry):
        up = pl.ds(pl.multiple_of(j * 48, 16), 48)
        deep = pl.ds(j * 4, 4)
        wu = gb_ref[:, up, :].reshape(768, 768)
        h2 = h2_ref[...]
        u = nn(h2, wu)
        phi = 0.5 + 0.5 * lax.erf(u * (1.0 / math.sqrt(2.0)))
        act = (u * phi).astype(BF)
        slope = phi + u * jnp.exp(-0.5 * u * u) * (1.0 / math.sqrt(2.0 * math.pi))
        wd = gb_ref[deep, pl.ds(192, 192), :].reshape(768, 768)
        dy = dy_ref[...].reshape(256, 768)
        y_ref[...] += nn(act, wd)
        du = (nt(dy, wd) * slope).astype(BF)
        gb_ref[deep, pl.ds(192, 192), :] = tn(act, dy).astype(BF).reshape(4, 192, 768)
        dh_ref[...] += nt(du, wu)
        gb_ref[:, up, :] = tn(h2, du).astype(BF).reshape(16, 48, 768)
        return carry

    lax.fori_loop(0, 4, block, 0)


def norm_parts(grad, gain, scaled, inverse):
    weighted = grad * gain
    first = jnp.mean(weighted, axis=-1, keepdims=True)
    second = jnp.mean(weighted * scaled, axis=-1, keepdims=True)
    grad_in = inverse * (weighted - first - scaled * second)
    return grad_in, jnp.sum(grad * scaled, axis=0, keepdims=True), jnp.sum(grad, axis=0, keepdims=True)


HBM = pl.BlockSpec(memory_space=pl.ANY)


class Counter:
    def __init__(self):
        self.n = 0

    def take(self, k):
        first = self.n
        self.n += k
        return first


def plan():
    c = Counter()
    at = {"xa": c.take(7), "xb": c.take(7), "ga": c.take(GATHER_SEMS), "gb": c.take(GATHER_SEMS)}
    for name in ("q", "o", "do", "dq"):
        at[name] = c.take(14)
    at["ra"] = c.take(SCATTER_SEMS)
    at["rb"] = c.take(SCATTER_SEMS)
    at["sa"] = c.take(7)
    at["sb"] = c.take(7)
    return at, c.n


def scatter_scratch(rows, cut):
    return [
        pltpu.VMEM((8, rows, 768), BF),
        pltpu.VMEM((2, cut, 768), BF),
        pltpu.VMEM((2, rows - cut, 768), BF),
        pltpu.VMEM((2, 2, rows, 768), BF),
        pltpu.VMEM((rows, 768), BF),
    ]


SCRATCH = dict(
    x=pltpu.VMEM((2, 128, 768), BF),
    dy=pltpu.VMEM((2, 128, 768), BF),
    wq=pltpu.VMEM((6, 3, 768), F32),
    wo=pltpu.VMEM((6, 768), F32),
    wu=pltpu.VMEM((6, 3072), F32),
    wd=pltpu.VMEM((24, 768), F32),
    pa=pltpu.VMEM((ROWS_A, 256), BF),
    pb=pltpu.VMEM((ROWS_B, 384), BF),
    sm=pltpu.VMEM((256, 768), BF),
    se=pltpu.VMEM((128, 768), BF),
    f=pltpu.VMEM((80, 768), F32),
    ka=pltpu.VMEM((32, 768), BF),
    kb=pltpu.VMEM((48, 768), BF),
    xa=pltpu.VMEM((8, 32, 768), BF),
    xb=pltpu.VMEM((8, 48, 768), BF),
    ga=pltpu.VMEM((16, ROWS_A, 768), BF),
    gb=pltpu.VMEM((16, ROWS_B, 768), BF),
    lnp=pltpu.VMEM((8, 768), F32),
    xhat=pltpu.VMEM((256, 768), F32),
    inv=pltpu.VMEM((256, 1), F32),
    h1=pltpu.VMEM((256, 768), BF),
    sq=pltpu.VMEM((8, 2, 3, 96, 128), BF),
    heads=pltpu.VMEM((2, 8, 3, 96, 128), BF),
    p=pltpu.VMEM((6, 2560, 256), BF),
    l=pltpu.VMEM((6, 4, 256), F32),
    os=pltpu.VMEM((2, 8, 96, 128), BF),
    ot=pltpu.VMEM((2, 8, 96, 128), BF),
    h2=pltpu.VMEM((256, 768), BF),
    xh2=pltpu.VMEM((256, 768), F32),
    y=pltpu.VMEM((256, 768), F32),
    dh=pltpu.VMEM((256, 768), F32),
    dx=pltpu.VMEM((256, 768), F32),
    dot=pltpu.VMEM((2, 8, 96, 128), BF),
    do=pltpu.VMEM((2, 8, 96, 128), BF),
    acc=pltpu.VMEM((2, 32, 1024), F32),
    dq=pltpu.VMEM((2, 8, 3, 96, 128), BF),
    dqt=pltpu.VMEM((2, 8, 3, 96, 128), BF),
    outv=pltpu.VMEM((2, 128, 768), BF),
    pka=pltpu.VMEM((8, 32, 768), BF),
    pkb=pltpu.VMEM((8, 48, 768), BF),
    xsa=pltpu.VMEM((8, 32, 768), BF),
    xsb=pltpu.VMEM((8, 48, 768), BF),
)


def feature_major(ref, b):
    return ref[b].reshape(768, 128)


def layer_kernel(*refs):
    (x_in, wq_in, wo_in, wu_in, wd_in, dy_in, pa_in, pb_in, sm_in, se_in, len_ref, g1_ref, b1_ref, g2_ref, b2_ref) = refs[:15]
    out_ref, ig_ref, sum_ref = refs[15:18]
    names = list(SCRATCH)
    v = dict(zip(names, refs[18 : 18 + len(names)]))
    rest = refs[18 + len(names) :]
    scr_a, scr_b = rest[:5], rest[5:10]
    ss, rs, ls = rest[10:]
    at, _ = plan()
    me = Place()

    loads = {}
    for i, (name, src) in enumerate(
        (("wq", wq_in), ("wo", wo_in), ("wu", wu_in), ("wd", wd_in), ("pa", pa_in), ("x", x_in), ("pb", pb_in),
         ("sm", sm_in), ("se", se_in), ("dy", dy_in))
    ):
        loads[name] = pltpu.make_async_copy(src, v[name], ls.at[i])
        loads[name].start()

    f = v["f"]
    f[pl.ds(24, 8), :] = jnp.zeros((8, 768), F32)
    for p, ref in enumerate((g1_ref, b1_ref, g2_ref, b2_ref)):
        f[pl.ds(24, 1), pl.ds(p * 128, 128)] = small_vec(ref, p)
    for name in ("wq", "wo", "wu", "wd"):
        loads[name].wait()
    for c in range(3):
        for i in range(6):
            f[pl.ds(c * 6 + i, 1), :] = v["wq"][i, pl.ds(c, 1), :]
    f[pl.ds(18, 6), :] = v["wo"][...]
    v["ka"][...] = f[pl.ds(0, 32), :].astype(BF)
    for j in range(4):
        f[pl.ds(32 + j * 6, 6), :] = v["wu"][:, pl.ds(j * 768, 768)]
    f[pl.ds(56, 24), :] = v["wd"][...]
    v["kb"][...] = f[pl.ds(32, 48), :].astype(BF)
    barrier(me)

    def seq_gather(src, dst, key):
        return Exchange(me, lambda d: src, lambda d: dst.at[me.s], lambda d: dst.at[me.seq_at(8 - d)], ss, rs, at[key])

    def by_row(src, dst, key, flip=False):
        made = []
        for b in range(2):
            if flip:
                out = lambda d, b=b: src.at[me.seq_at(d), b]
            else:
                out = lambda d, b=b: src.at[b, me.seq_at(d)]
            made.append(
                Exchange(me, out, lambda d, b=b: dst.at[b, me.s], lambda d, b=b: dst.at[b, me.seq_at(8 - d)], ss, rs, at[key] + 7 * b)
            )
        return made

    x_a = seq_gather(v["ka"], v["xa"], "xa")
    x_b = seq_gather(v["kb"], v["xb"], "xb")
    x_a.start()
    x_b.start()
    v["xa"][me.s] = v["ka"][...]
    v["xb"][me.s] = v["kb"][...]
    loads["x"].wait()
    xhat, inverse = normalise(v["x"][...].reshape(256, 768).astype(F32))
    v["xhat"][...] = xhat
    v["inv"][...] = inverse
    for name in ("pa", "pb", "sm", "se", "dy"):
        loads[name].wait()

    ga, gb = v["ga"], v["gb"]
    ag_a = RowsGather(me, ga, 112, ss, rs, at["ga"])
    ag_b = RowsGather(me, gb, 192, ss, rs, at["gb"])
    x_a.wait_recv()
    ga[me.r] = nn(v["pa"][...], v["xa"][...].reshape(256, 768)).astype(BF)
    ag_a.step0()
    x_b.wait_recv()
    gb[me.r] = nn(v["pb"][...], v["xb"][...].reshape(384, 768)).astype(BF)
    ag_a.step1()
    ag_a.step2()
    ag_a.step3()
    ag_b.step0()
    ag_a.step4()
    ag_a.step5()
    ag_a.step6()

    lnp = v["lnp"]
    ln = ga[:, pl.ds(192, 16), :].reshape(256, 768)
    for p in range(4):
        spread = nn(ln[:, p * 128 : (p + 1) * 128], v["se"][...])
        lnp[pl.ds(p, 1), :] = jnp.sum(spread * v["sm"][...].astype(F32), axis=0, keepdims=True)
    h1 = (v["xhat"][...] * lnp[pl.ds(0, 1), :] + lnp[pl.ds(1, 1), :]).astype(BF)
    v["h1"][...] = h1
    for c in range(3):
        w = ga[:, pl.ds(c * 48, 48), :].reshape(768, 768)
        val = nn(h1, w).T.astype(BF)
        for k in range(8):
            for b in range(2):
                v["sq"][k, b, c] = val[k * 96 : (k + 1) * 96, b * 128 : (b + 1) * 128]
    x_q = by_row(v["sq"], v["heads"], "q", flip=True)
    for b in range(2):
        x_q[b].start()
        v["heads"][b, me.s] = v["sq"][me.s, b]
    ag_b.step1()

    x_o = by_row(v["os"], v["ot"], "o")

    def forward(b):
        x_q[b].wait_recv()

        def one(h, carry):
            attend_one(v["heads"], len_ref[b], v["p"], v["l"], v["os"], b, h, b * 3 + h)
            return carry

        lax.fori_loop(0, 3, one, 0)
        x_o[b].start()
        v["ot"][b, me.s] = v["os"][b, me.s]

    forward(0)
    ag_b.step2()
    forward(1)
    ag_b.step3()
    ag_b.step4()
    ag_b.step5()

    for b in range(2):
        x_o[b].wait_recv()
    ot = jnp.concatenate([feature_major(v["ot"], b) for b in range(2)], axis=1)
    wo = ga[:, pl.ds(144, 48), :].reshape(768, 768)
    x1 = v["x"][...].reshape(256, 768).astype(F32) + tn(ot, wo)
    xhat2, inverse2 = normalise(x1)
    v["xh2"][...] = xhat2
    v["h2"][...] = (xhat2 * lnp[pl.ds(2, 1), :] + lnp[pl.ds(3, 1), :]).astype(BF)
    v["y"][...] = x1
    ag_b.step6()
    ag_b.finish()
    ag_a.finish()

    feed_forward(gb, v["h2"], v["dy"], v["y"], v["dh"])
    rs_b = RowsScatter(me, gb, *scr_b, 192, ss, rs, at["rb"])
    rs_b.start_core()

    v["outv"][...] = v["y"][...].astype(BF).reshape(2, 128, 768)
    store_out = pltpu.make_async_copy(v["outv"], out_ref, ls.at[10])
    store_out.start()
    grad_in, gg2, gb2 = norm_parts(v["dh"][...], lnp[pl.ds(2, 1), :], v["xh2"][...], inverse2)
    dx = v["dy"][...].reshape(256, 768).astype(F32) + grad_in
    v["dx"][...] = dx
    low = dx.astype(BF)
    d = nt(wo, low).astype(BF)
    for k in range(8):
        for b in range(2):
            v["dot"][b, k] = d[k * 96 : (k + 1) * 96, b * 128 : (b + 1) * 128]
    x_do = by_row(v["dot"], v["do"], "do")
    for b in range(2):
        x_do[b].start()
        v["do"][b, me.s] = v["dot"][b, me.s]
    ga[:, pl.ds(144, 48), :] = nn(ot, low).astype(BF).reshape(16, 48, 768)
    rs_b.add_far()
    rs_b.add_near()

    x_dq = by_row(v["dq"], v["dqt"], "dq")

    def backward(b):
        x_do[b].wait_recv()

        def one(h, carry):
            attend_one_back(v["heads"], v["p"], v["l"], v["os"], v["do"], v["dq"], v["acc"], b, h, b * 3 + h)
            return carry

        lax.fori_loop(0, 3, one, 0)
        x_dq[b].start()
        v["dqt"][b, me.s] = v["dq"][b, me.s]

    backward(0)
    rs_b.pass_near()
    backward(1)
    rs_b.own_core()
    for b in range(2):
        x_dq[b].wait_recv()

    dh1 = jnp.zeros((256, 768), F32)
    for c in range(3):
        dqt = jnp.concatenate([v["dqt"][b, :, c].reshape(768, 128) for b in range(2)], axis=1)
        dq = dqt.T
        dh1 += nt(dq, ga[:, pl.ds(c * 48, 48), :].reshape(768, 768))
        ga[:, pl.ds(c * 48, 48), :] = tn(v["h1"][...], dq).astype(BF).reshape(16, 48, 768)
    grad_in, gg1, gb1 = norm_parts(dh1, lnp[pl.ds(0, 1), :], v["xhat"][...], v["inv"][...])
    ga[:, pl.ds(192, 16), pl.ds(512, 256)] = jnp.zeros((16, 16, 256), BF)
    for p, vec in enumerate((gg1, gb1, gg2, gb2)):
        rows = (v["sm"][...].astype(F32) * vec).astype(BF)
        ga[:, pl.ds(192, 16), pl.ds(p * 128, 128)] = nt(rows, v["se"][...]).astype(BF).reshape(16, 16, 128)
    rs_a = RowsScatter(me, ga, *scr_a, 112, ss, rs, at["ra"])
    rs_a.start_core()
    v["xhat"][...] = v["dx"][...] + grad_in
    store_ig = []
    for b in range(2):
        store_ig.append(pltpu.make_async_copy(v["xhat"].at[pl.ds(b * 128, 128)], ig_ref.at[b], ls.at[11 + b]))
        store_ig[b].start()
    rs_b.cross()
    rs_a.add_far()
    rs_a.add_near()
    total = rs_b.last().astype(BF)
    v["pkb"][...] = tn(v["pb"][...], total).astype(BF).reshape(8, 48, 768)

    def seq_scatter(src, dst, key):
        made = Exchange(
            me, lambda d: src.at[me.seq_at(d)], lambda d: dst.at[me.s], lambda d: dst.at[me.seq_at(8 - d)], ss, rs, at[key]
        )
        made.start()
        dst[me.s] = src[me.s]
        return made

    s_b = seq_scatter(v["pkb"], v["xsb"], "sb")
    rs_a.pass_near()
    rs_a.own_core()
    rs_a.cross()
    total = rs_a.last().astype(BF)
    v["pka"][...] = tn(v["pa"][...], total).astype(BF).reshape(8, 32, 768)
    s_a = seq_scatter(v["pka"], v["xsa"], "sa")
    s_b.wait_recv()
    f[pl.ds(32, 48), :] = jnp.sum(v["xsb"][...].astype(F32), axis=0)
    s_a.wait_recv()
    f[pl.ds(0, 32), :] = jnp.sum(v["xsa"][...].astype(F32), axis=0)
    store_f = pltpu.make_async_copy(f, sum_ref, ls.at[13])
    store_f.start()
    for each in (x_a, x_b, *x_q, *x_o, *x_do, *x_dq, s_a, s_b):
        each.wait_send()
    rs_a.finish()
    rs_b.finish()
    for store in (store_out, *store_ig, store_f):
        store.wait()


def final_kernel(out_in, ig_in, f_in, out_ref, ig_ref, dwq_ref, dwo_ref, dwu_ref, dwd_ref, ln_ref, out_v, ig_v, f_ref, sem):
    loads = [
        pltpu.make_async_copy(src, dst, sem.at[i])
        for i, (src, dst) in enumerate(((f_in, f_ref), (ig_in, ig_v), (out_in, out_v)))
    ]
    for load in loads:
        load.start()
    a = pltpu.make_async_copy(out_v, out_ref, sem.at[3])
    b = pltpu.make_async_copy(ig_v, ig_ref, sem.at[4])
    loads[1].wait()
    b.start()
    loads[2].wait()
    a.start()
    loads[0].wait()
    for c in range(3):
        for i in range(6):
            dwq_ref[i, pl.ds(c, 1), :] = f_ref[pl.ds(c * 6 + i, 1), :]
    dwo_ref[...] = f_ref[pl.ds(18, 6), :]
    ln_ref[...] = f_ref[pl.ds(24, 8), :]
    for j in range(4):
        dwu_ref[:, pl.ds(j * 768, 768)] = f_ref[pl.ds(32 + j * 6, 6), :]
    dwd_ref[...] = f_ref[pl.ds(56, 24), :]
    a.wait()
    b.wait()


def on_device(inputs, lengths, qkv_weight, out_weight, up_weight, down_weight, ln1_gain, ln1_bias, ln2_gain, ln2_bias, cotangent):
    sds = jax.ShapeDtypeStruct
    n = plan()[1]
    out, ig, sums = pl.pallas_call(
        layer_kernel,
        out_shape=(sds((2, 128, 768), BF), sds((2, 128, 768), F32), sds((80, 768), F32)),
        in_specs=[HBM] * 10 + [SM] * 5,
        out_specs=[HBM] * 3,
        scratch_shapes=[
            *SCRATCH.values(),
            *scatter_scratch(ROWS_A, 112),
            *scatter_scratch(ROWS_B, 192),
            pltpu.SemaphoreType.DMA((n,)),
            pltpu.SemaphoreType.DMA((n,)),
            pltpu.SemaphoreType.DMA((14,)),
        ],
        compiler_params=pltpu.CompilerParams(collective_id=0, has_side_effects=True, vmem_limit_bytes=60 * 1024 * 1024),
        name="layer",
    )(
        inputs, qkv_weight, out_weight, up_weight, down_weight, cotangent,
        const(perm_a()), const(perm_b()), const(spread_m()), const(spread_e()),
        lengths, ln1_gain, ln1_bias, ln2_gain, ln2_bias,
    )
    res = pl.pallas_call(
        final_kernel,
        out_shape=(
            sds((2, 128, 768), BF), sds((2, 128, 768), F32), sds((6, 3, 768), F32), sds((6, 768), F32),
            sds((6, 3072), F32), sds((24, 768), F32), sds((8, 768), F32),
        ),
        in_specs=[HBM] * 3,
        out_specs=[HBM, HBM] + [VM] * 5,
        scratch_shapes=[
            pltpu.VMEM((2, 128, 768), BF),
            pltpu.VMEM((2, 128, 768), F32),
            pltpu.VMEM((80, 768), F32),
            pltpu.SemaphoreType.DMA((5,)),
        ],
        name="final",
    )(out, ig, sums)
    return (*res[:6], *[res[6][0, p * 128 : p * 128 + 6] for p in range(4)])


def solution(mesh):
    both = ("rows", "seq")
    return jax.shard_map(
        on_device,
        mesh=mesh,
        in_specs=(P("rows", "seq", None), P("rows"), P(both, None, None), P(both, None), P(both, None), P(both, None),
                  P(both), P(both), P(both), P(both), P("rows", "seq", None)),
        out_specs=(P("rows", "seq", None), P("rows", "seq", None), P(both, None, None), P(both, None), P(both, None),
                   P(both, None), P(both), P(both), P(both), P(both)),
        check_vma=False,
    )
```

```python
import functools
import math

import jax
import jax.numpy as jnp
import numpy as np
from jax import lax
from jax.experimental import pallas as pl
from jax.experimental.pallas import tpu as pltpu
from jax.sharding import PartitionSpec as P

MESH = pl.DeviceIdType.MESH
BF = jnp.bfloat16
F32 = jnp.float32
HEAD_DIM = 32
EPS = 1e-05
ROWS_A = 160
ROWS_U = 240
ROWS_W = 192
VM = pl.BlockSpec(memory_space=pltpu.VMEM)
SM = pl.BlockSpec(memory_space=pltpu.SMEM)


def perm_a():
    m = np.zeros((ROWS_A, 256), np.float32)
    for s in range(8):
        for c in range(3):
            for i in range(6):
                m[c * 48 + s * 6 + i, s * 32 + c * 6 + i] = 1
        m[144 + s, s * 32 + 18] = 1
    return m


def perm_u():
    m = np.zeros((ROWS_U, 256), np.float32)
    for s in range(8):
        for j in range(5):
            for i in range(6):
                m[j * 48 + s * 6 + i, s * 32 + j * 6 + i] = 1
    return m


def perm_w():
    m = np.zeros((ROWS_W, 256), np.float32)
    for s in range(8):
        for i in range(24):
            m[s * 24 + i, s * 32 + i] = 1
    return m


def spread_m():
    m = np.zeros((256, 768), np.float32)
    for r in range(16):
        for s in range(8):
            m[r * 16 + s, (r * 8 + s) * 6 : (r * 8 + s) * 6 + 6] = 1
    return m


def spread_e():
    m = np.zeros((4, 128, 768), np.float32)
    for p in range(4):
        for j in range(768):
            m[p, p * 32 + j % 6, j] = 1
    return m


def groups_e():
    m = np.zeros((768, 1024), np.float32)
    for j in range(768):
        m[j, j // 96 * 128 + j % 96] = 1
    return m


def const(m):
    return jnp.asarray(m, BF)


def nn(a, b):
    return lax.dot_general(a, b, (((1,), (0,)), ((), ())), preferred_element_type=F32)


def nt(a, b):
    return lax.dot_general(a, b, (((1,), (1,)), ((), ())), preferred_element_type=F32)


def tn(a, b):
    return lax.dot_general(a, b, (((0,), (0,)), ((), ())), preferred_element_type=F32)


class Place:
    def __init__(self):
        self.r = lax.axis_index("rows")
        self.s = lax.axis_index("seq")
        self.z = self.r // 4
        self.y = (self.r // 2) % 2
        self.c = self.r % 2

    def slot(self, dz, dy, dc):
        z = (self.z + dz) % 4
        y = (self.y + dy) % 2
        c = (self.c + dc) % 2
        return z * 4 + y * 2 + c

    def row_dev(self, dz, dy, dc):
        return {"rows": self.slot(dz, dy, dc)}

    def along_seq(self):
        return SeqPlace(self.s)

    def seq_at(self, d):
        return (self.s + d) % 8

    def seq_dev(self, d):
        return {"seq": self.seq_at(d)}


class SeqPlace:
    def __init__(self, s):
        self.s = s

    def slot(self, dx, dy, dc):
        return (self.s // 4 + dy) % 2 * 4 + (self.s + dx) % 4

    def row_dev(self, dx, dy, dc):
        return {"seq": self.slot(dx, dy, dc)}


ROW_PEERS = ((0, 0, 1), (0, 1, 0), (1, 0, 0), (3, 0, 0))


def barrier_signal(me):
    sem = pltpu.get_barrier_semaphore()
    for p in ROW_PEERS:
        pl.semaphore_signal(sem, inc=1, device_id=me.row_dev(*p), device_id_type=MESH)
    for d in range(1, 8):
        pl.semaphore_signal(sem, inc=1, device_id=me.seq_dev(d), device_id_type=MESH)


def barrier_wait():
    pl.semaphore_wait(pltpu.get_barrier_semaphore(), len(ROW_PEERS) + 7)


def remote(src, dst, ss, rs, dev):
    return pltpu.make_async_remote_copy(
        src_ref=src, dst_ref=dst, send_sem=ss, recv_sem=rs, device_id=dev, device_id_type=MESH
    )


class Exchange:
    def __init__(self, me, src, dst, land, ss, rs, base):
        self.me, self.src, self.dst, self.land = me, src, dst, land
        self.ss, self.rs, self.base = ss, rs, base

    def _copy(self, d):
        return remote(
            self.src(d),
            self.dst(d),
            self.ss.at[self.base + d - 1],
            self.rs.at[self.base + d - 1],
            self.me.seq_dev(d),
        )

    def start(self):
        for d in range(1, 8):
            self._copy(d).start()

    def wait_recv(self):
        for d in range(1, 8):
            here = self.land(d)
            remote(
                here, here, self.ss.at[self.base + d - 1], self.rs.at[self.base + d - 1], self.me.seq_dev(d)
            ).wait_recv()

    def wait_send(self):
        for d in range(1, 8):
            self._copy(d).wait_send()


GATHER_SEMS = 17


class RowsGather:
    def __init__(self, me, buf, cut, ss, rs, base, core=True):
        self.me, self.buf, self.cut, self.core = me, buf, cut, core
        self.ss, self.rs, self.base = ss, rs, base
        self.sent = []

    def _part(self, rel, part):
        slot = self.me.slot(*rel)
        full = self.buf.shape[1]
        if part == 0:
            return self.buf.at[slot]
        if part == 1:
            return self.buf.at[slot, pl.ds(0, self.cut)]
        return self.buf.at[slot, pl.ds(self.cut, full - self.cut)]

    PLAN = {
        "y": (0, (0, 1, 0), (0, 0, 0), 0),
        "p0": (1, (1, 0, 0), (0, 0, 0), 0),
        "m0": (2, (3, 0, 0), (0, 0, 0), 0),
        "p1": (3, (1, 0, 0), (0, 1, 0), 0),
        "m1": (4, (3, 0, 0), (0, 1, 0), 0),
        "fp0": (5, (1, 0, 0), (3, 0, 0), 1),
        "fm0": (6, (3, 0, 0), (1, 0, 0), 2),
        "fp1": (7, (1, 0, 0), (3, 1, 0), 1),
        "fm1": (8, (3, 0, 0), (1, 1, 0), 2),
        "c00": (9, (0, 0, 1), (0, 0, 0), 0),
        "c01": (10, (0, 0, 1), (0, 1, 0), 0),
        "c10": (11, (0, 0, 1), (1, 0, 0), 0),
        "c11": (12, (0, 0, 1), (1, 1, 0), 0),
        "c20": (13, (0, 0, 1), (2, 0, 0), 0),
        "c21": (14, (0, 0, 1), (2, 1, 0), 0),
        "c30": (15, (0, 0, 1), (3, 0, 0), 0),
        "c31": (16, (0, 0, 1), (3, 1, 0), 0),
    }

    def _send(self, name):
        i, to, block, part = self.PLAN[name]
        ref = self._part(block, part)
        return remote(ref, ref, self.ss.at[self.base + i], self.rs.at[self.base + i], self.me.row_dev(*to))

    def send(self, *names):
        for name in names:
            if self.core or name[0] != "c":
                self._send(name).start()
                self.sent.append(name)

    def recv(self, *names):
        for name in names:
            i, to, block, part = self.PLAN[name]
            rel = ((block[0] - to[0]) % 4, (block[1] - to[1]) % 2, (block[2] - to[2]) % 2)
            ref = self._part(rel, part)
            remote(ref, ref, self.ss.at[self.base + i], self.rs.at[self.base + i], self.me.row_dev(*to)).wait_recv()

    def step0(self):
        self.send("p0", "m0", "y", "c00")

    def step1(self):
        self.recv("y")
        self.send("p1", "m1", "c01")

    def step2(self):
        self.recv("p0")
        self.send("fp0", "c30")
        self.recv("m0")
        self.send("fm0", "c10")

    def step3(self):
        self.recv("p1")
        self.send("fp1", "c31")
        self.recv("m1")
        self.send("fm1", "c11")

    def step4(self):
        self.recv("fp0", "fm0")
        self.send("c20")

    def step5(self):
        self.recv("fp1", "fm1")
        self.send("c21")

    def step6(self):
        self.recv("c00", "c01", "c10", "c11", "c20", "c21", "c30", "c31")

    def finish(self):
        for name in self.sent:
            self._send(name).wait_send()


class RowsScatter:
    def __init__(self, me, g, cr, zlo, zhi, zr, yr, ss, rs, base, first=0):
        self.me, self.g, self.cr, self.zlo, self.zhi, self.zr, self.yr = me, g, cr, zlo, zhi, zr, yr
        self.ss, self.rs, self.base = ss, rs, base
        cut, rows = zlo.shape[1], yr.shape[0]
        self.all, self.lo, self.hi = pl.ds(first, rows), pl.ds(first, cut), pl.ds(first + cut, rows - cut)
        self.open = []

    def _copy(self, i, src, dst, to):
        return remote(src, dst, self.ss.at[self.base + i], self.rs.at[self.base + i], self.me.row_dev(*to))

    def _start(self, i, src, dst, to):
        copy = self._copy(i, src, dst, to)
        copy.start()
        self.open.append(copy)

    def _landed(self, i, dst, to):
        self._copy(i, dst, dst, to).wait_recv()

    ORDER = ((2, 0), (2, 1), (1, 0), (1, 1), (3, 0), (3, 1), (0, 1), (0, 0))

    def start_core(self):
        for k, (dz, dy) in enumerate(self.ORDER):
            self._start(k, self.g.at[self.me.slot(dz, dy, 1), self.all], self.cr.at[k], (0, 0, 1))

    def _add(self, k):
        if self.cr is None:
            return
        dz, dy = self.ORDER[k]
        self._landed(k, self.cr.at[k], (0, 0, 1))
        slot = self.me.slot(dz, dy, 0)
        self.g[slot, self.all] = (self.g[slot, self.all].astype(F32) + self.cr[k].astype(F32)).astype(BF)

    def add_far(self):
        for dy in (0, 1):
            self._add(dy)
            slot = self.me.slot(2, dy, 0)
            self._start(8 + dy, self.g.at[slot, self.lo], self.zlo.at[dy], (1, 0, 0))
            self._start(10 + dy, self.g.at[slot, self.hi], self.zhi.at[dy], (3, 0, 0))

    def add_near(self):
        for k in (2, 3, 4, 5):
            self._add(k)

    def pass_near(self):
        for dy in (1, 0):
            self._landed(8 + dy, self.zlo.at[dy], (1, 0, 0))
            slot = self.me.slot(1, dy, 0)
            self.g[slot, self.lo] = (self.g[slot, self.lo].astype(F32) + self.zlo[dy].astype(F32)).astype(BF)
            self._start(12 + 2 * dy, self.g.at[slot, self.all], self.zr.at[0, dy], (1, 0, 0))
            self._landed(10 + dy, self.zhi.at[dy], (3, 0, 0))
            slot = self.me.slot(3, dy, 0)
            self.g[slot, self.hi] = (self.g[slot, self.hi].astype(F32) + self.zhi[dy].astype(F32)).astype(BF)
            self._start(13 + 2 * dy, self.g.at[slot, self.all], self.zr.at[1, dy], (3, 0, 0))

    def own_core(self):
        self._add(6)
        self._add(7)

    def cross(self):
        self._landed(14, self.zr.at[0, 1], (1, 0, 0))
        self._landed(15, self.zr.at[1, 1], (3, 0, 0))
        slot = self.me.slot(0, 1, 0)
        total = self.g[slot, self.all].astype(F32) + self.zr[0, 1].astype(F32) + self.zr[1, 1].astype(F32)
        self.g[slot, self.all] = total.astype(BF)
        self._start(16, self.g.at[slot, self.all], self.yr, (0, 1, 0))

    def last(self):
        self._landed(12, self.zr.at[0, 0], (1, 0, 0))
        self._landed(13, self.zr.at[1, 0], (3, 0, 0))
        self._landed(16, self.yr, (0, 1, 0))
        slot = self.me.slot(0, 0, 0)
        return (
            self.g[slot, self.all].astype(F32)
            + self.zr[0, 0].astype(F32)
            + self.zr[1, 0].astype(F32)
            + self.yr[...].astype(F32)
        )

    def finish(self):
        for copy in self.open:
            copy.wait_send()


SCATTER_SEMS = 17


def small_vec(refs):
    lane = lax.broadcasted_iota(jnp.int32, (1, 128), 1)
    out = jnp.zeros((1, 128), F32)
    for p, ref in enumerate(refs):
        for i in range(6):
            out = jnp.where(lane == p * 32 + i, ref[i], out)
    return out


def normalise(v):
    mean = jnp.mean(v, axis=-1, keepdims=True)
    centred = v - mean
    var = jnp.mean(centred * centred, axis=-1, keepdims=True)
    inverse = lax.rsqrt(var + EPS)
    return centred * inverse, inverse


SCALE = HEAD_DIM**-0.5
LOG2E = 1.4426950408889634
BASE = (0, 256, 768, 1536)


def lanes(ref, b, c, h, first, count):
    rows = pl.ds(pl.multiple_of(h * 32, 32), 32)
    if c is None:
        parts = [ref[b, first + i, rows, :] for i in range(count)]
    else:
        parts = [ref[b, first + i, c, rows, :] for i in range(count)]
    return parts[0] if count == 1 else jnp.concatenate(parts, axis=1)


def allowed(nk, length):
    key = lax.broadcasted_iota(jnp.int32, (nk, 256), 0)
    query = lax.broadcasted_iota(jnp.int32, (nk, 256), 1) + (nk - 256)
    return (key <= query) & (key < length)


def attend_one(heads_ref, length, p_ref, l_ref, os_ref, b, h, i):
    rows = pl.ds(pl.multiple_of(h * 32, 32), 32)
    kt = lanes(heads_ref, b, 1, h, 0, 8)
    vt = lanes(heads_ref, b, 2, h, 0, 8)
    for qb in range(4):
        nk = (qb + 1) * 256
        qt = lanes(heads_ref, b, 0, h, 2 * qb, 2)
        s = tn(kt[:, :nk], qt)
        s = jnp.where(allowed(nk, length), s, -1e30)
        top = jnp.max(s, axis=0, keepdims=True)
        p = jnp.exp2((s - top) * (SCALE * LOG2E))
        inverse = 1.0 / jnp.sum(p, axis=0, keepdims=True)
        low = p.astype(BF)
        p_ref[i, pl.ds(BASE[qb], nk), :] = low
        l_ref[i, pl.ds(qb, 1), :] = inverse
        o = (nn(vt[:, :nk], low) * inverse).astype(BF)
        os_ref[b, 2 * qb, rows, :] = o[:, :128]
        os_ref[b, 2 * qb + 1, rows, :] = o[:, 128:]


def attend_one_back(heads_ref, p_ref, l_ref, os_ref, do_ref, dq_ref, acc_ref, b, h, i):
    rows = pl.ds(pl.multiple_of(h * 32, 32), 32)
    kt = lanes(heads_ref, b, 1, h, 0, 8)
    vt = lanes(heads_ref, b, 2, h, 0, 8)
    for qb in range(4):
        nk = (qb + 1) * 256
        qt = lanes(heads_ref, b, 0, h, 2 * qb, 2)
        do = lanes(do_ref, b, None, h, 2 * qb, 2).astype(F32) * l_ref[i, pl.ds(qb, 1), :]
        o = lanes(os_ref, b, None, h, 2 * qb, 2).astype(F32)
        delta = jnp.sum(do * o, axis=0, keepdims=True)
        low = do.astype(BF)
        p = p_ref[i, pl.ds(BASE[qb], nk), :]
        ds = (p.astype(F32) * (tn(vt[:, :nk], low) - delta)).astype(BF)
        dv = nt(low, p)
        dk = nt(qt, ds)
        if nk > 256:
            acc_ref[0, :, : nk - 256] += dk[:, : nk - 256]
            acc_ref[1, :, : nk - 256] += dv[:, : nk - 256]
        acc_ref[0, :, nk - 256 : nk] = dk[:, nk - 256 :]
        acc_ref[1, :, nk - 256 : nk] = dv[:, nk - 256 :]
        dq = (nn(kt[:, :nk], ds) * SCALE).astype(BF)
        dq_ref[2 * qb, 0, rows, :] = dq[:, :128]
        dq_ref[2 * qb + 1, 0, rows, :] = dq[:, 128:]
    for j in range(8):
        dq_ref[j, 1, rows, :] = (acc_ref[0, :, j * 128 : (j + 1) * 128] * SCALE).astype(BF)
        dq_ref[j, 2, rows, :] = acc_ref[1, :, j * 128 : (j + 1) * 128].astype(BF)


def feed_forward(first, end, gu_ref, gw_ref, h2_ref, dy_ref, y_ref, dh_ref):
    def block(j, carry):
        up = pl.ds(pl.multiple_of(j * 48, 16), 48)
        deep = pl.ds(j * 4, 4)
        wu = gu_ref[:, up, :].reshape(768, 768)
        h2 = h2_ref[...]
        u = nn(h2, wu)
        phi = 0.5 + 0.5 * lax.erf(u * (1.0 / math.sqrt(2.0)))
        act = (u * phi).astype(BF)
        slope = phi + u * jnp.exp(-0.5 * u * u) * (1.0 / math.sqrt(2.0 * math.pi))
        wd = gw_ref[deep].reshape(768, 768)
        dy = dy_ref[...].reshape(256, 768)
        y_ref[...] += nn(act, wd)
        du = (nt(dy, wd) * slope).astype(BF)
        gw_ref[deep] = tn(act, dy).astype(BF).reshape(4, 192, 768)
        dh_ref[...] += nt(du, wu)
        gu_ref[:, up, :] = tn(h2, du).astype(BF).reshape(16, 48, 768)
        return carry

    lax.fori_loop(first, end, block, 0)


def norm_parts(grad, gain, scaled, inverse):
    weighted = grad * gain
    first = jnp.mean(weighted, axis=-1, keepdims=True)
    second = jnp.mean(weighted * scaled, axis=-1, keepdims=True)
    grad_in = inverse * (weighted - first - scaled * second)
    return grad_in, jnp.sum(grad * scaled, axis=0, keepdims=True), jnp.sum(grad, axis=0, keepdims=True)


HBM = pl.BlockSpec(memory_space=pl.ANY)


class Counter:
    def __init__(self):
        self.n = 0

    def take(self, k):
        first = self.n
        self.n += k
        return first


def plan():
    c = Counter()
    at = {}
    for name in ("xa", "xu", "xw", "sa", "su", "sw"):
        at[name] = c.take(7)
    for name in ("ga", "gu", "gw", "gx0", "gx1"):
        at[name] = c.take(GATHER_SEMS)
    for name in ("o", "do"):
        at[name] = c.take(14)
    for name in ("ra", "ru1", "ru2", "rw", "rx0", "rx1"):
        at[name] = c.take(SCATTER_SEMS)
    return at, c.n


def scatter_scratch(rows, cut, wide, core=True):
    made = [
        pltpu.VMEM((2, cut, wide), BF),
        pltpu.VMEM((2, rows - cut, wide), BF),
        pltpu.VMEM((2, 2, rows, wide), BF),
        pltpu.VMEM((rows, wide), BF),
    ]
    return ([pltpu.VMEM((8, rows, wide), BF)] if core else []) + made


CUT_A, CUT_U, CUT_W, CUT_X = 80, 128, 96, 64
U1, U2 = 96, 144
SCRATCH = dict(
    xl=pltpu.VMEM((2, 8, 128, 768), BF),
    h1=pltpu.VMEM((2, 8, 128, 768), BF),
    dy=pltpu.VMEM((2, 128, 768), BF),
    wq=pltpu.VMEM((6, 3, 768), F32),
    wo=pltpu.VMEM((6, 768), F32),
    wu=pltpu.VMEM((6, 3072), F32),
    wd=pltpu.VMEM((24, 768), F32),
    pa=pltpu.VMEM((ROWS_A, 256), BF),
    pu=pltpu.VMEM((ROWS_U, 256), BF),
    pw=pltpu.VMEM((ROWS_W, 256), BF),
    sm=pltpu.VMEM((256, 768), BF),
    se=pltpu.VMEM((4, 128, 768), BF),
    ge=pltpu.VMEM((768, 1024), BF),
    f=pltpu.VMEM((96, 768), F32),
    fl=pltpu.VMEM((32, 128), F32),
    ka=pltpu.VMEM((8, 32, 128), BF),
    k=pltpu.VMEM((2, 32, 768), BF),
    xa=pltpu.VMEM((8, 32, 128), BF),
    xu=pltpu.VMEM((8, 32, 768), BF),
    xw=pltpu.VMEM((8, 32, 768), BF),
    ga=pltpu.VMEM((16, ROWS_A, 128), BF),
    gu=pltpu.VMEM((16, ROWS_U, 768), BF),
    gw=pltpu.VMEM((16, ROWS_W, 768), BF),
    lnp=pltpu.VMEM((8, 768), F32),
    wt=pltpu.VMEM((288, 768), BF),
    dwt=pltpu.VMEM((3, 128, 768), F32),
    xhat=pltpu.VMEM((256, 768), F32),
    inv=pltpu.VMEM((256, 1), F32),
    heads=pltpu.VMEM((2, 8, 3, 96, 128), BF),
    p=pltpu.VMEM((6, 2560, 256), BF),
    l=pltpu.VMEM((6, 4, 256), F32),
    os=pltpu.VMEM((2, 8, 96, 128), BF),
    ot=pltpu.VMEM((2, 8, 96, 128), BF),
    h2=pltpu.VMEM((256, 768), BF),
    xh2=pltpu.VMEM((256, 768), F32),
    y=pltpu.VMEM((256, 768), F32),
    dh=pltpu.VMEM((256, 768), F32),
    dot=pltpu.VMEM((2, 8, 96, 128), BF),
    do=pltpu.VMEM((2, 8, 96, 128), BF),
    acc=pltpu.VMEM((2, 32, 1024), F32),
    dq=pltpu.VMEM((8, 3, 96, 128), BF),
    lng=pltpu.VMEM((8, 768), F32),
    xsa=pltpu.VMEM((8, 32, 128), BF),
    xs=pltpu.VMEM((2, 8, 32, 768), BF),
)
SMALL = dict(
    len=pltpu.SMEM((2,), jnp.int32),
    g1=pltpu.SMEM((6,), F32),
    b1=pltpu.SMEM((6,), F32),
    g2=pltpu.SMEM((6,), F32),
    b2=pltpu.SMEM((6,), F32),
)
INPUTS = ("x", "wq", "g1", "b1", "g2", "b2", "ge", "wu", "wo", "wd", "pa", "pu", "pw", "sm", "se", "dy", "len")


def feature_major(ref, b):
    return ref[b].reshape(768, 128)


def layer_kernel(*refs):
    inputs = dict(zip(INPUTS, refs))
    refs = refs[len(INPUTS) :]
    out_ref, ig_ref, sum_ref = refs[:3]
    names = [*SCRATCH, *SMALL]
    v = dict(zip(names, refs[3 : 3 + len(names)]))
    rest = refs[3 + len(names) :]
    scr_a, scr_u1, scr_u2, scr_w = rest[:5], rest[5:10], rest[10:15], rest[15:20]
    scr_x = (rest[20:24], rest[24:28])
    ss, rs, ls = rest[28:]
    at, _ = plan()
    me = Place()
    seq = me.along_seq()
    barrier_signal(me)
    xl = v["xl"]
    loads = {}
    for b in range(2):
        loads[b] = pltpu.make_async_copy(inputs["x"].at[b], xl.at[b, me.s], ls.at[21 + b])
        loads[b].start()
    for i, name in enumerate(INPUTS):
        if name != "x":
            loads[name] = pltpu.make_async_copy(inputs[name], v[name], ls.at[i])
            loads[name].start()

    def loaded(*which):
        for name in which:
            loads[name].wait()

    def seq_gather(src, dst, key):
        made = Exchange(me, lambda d: src, lambda d: dst.at[me.s], lambda d: dst.at[me.seq_at(8 - d)], ss, rs, at[key])
        made.start()
        dst[me.s] = src[...]
        return made

    def seq_scatter(src, dst, key):
        made = Exchange(
            me, lambda d: src.at[me.seq_at(d)], lambda d: dst.at[me.s], lambda d: dst.at[me.seq_at(8 - d)], ss, rs, at[key]
        )
        made.start()
        dst[me.s] = src[me.s]
        return made

    def by_row(src, dst, key):
        return [
            Exchange(
                me,
                lambda d, b=b: src.at[b, me.seq_at(d)],
                lambda d, b=b: dst.at[b, me.s],
                lambda d, b=b: dst.at[b, me.seq_at(8 - d)],
                ss,
                rs,
                at[key] + 7 * b,
            )
            for b in range(2)
        ]

    f, fl = v["f"], v["fl"]
    f[...] = jnp.zeros_like(f)
    fl[...] = jnp.zeros_like(fl)
    ga, gu, gw = v["ga"], v["gu"], v["gw"]
    ag_x = [RowsGather(seq, xl.at[b], CUT_X, ss, rs, at[f"gx{b}"], core=False) for b in range(2)]
    ag_a = RowsGather(me, ga, CUT_A, ss, rs, at["ga"])
    ag_u = RowsGather(me, gu, CUT_U, ss, rs, at["gu"])
    ag_w = RowsGather(me, gw, CUT_W, ss, rs, at["gw"])
    loaded(0)
    barrier_wait()
    ag_x[0].step0()
    loaded("wq", "g1", "b1", "g2", "b2", "ge")
    for c in range(3):
        for i in range(6):
            f[pl.ds(c * 6 + i, 1), :] = v["wq"][i, pl.ds(c, 1), :]
    fl[pl.ds(18, 1), :] = small_vec([v[name] for name in ("g1", "b1", "g2", "b2")])
    wide = nn(f[pl.ds(0, 32), :].astype(BF), v["ge"][...])
    for k in range(8):
        v["ka"][k] = (wide[:, k * 128 : (k + 1) * 128] + fl[...]).astype(BF)
    x_a = seq_scatter(v["ka"], v["xa"], "xa")
    loaded("wu", "wo", "wd")
    for j in range(4):
        f[pl.ds(32 + j * 6, 6), :] = v["wu"][:, pl.ds(j * 768, 768)]
    f[pl.ds(56, 6), :] = v["wo"][...]
    f[pl.ds(64, 24), :] = v["wd"][...]
    v["k"][0] = f[pl.ds(32, 32), :].astype(BF)
    v["k"][1] = f[pl.ds(64, 32), :].astype(BF)
    x_u = seq_gather(v["k"].at[0], v["xu"], "xu")
    x_w = seq_gather(v["k"].at[1], v["xw"], "xw")
    loaded(1, "pa", "pu", "pw", "sm", "se", "dy", "len")
    ag_x[0].step1()
    x_a.wait_recv()
    ga[me.r] = nn(v["pa"][...], v["xa"][...].reshape(256, 128)).astype(BF)
    ag_a.step0()
    ag_x[0].step2()
    for b in range(2):
        xhat, inverse = normalise(xl[b, me.s].astype(F32))
        v["xhat"][pl.ds(b * 128, 128), :] = xhat
        v["inv"][pl.ds(b * 128, 128), :] = inverse
    x_u.wait_recv()
    gu[me.r] = nn(v["pu"][...], v["xu"][...].reshape(256, 768)).astype(BF)
    ag_a.step1()
    ag_u.step0()
    ag_a.step2()
    x_w.wait_recv()
    gw[me.r] = nn(v["pw"][...], v["xw"][...].reshape(256, 768)).astype(BF)
    ag_a.step3()
    ag_w.step0()
    ag_x[1].step0()
    ag_x[0].step3()
    ag_a.step4()
    ag_a.step5()
    ag_u.step1()
    ag_a.step6()

    lnp = v["lnp"]
    ln = ga[:, pl.ds(144, 16), :].reshape(256, 128)
    for p in range(4):
        spread = nn(ln, v["se"][p])
        lnp[pl.ds(p, 1), :] = jnp.sum(spread * v["sm"][...].astype(F32), axis=0, keepdims=True)
    for c in range(3):
        w = ga[:, pl.ds(c * 48, 48), :].reshape(768, 128)
        v["wt"][pl.ds(c * 96, 96), :] = w.T[:96]

    def prepare(b, slot):
        xhat, _ = normalise(xl[b, slot].astype(F32))
        h = (xhat * lnp[pl.ds(0, 1), :] + lnp[pl.ds(1, 1), :]).astype(BF)
        v["h1"][b, slot] = h
        v["heads"][b, slot] = nt(v["wt"][...], h).astype(BF).reshape(3, 96, 128)

    def prepare_pair(b, dx, dy, step_x, step_y):
        def one(i, carry):
            prepare(b, seq.slot(dx + i * step_x, dy + i * step_y, 0))
            return carry

        lax.fori_loop(0, 2, one, 0)

    x_o = by_row(v["os"], v["ot"], "o")

    def forward(b):
        def one(h, carry):
            attend_one(v["heads"], v["len"][b], v["p"], v["l"], v["os"], b, h, b * 3 + h)
            return carry

        lax.fori_loop(0, 3, one, 0)
        x_o[b].start()
        v["ot"][b, me.s] = v["os"][b, me.s]

    prepare_pair(0, 0, 0, 0, 1)
    prepare_pair(0, 1, 0, 2, 0)
    prepare_pair(0, 1, 1, 2, 0)
    ag_w.step1()
    ag_x[1].step1()
    ag_x[0].step4()
    ag_x[0].step5()
    prepare_pair(0, 2, 0, 0, 1)
    ag_x[1].step2()
    ag_u.step2()
    forward(0)
    ag_w.step2()
    ag_x[1].step3()
    prepare_pair(1, 0, 0, 0, 1)
    prepare_pair(1, 1, 0, 2, 0)
    prepare_pair(1, 1, 1, 2, 0)
    ag_u.step3()
    ag_x[1].step4()
    ag_x[1].step5()
    prepare_pair(1, 2, 0, 0, 1)
    ag_w.step3()
    forward(1)
    ag_u.step4()
    ag_u.step5()
    for b in range(2):
        x_o[b].wait_recv()
    ag_u.step6()

    ot = jnp.concatenate([feature_major(v["ot"], b) for b in range(2)], axis=1)
    wo = gu[:, pl.ds(192, 48), :].reshape(768, 768)
    x1 = jnp.concatenate([xl[b, me.s] for b in range(2)], axis=0).astype(F32) + tn(ot, wo)
    xhat2, inverse2 = normalise(x1)
    v["xh2"][...] = xhat2
    v["h2"][...] = (xhat2 * lnp[pl.ds(2, 1), :] + lnp[pl.ds(3, 1), :]).astype(BF)
    v["y"][...] = x1
    v["dh"][...] = jnp.zeros_like(v["dh"])
    ag_w.step4()
    ag_w.step5()
    ag_w.step6()
    ag_u.finish()
    ag_w.finish()
    rs_u1 = RowsScatter(me, gu, *scr_u1, ss, rs, at["ru1"])
    rs_u2 = RowsScatter(me, gu, *scr_u2, ss, rs, at["ru2"], U1)
    rs_w = RowsScatter(me, gw, *scr_w, ss, rs, at["rw"])
    rs_a = RowsScatter(me, ga, *scr_a, ss, rs, at["ra"])
    feed_forward(0, 2, gu, gw, v["h2"], v["dy"], v["y"], v["dh"])
    rs_u1.start_core()
    feed_forward(2, 4, gu, gw, v["h2"], v["dy"], v["y"], v["dh"])
    rs_w.start_core()
    rs_u1.add_far()
    rs_u1.add_near()
    grad_in, gg2, gb2 = norm_parts(v["dh"][...], lnp[pl.ds(2, 1), :], v["xh2"][...], inverse2)
    v["lng"][pl.ds(2, 1), :] = gg2
    v["lng"][pl.ds(3, 1), :] = gb2
    dx = v["dy"][...].reshape(256, 768).astype(F32) + grad_in
    v["xh2"][...] = dx
    low = dx.astype(BF)
    d = nt(wo, low).astype(BF)
    for k in range(8):
        for b in range(2):
            v["dot"][b, k] = d[k * 96 : (k + 1) * 96, b * 128 : (b + 1) * 128]
    x_do = by_row(v["dot"], v["do"], "do")
    for b in range(2):
        x_do[b].start()
        v["do"][b, me.s] = v["dot"][b, me.s]
    rs_w.add_far()
    rs_u1.pass_near()
    gu[:, pl.ds(192, 48), :] = nn(ot, low).astype(BF).reshape(16, 48, 768)
    rs_u2.start_core()
    rs_w.add_near()
    v["h2"][...] = v["y"][...].astype(BF)
    stores = [pltpu.make_async_copy(v["h2"].at[pl.ds(b * 128, 128)], out_ref.at[b], ls.at[17 + b]) for b in range(2)]
    for b in range(2):
        stores[b].start()
    rs_u2.add_far()
    rs_u2.add_near()
    rs_w.pass_near()

    v["dwt"][...] = jnp.zeros_like(v["dwt"])
    v["lng"][pl.ds(0, 2), :] = jnp.zeros((2, 768), F32)
    dq_ref = v["dq"]

    def one_back(b, slot):
        grad = tn(dq_ref[slot].reshape(288, 128), v["wt"][...])
        v["lng"][pl.ds(0, 1), :] += jnp.sum(grad * v["h1"][b, slot].astype(F32), axis=0, keepdims=True)
        v["lng"][pl.ds(1, 1), :] += jnp.sum(grad, axis=0, keepdims=True)
        xl[b, slot] = grad.astype(BF)

    rs_x = [RowsScatter(seq, xl.at[b], None, *scr_x[b], ss, rs, at[f"rx{b}"]) for b in range(2)]

    def backward(b):
        x_do[b].wait_recv()
        ag_x[b].finish()

        def one(h, carry):
            attend_one_back(v["heads"], v["p"], v["l"], v["os"], v["do"], dq_ref, v["acc"], b, h, b * 3 + h)
            return carry

        lax.fori_loop(0, 3, one, 0)

        def far(i, carry):
            one_back(b, seq.slot(2, i, 0))
            return carry

        def near(i, carry):
            one_back(b, seq.slot((1 + 2 * (i // 2)) % 5, i, 0))
            return carry

        lax.fori_loop(0, 2, far, 0)
        rs_x[b].add_far()
        lax.fori_loop(0, 6, near, 0)
        grad = jnp.concatenate([dq_ref[i].reshape(288, 128) for i in range(8)], axis=1)
        dw = nn(grad, v["h1"][b].reshape(1024, 768))
        for c in range(3):
            v["dwt"][c, pl.ds(0, 96), :] += dw[c * 96 : (c + 1) * 96]

    backward(0)
    rs_u1.own_core()
    rs_u1.cross()
    rs_u2.pass_near()
    rs_x[0].pass_near()
    backward(1)

    def norm1_back(b):
        rows = pl.ds(b * 128, 128)
        grad = rs_x[b].last()
        grad_in, _, _ = norm_parts(grad, lnp[pl.ds(0, 1), :], v["xhat"][rows, :], v["inv"][rows, :])
        v["xhat"][rows, :] = v["xh2"][rows, :] + grad_in
        stores.append(pltpu.make_async_copy(v["xhat"].at[rows], ig_ref.at[b], ls.at[19 + b]))
        stores[2 + b].start()

    ag_a.finish()
    for c in range(3):
        ga[:, pl.ds(c * 48, 48), :] = v["dwt"][c].T.astype(BF).reshape(16, 48, 128)
    lng = v["lng"]
    lng[pl.ds(0, 1), :] = (lng[pl.ds(0, 1), :] - lnp[pl.ds(1, 1), :] * lng[pl.ds(1, 1), :]) / lnp[pl.ds(0, 1), :]
    parts = jnp.zeros((256, 128), F32)
    for p in range(4):
        parts += nt((v["sm"][...].astype(F32) * lng[pl.ds(p, 1), :]).astype(BF), v["se"][p])
    ga[:, pl.ds(144, 16), :] = parts.astype(BF).reshape(16, 16, 128)
    rs_a.start_core()
    def scatter_rows(ref, perm, rows):
        ref[...] = tn(perm[...], rows.astype(BF)).astype(BF).reshape(ref.shape)

    rs_w.own_core()
    rs_w.cross()
    rs_a.add_far()
    rs_a.add_near()
    rs_x[0].cross()
    rs_x[1].pass_near()
    rs_a.pass_near()
    rs_a.own_core()
    scatter_rows(v["xw"], v["pw"], rs_w.last())
    s_w = seq_scatter(v["xw"], v["xs"].at[1], "sw")
    rs_u2.own_core()
    rs_u2.cross()
    rs_a.cross()
    norm1_back(0)
    rs_x[1].cross()
    total = jnp.concatenate([rs_u1.last(), rs_u2.last()], axis=0)
    scatter_rows(v["xu"], v["pu"], total)
    s_u = seq_scatter(v["xu"], v["xs"].at[0], "su")
    scatter_rows(v["xa"], v["pa"], rs_a.last())
    s_a = seq_scatter(v["xa"], v["xsa"], "sa")
    norm1_back(1)
    s_w.wait_recv()
    f[pl.ds(64, 32), :] = jnp.sum(v["xs"][1].astype(F32), axis=0)
    s_a.wait_recv()
    packets = jnp.concatenate([v["xsa"][k] for k in range(8)], axis=1)
    f[pl.ds(0, 32), :] = nt(packets, v["ge"][...])
    fl[...] = jnp.sum(v["xsa"][...].astype(F32), axis=0)
    f[pl.ds(24, 1), pl.ds(0, 128)] = fl[pl.ds(18, 1), :]
    s_u.wait_recv()
    f[pl.ds(32, 32), :] = jnp.sum(v["xs"][0].astype(F32), axis=0)
    stores.append(pltpu.make_async_copy(f, sum_ref, ls.at[0]))
    stores[4].start()
    for each in (x_a, x_u, x_w, *x_o, *x_do, s_a, s_u, s_w):
        each.wait_send()
    for each in (rs_a, rs_u1, rs_u2, rs_w, *rs_x):
        each.finish()
    for store in stores:
        store.wait()


def final_kernel(out_in, ig_in, f_in, out_ref, ig_ref, dwq_ref, dwo_ref, dwu_ref, dwd_ref, ln_ref, out_v, ig_v, f_ref, sem):
    loads = [
        pltpu.make_async_copy(src, dst, sem.at[i])
        for i, (src, dst) in enumerate(((f_in, f_ref), (ig_in, ig_v), (out_in, out_v)))
    ]
    for load in loads:
        load.start()
    a = pltpu.make_async_copy(out_v, out_ref, sem.at[3])
    b = pltpu.make_async_copy(ig_v, ig_ref, sem.at[4])
    loads[1].wait()
    b.start()
    loads[2].wait()
    a.start()
    loads[0].wait()
    for c in range(3):
        for i in range(6):
            dwq_ref[i, pl.ds(c, 1), :] = f_ref[pl.ds(c * 6 + i, 1), :]
    ln_ref[...] = f_ref[pl.ds(24, 8), :]
    for j in range(4):
        dwu_ref[:, pl.ds(j * 768, 768)] = f_ref[pl.ds(32 + j * 6, 6), :]
    dwo_ref[...] = f_ref[pl.ds(56, 6), :]
    dwd_ref[...] = f_ref[pl.ds(64, 24), :]
    a.wait()
    b.wait()


def on_device(inputs, lengths, qkv_weight, out_weight, up_weight, down_weight, ln1_gain, ln1_bias, ln2_gain, ln2_bias, cotangent):
    sds = jax.ShapeDtypeStruct
    n = plan()[1]
    given = dict(
        x=inputs, dy=cotangent, wq=qkv_weight, wo=out_weight, wu=up_weight, wd=down_weight,
        g1=ln1_gain, b1=ln1_bias, g2=ln2_gain, b2=ln2_bias, len=lengths,
        pa=const(perm_a()), pu=const(perm_u()), pw=const(perm_w()), sm=const(spread_m()), se=const(spread_e()), ge=const(groups_e()),
    )
    out, ig, sums = pl.pallas_call(
        layer_kernel,
        out_shape=(sds((2, 128, 768), BF), sds((2, 128, 768), F32), sds((96, 768), F32)),
        in_specs=[HBM] * len(INPUTS),
        out_specs=[HBM] * 3,
        scratch_shapes=[
            *SCRATCH.values(),
            *SMALL.values(),
            *scatter_scratch(ROWS_A, CUT_A, 128),
            *scatter_scratch(U1, 48, 768),
            *scatter_scratch(U2, 80, 768),
            *scatter_scratch(ROWS_W, CUT_W, 768),
            *scatter_scratch(128, CUT_X, 768, core=False),
            *scatter_scratch(128, CUT_X, 768, core=False),
            pltpu.SemaphoreType.DMA((n,)),
            pltpu.SemaphoreType.DMA((n,)),
            pltpu.SemaphoreType.DMA((23,)),
        ],
        compiler_params=pltpu.CompilerParams(collective_id=0, has_side_effects=True, vmem_limit_bytes=63_000_000),
        name="layer",
    )(*[given[name] for name in INPUTS])
    res = pl.pallas_call(
        final_kernel,
        out_shape=(
            sds((2, 128, 768), BF), sds((2, 128, 768), F32), sds((6, 3, 768), F32), sds((6, 768), F32),
            sds((6, 3072), F32), sds((24, 768), F32), sds((8, 768), F32),
        ),
        in_specs=[HBM] * 3,
        out_specs=[HBM, HBM] + [VM] * 5,
        scratch_shapes=[
            pltpu.VMEM((2, 128, 768), BF),
            pltpu.VMEM((2, 128, 768), F32),
            pltpu.VMEM((96, 768), F32),
            pltpu.SemaphoreType.DMA((5,)),
        ],
        name="final",
    )(out, ig, sums)
    return (*res[:6], *[res[6][0, p * 32 : p * 32 + 6] for p in range(4)])


def solution(mesh):
    both = ("rows", "seq")
    return jax.shard_map(
        on_device,
        mesh=mesh,
        in_specs=(P("rows", "seq", None), P("rows"), P(both, None, None), P(both, None), P(both, None), P(both, None),
                  P(both), P(both), P(both), P(both), P("rows", "seq", None)),
        out_specs=(P("rows", "seq", None), P("rows", "seq", None), P(both, None, None), P(both, None), P(both, None),
                   P(both, None), P(both), P(both), P(both), P(both)),
        check_vma=False,
    )
```

```python
import functools
import math

import jax
import jax.numpy as jnp
import numpy as np
from jax import lax
from jax.experimental import pallas as pl
from jax.experimental.pallas import tpu as pltpu
from jax.sharding import PartitionSpec as P

MESH = pl.DeviceIdType.MESH
BF = jnp.bfloat16
F32 = jnp.float32
HEAD_DIM = 32
EPS = 1e-05
ROWS_A = 160
ROWS_U = 240
ROWS_W = 192
VM = pl.BlockSpec(memory_space=pltpu.VMEM)
SM = pl.BlockSpec(memory_space=pltpu.SMEM)


def perm_a():
    m = np.zeros((ROWS_A, 256), np.float32)
    for s in range(8):
        for c in range(3):
            for i in range(6):
                m[c * 48 + s * 6 + i, s * 32 + c * 6 + i] = 1
        m[144 + s, s * 32 + 18] = 1
    return m


def perm_u():
    m = np.zeros((ROWS_U, 256), np.float32)
    for s in range(8):
        for j in range(5):
            for i in range(6):
                m[j * 48 + s * 6 + i, s * 32 + j * 6 + i] = 1
    return m


def perm_w():
    m = np.zeros((ROWS_W, 256), np.float32)
    for s in range(8):
        for i in range(24):
            m[s * 24 + i, s * 32 + i] = 1
    return m


def spread_m():
    m = np.zeros((256, 768), np.float32)
    for r in range(16):
        for s in range(8):
            m[r * 16 + s, (r * 8 + s) * 6 : (r * 8 + s) * 6 + 6] = 1
    return m


def spread_e():
    m = np.zeros((4, 128, 768), np.float32)
    for p in range(4):
        for j in range(768):
            m[p, p * 32 + j % 6, j] = 1
    return m


def groups_e():
    m = np.zeros((768, 1024), np.float32)
    for j in range(768):
        m[j, j // 96 * 128 + j % 96] = 1
    return m


def const(m):
    return jnp.asarray(m, BF)


def nn(a, b):
    return lax.dot_general(a, b, (((1,), (0,)), ((), ())), preferred_element_type=F32)


def nt(a, b):
    return lax.dot_general(a, b, (((1,), (1,)), ((), ())), preferred_element_type=F32)


def tn(a, b):
    return lax.dot_general(a, b, (((0,), (0,)), ((), ())), preferred_element_type=F32)


class Place:
    def __init__(self):
        self.r = lax.axis_index("rows")
        self.s = lax.axis_index("seq")
        self.z = self.r // 4
        self.y = (self.r // 2) % 2
        self.c = self.r % 2

    def slot(self, dz, dy, dc):
        z = (self.z + dz) % 4
        y = (self.y + dy) % 2
        c = (self.c + dc) % 2
        return z * 4 + y * 2 + c

    def row_dev(self, dz, dy, dc):
        return {"rows": self.slot(dz, dy, dc)}

    def along_seq(self):
        return SeqPlace(self.s)

    def seq_at(self, d):
        return (self.s + d) % 8

    def seq_dev(self, d):
        return {"seq": self.seq_at(d)}


class SeqPlace:
    def __init__(self, s):
        self.s = s

    def slot(self, dx, dy, dc):
        return (self.s // 4 + dy) % 2 * 4 + (self.s + dx) % 4

    def row_dev(self, dx, dy, dc):
        return {"seq": self.slot(dx, dy, dc)}


NEAR = ((1, 0), (3, 0), (0, 1), (1, 1), (3, 1), (2, 0), (2, 1))
ROW_PEERS = ((0, 0, 1), *[(dz, dy, 0) for dz, dy in NEAR])


def barrier_signal(me):
    sem = pltpu.get_barrier_semaphore()
    for p in ROW_PEERS:
        pl.semaphore_signal(sem, inc=1, device_id=me.row_dev(*p), device_id_type=MESH)
    for d in range(1, 8):
        pl.semaphore_signal(sem, inc=1, device_id=me.seq_dev(d), device_id_type=MESH)


def barrier_wait():
    pl.semaphore_wait(pltpu.get_barrier_semaphore(), len(ROW_PEERS) + 7)


def remote(src, dst, ss, rs, dev):
    return pltpu.make_async_remote_copy(
        src_ref=src, dst_ref=dst, send_sem=ss, recv_sem=rs, device_id=dev, device_id_type=MESH
    )


class Exchange:
    def __init__(self, me, src, dst, land, ss, rs, base):
        self.me, self.src, self.dst, self.land = me, src, dst, land
        self.ss, self.rs, self.base = ss, rs, base

    def _copy(self, d):
        return remote(
            self.src(d),
            self.dst(d),
            self.ss.at[self.base + d - 1],
            self.rs.at[self.base + d - 1],
            self.me.seq_dev(d),
        )

    def start(self):
        for d in range(1, 8):
            self._copy(d).start()

    def wait_recv(self):
        for d in range(1, 8):
            here = self.land(d)
            remote(
                here, here, self.ss.at[self.base + d - 1], self.rs.at[self.base + d - 1], self.me.seq_dev(d)
            ).wait_recv()

    def wait_send(self):
        for d in range(1, 8):
            self._copy(d).wait_send()


GATHER_SEMS = 17


class RowsGather:
    def __init__(self, me, buf, cut, ss, rs, base, core=True):
        self.me, self.buf, self.cut, self.core = me, buf, cut, core
        self.ss, self.rs, self.base = ss, rs, base
        self.sent = []

    def _part(self, rel, part):
        slot = self.me.slot(*rel)
        full = self.buf.shape[1]
        if part == 0:
            return self.buf.at[slot]
        if part == 1:
            return self.buf.at[slot, pl.ds(0, self.cut)]
        return self.buf.at[slot, pl.ds(self.cut, full - self.cut)]

    PLAN = {
        "y": (0, (0, 1, 0), (0, 0, 0), 0),
        "p0": (1, (1, 0, 0), (0, 0, 0), 0),
        "m0": (2, (3, 0, 0), (0, 0, 0), 0),
        "p1": (3, (1, 0, 0), (0, 1, 0), 0),
        "m1": (4, (3, 0, 0), (0, 1, 0), 0),
        "fp0": (5, (1, 0, 0), (3, 0, 0), 1),
        "fm0": (6, (3, 0, 0), (1, 0, 0), 2),
        "fp1": (7, (1, 0, 0), (3, 1, 0), 1),
        "fm1": (8, (3, 0, 0), (1, 1, 0), 2),
        "c00": (9, (0, 0, 1), (0, 0, 0), 0),
        "c01": (10, (0, 0, 1), (0, 1, 0), 0),
        "c10": (11, (0, 0, 1), (1, 0, 0), 0),
        "c11": (12, (0, 0, 1), (1, 1, 0), 0),
        "c20": (13, (0, 0, 1), (2, 0, 0), 0),
        "c21": (14, (0, 0, 1), (2, 1, 0), 0),
        "c30": (15, (0, 0, 1), (3, 0, 0), 0),
        "c31": (16, (0, 0, 1), (3, 1, 0), 0),
    }

    def _send(self, name):
        i, to, block, part = self.PLAN[name]
        ref = self._part(block, part)
        return remote(ref, ref, self.ss.at[self.base + i], self.rs.at[self.base + i], self.me.row_dev(*to))

    def send(self, *names):
        for name in names:
            if self.core or name[0] != "c":
                self._send(name).start()
                self.sent.append(name)

    def recv(self, *names):
        for name in names:
            i, to, block, part = self.PLAN[name]
            rel = ((block[0] - to[0]) % 4, (block[1] - to[1]) % 2, (block[2] - to[2]) % 2)
            ref = self._part(rel, part)
            remote(ref, ref, self.ss.at[self.base + i], self.rs.at[self.base + i], self.me.row_dev(*to)).wait_recv()

    def step0(self):
        self.send("p0", "m0", "y", "c00")

    def step1(self):
        self.recv("y")
        self.send("p1", "m1", "c01")

    def step2(self):
        self.recv("p0")
        self.send("fp0", "c30")
        self.recv("m0")
        self.send("fm0", "c10")

    def step3(self):
        self.recv("p1")
        self.send("fp1", "c31")
        self.recv("m1")
        self.send("fm1", "c11")

    def step4(self):
        self.recv("fp0", "fm0")
        self.send("c20")

    def step5(self):
        self.recv("fp1", "fm1")
        self.send("c21")

    def step6(self):
        self.recv("c00", "c01", "c10", "c11", "c20", "c21", "c30", "c31")

    def finish(self):
        for name in self.sent:
            self._send(name).wait_send()


class RowsScatter:
    def __init__(self, me, g, cr, zlo, zhi, zr, yr, ss, rs, base, first=0):
        self.me, self.g, self.cr, self.zlo, self.zhi, self.zr, self.yr = me, g, cr, zlo, zhi, zr, yr
        self.ss, self.rs, self.base = ss, rs, base
        cut, rows = zlo.shape[1], yr.shape[0]
        self.all, self.lo, self.hi = pl.ds(first, rows), pl.ds(first, cut), pl.ds(first + cut, rows - cut)
        self.open = []

    def _copy(self, i, src, dst, to):
        return remote(src, dst, self.ss.at[self.base + i], self.rs.at[self.base + i], self.me.row_dev(*to))

    def _start(self, i, src, dst, to):
        copy = self._copy(i, src, dst, to)
        copy.start()
        self.open.append(copy)

    def _landed(self, i, dst, to):
        self._copy(i, dst, dst, to).wait_recv()

    ORDER = ((2, 0), (2, 1), (1, 0), (1, 1), (3, 0), (3, 1), (0, 1), (0, 0))

    def start_core(self):
        for k, (dz, dy) in enumerate(self.ORDER):
            self._start(k, self.g.at[self.me.slot(dz, dy, 1), self.all], self.cr.at[k], (0, 0, 1))

    def _add(self, k):
        if self.cr is None:
            return
        dz, dy = self.ORDER[k]
        self._landed(k, self.cr.at[k], (0, 0, 1))
        slot = self.me.slot(dz, dy, 0)
        self.g[slot, self.all] = (self.g[slot, self.all].astype(F32) + self.cr[k].astype(F32)).astype(BF)

    def add_far(self):
        for dy in (0, 1):
            self._add(dy)
            slot = self.me.slot(2, dy, 0)
            self._start(8 + dy, self.g.at[slot, self.lo], self.zlo.at[dy], (1, 0, 0))
            self._start(10 + dy, self.g.at[slot, self.hi], self.zhi.at[dy], (3, 0, 0))

    def add_near(self):
        for k in (2, 3, 4, 5):
            self._add(k)

    def pass_near(self):
        for dy in (1, 0):
            self._landed(8 + dy, self.zlo.at[dy], (1, 0, 0))
            slot = self.me.slot(1, dy, 0)
            self.g[slot, self.lo] = (self.g[slot, self.lo].astype(F32) + self.zlo[dy].astype(F32)).astype(BF)
            self._start(12 + 2 * dy, self.g.at[slot, self.all], self.zr.at[0, dy], (1, 0, 0))
            self._landed(10 + dy, self.zhi.at[dy], (3, 0, 0))
            slot = self.me.slot(3, dy, 0)
            self.g[slot, self.hi] = (self.g[slot, self.hi].astype(F32) + self.zhi[dy].astype(F32)).astype(BF)
            self._start(13 + 2 * dy, self.g.at[slot, self.all], self.zr.at[1, dy], (3, 0, 0))

    def own_core(self):
        self._add(6)
        self._add(7)

    def cross(self):
        self._landed(14, self.zr.at[0, 1], (1, 0, 0))
        self._landed(15, self.zr.at[1, 1], (3, 0, 0))
        slot = self.me.slot(0, 1, 0)
        total = self.g[slot, self.all].astype(F32) + self.zr[0, 1].astype(F32) + self.zr[1, 1].astype(F32)
        self.g[slot, self.all] = total.astype(BF)
        self._start(16, self.g.at[slot, self.all], self.yr, (0, 1, 0))

    def last(self):
        self._landed(12, self.zr.at[0, 0], (1, 0, 0))
        self._landed(13, self.zr.at[1, 0], (3, 0, 0))
        self._landed(16, self.yr, (0, 1, 0))
        slot = self.me.slot(0, 0, 0)
        return (
            self.g[slot, self.all].astype(F32)
            + self.zr[0, 0].astype(F32)
            + self.zr[1, 0].astype(F32)
            + self.yr[...].astype(F32)
        )

    def finish(self):
        for copy in self.open:
            copy.wait_send()


SCATTER_SEMS = 17


class DirectGather:
    SEMS = 15

    def __init__(self, me, buf, ss, rs, base):
        self.me, self.buf, self.ss, self.rs, self.base = me, buf, ss, rs, base
        self.open = []

    def _copy(self, i, rel, to):
        block = self.buf.at[self.me.slot(*rel)]
        return remote(block, block, self.ss.at[self.base + i], self.rs.at[self.base + i], self.me.row_dev(*to))

    def _start(self, i, rel, to):
        copy = self._copy(i, rel, to)
        copy.start()
        self.open.append(copy)

    def start(self):
        for k, (dz, dy) in enumerate(NEAR):
            self._start(k, (0, 0, 0), (dz, dy, 0))
        self._start(7, (0, 0, 0), (0, 0, 1))

    def share(self):
        for k, (dz, dy) in enumerate(NEAR):
            self._copy(k, (4 - dz, dy, 0), (dz, dy, 0)).wait_recv()
            self._start(8 + k, (4 - dz, dy, 0), (0, 0, 1))

    def wait(self):
        self._copy(7, (0, 0, 1), (0, 0, 1)).wait_recv()
        for k, (dz, dy) in enumerate(NEAR):
            self._copy(8 + k, (4 - dz, dy, 1), (0, 0, 1)).wait_recv()

    def finish(self):
        for copy in self.open:
            copy.wait_send()


class DirectScatter:
    SEMS = 15

    def __init__(self, me, g, cr, dr, ss, rs, base):
        self.me, self.g, self.cr, self.dr, self.ss, self.rs, self.base = me, g, cr, dr, ss, rs, base
        self.open = []

    def _copy(self, i, src, dst, to):
        return remote(src, dst, self.ss.at[self.base + i], self.rs.at[self.base + i], self.me.row_dev(*to))

    def _start(self, i, src, dst, to):
        copy = self._copy(i, src, dst, to)
        copy.start()
        self.open.append(copy)

    def start_core(self):
        for k, (dz, dy) in enumerate((*NEAR, (0, 0))):
            self._start(k, self.g.at[self.me.slot(dz, dy, 1)], self.cr.at[k], (0, 0, 1))

    def send(self):
        for k, (dz, dy) in enumerate((*NEAR, (0, 0))):
            self._copy(k, self.cr.at[k], self.cr.at[k], (0, 0, 1)).wait_recv()
            slot = self.me.slot(dz, dy, 0)
            self.g[slot] = (self.g[slot].astype(F32) + self.cr[k].astype(F32)).astype(BF)
            if k < 7:
                self._start(8 + k, self.g.at[slot], self.dr.at[k], (dz, dy, 0))

    def last(self):
        total = self.g[self.me.slot(0, 0, 0)].astype(F32)
        for k, (dz, dy) in enumerate(NEAR):
            self._copy(8 + k, self.dr.at[k], self.dr.at[k], (dz, dy, 0)).wait_recv()
            total += self.dr[k].astype(F32)
        return total

    def finish(self):
        for copy in self.open:
            copy.wait_send()


def small_vec(refs):
    lane = lax.broadcasted_iota(jnp.int32, (1, 128), 1)
    out = jnp.zeros((1, 128), F32)
    for p, ref in enumerate(refs):
        for i in range(6):
            out = jnp.where(lane == p * 32 + i, ref[i], out)
    return out


def normalise(v):
    mean = jnp.mean(v, axis=-1, keepdims=True)
    centred = v - mean
    var = jnp.mean(centred * centred, axis=-1, keepdims=True)
    inverse = lax.rsqrt(var + EPS)
    return centred * inverse, inverse


SCALE = HEAD_DIM**-0.5
LOG2E = 1.4426950408889634
BASE = (0, 256, 768, 1536)


def lanes(ref, b, c, h, first, count):
    rows = pl.ds(pl.multiple_of(h * 32, 32), 32)
    if c is None:
        parts = [ref[b, first + i, rows, :] for i in range(count)]
    else:
        parts = [ref[b, first + i, c, rows, :] for i in range(count)]
    return parts[0] if count == 1 else jnp.concatenate(parts, axis=1)


def allowed(nk, length):
    key = lax.broadcasted_iota(jnp.int32, (nk, 256), 0)
    query = lax.broadcasted_iota(jnp.int32, (nk, 256), 1) + (nk - 256)
    return (key <= query) & (key < length)


def attend_one(heads_ref, length, p_ref, l_ref, os_ref, b, h, i):
    rows = pl.ds(pl.multiple_of(h * 32, 32), 32)
    kt = lanes(heads_ref, b, 1, h, 0, 8)
    vt = lanes(heads_ref, b, 2, h, 0, 8)
    for qb in range(4):
        nk = (qb + 1) * 256
        qt = lanes(heads_ref, b, 0, h, 2 * qb, 2)
        s = tn(kt[:, :nk], qt)
        s = jnp.where(allowed(nk, length), s, -1e30)
        top = jnp.max(s, axis=0, keepdims=True)
        p = jnp.exp2((s - top) * (SCALE * LOG2E))
        inverse = 1.0 / jnp.sum(p, axis=0, keepdims=True)
        low = p.astype(BF)
        p_ref[i, pl.ds(BASE[qb], nk), :] = low
        l_ref[i, pl.ds(qb, 1), :] = inverse
        o = (nn(vt[:, :nk], low) * inverse).astype(BF)
        os_ref[b, 2 * qb, rows, :] = o[:, :128]
        os_ref[b, 2 * qb + 1, rows, :] = o[:, 128:]


def attend_one_back(heads_ref, p_ref, l_ref, os_ref, do_ref, dq_ref, acc_ref, b, h, i):
    rows = pl.ds(pl.multiple_of(h * 32, 32), 32)
    kt = lanes(heads_ref, b, 1, h, 0, 8)
    vt = lanes(heads_ref, b, 2, h, 0, 8)
    for qb in range(4):
        nk = (qb + 1) * 256
        qt = lanes(heads_ref, b, 0, h, 2 * qb, 2)
        do = lanes(do_ref, b, None, h, 2 * qb, 2).astype(F32) * l_ref[i, pl.ds(qb, 1), :]
        o = lanes(os_ref, b, None, h, 2 * qb, 2).astype(F32)
        delta = jnp.sum(do * o, axis=0, keepdims=True)
        low = do.astype(BF)
        p = p_ref[i, pl.ds(BASE[qb], nk), :]
        ds = (p.astype(F32) * (tn(vt[:, :nk], low) - delta)).astype(BF)
        dv = nt(low, p)
        dk = nt(qt, ds)
        if nk > 256:
            acc_ref[0, :, : nk - 256] += dk[:, : nk - 256]
            acc_ref[1, :, : nk - 256] += dv[:, : nk - 256]
        acc_ref[0, :, nk - 256 : nk] = dk[:, nk - 256 :]
        acc_ref[1, :, nk - 256 : nk] = dv[:, nk - 256 :]
        dq = (nn(kt[:, :nk], ds) * SCALE).astype(BF)
        dq_ref[2 * qb, 0, rows, :] = dq[:, :128]
        dq_ref[2 * qb + 1, 0, rows, :] = dq[:, 128:]
    for j in range(8):
        dq_ref[j, 1, rows, :] = (acc_ref[0, :, j * 128 : (j + 1) * 128] * SCALE).astype(BF)
        dq_ref[j, 2, rows, :] = acc_ref[1, :, j * 128 : (j + 1) * 128].astype(BF)


def feed_forward(first, end, gu_ref, gw_ref, h2_ref, dy_ref, y_ref, dh_ref):
    def block(j, carry):
        up = pl.ds(pl.multiple_of(j * 48, 16), 48)
        deep = pl.ds(j * 4, 4)
        wu = gu_ref[:, up, :].reshape(768, 768)
        h2 = h2_ref[...]
        u = nn(h2, wu)
        phi = 0.5 + 0.5 * lax.erf(u * (1.0 / math.sqrt(2.0)))
        act = (u * phi).astype(BF)
        slope = phi + u * jnp.exp(-0.5 * u * u) * (1.0 / math.sqrt(2.0 * math.pi))
        wd = gw_ref[deep].reshape(768, 768)
        dy = dy_ref[...].reshape(256, 768)
        y_ref[...] += nn(act, wd)
        du = (nt(dy, wd) * slope).astype(BF)
        gw_ref[deep] = tn(act, dy).astype(BF).reshape(4, 192, 768)
        dh_ref[...] += nt(du, wu)
        gu_ref[:, up, :] = tn(h2, du).astype(BF).reshape(16, 48, 768)
        return carry

    lax.fori_loop(first, end, block, 0)


def norm_parts(grad, gain, scaled, inverse):
    weighted = grad * gain
    first = jnp.mean(weighted, axis=-1, keepdims=True)
    second = jnp.mean(weighted * scaled, axis=-1, keepdims=True)
    grad_in = inverse * (weighted - first - scaled * second)
    return grad_in, jnp.sum(grad * scaled, axis=0, keepdims=True), jnp.sum(grad, axis=0, keepdims=True)


HBM = pl.BlockSpec(memory_space=pl.ANY)


class Counter:
    def __init__(self):
        self.n = 0

    def take(self, k):
        first = self.n
        self.n += k
        return first


def plan():
    c = Counter()
    at = {}
    for name in ("xa", "xu", "xw", "sa", "su", "sw"):
        at[name] = c.take(7)
    for name in ("ga", "gu", "gw", "gx0", "gx1"):
        at[name] = c.take(GATHER_SEMS)
    for name in ("o", "do"):
        at[name] = c.take(14)
    for name in ("ra", "ru1", "ru2", "rw", "rx0", "rx1"):
        at[name] = c.take(SCATTER_SEMS)
    return at, c.n


def scatter_scratch(rows, cut, wide, core=True):
    made = [
        pltpu.VMEM((2, cut, wide), BF),
        pltpu.VMEM((2, rows - cut, wide), BF),
        pltpu.VMEM((2, 2, rows, wide), BF),
        pltpu.VMEM((rows, wide), BF),
    ]
    return ([pltpu.VMEM((8, rows, wide), BF)] if core else []) + made


CUT_U, CUT_W, CUT_X = 128, 96, 64
U1, U2 = 96, 144
SCRATCH = dict(
    xl=pltpu.VMEM((2, 8, 128, 768), BF),
    h1=pltpu.VMEM((2, 8, 128, 768), BF),
    dy=pltpu.VMEM((2, 128, 768), BF),
    wq=pltpu.VMEM((6, 3, 768), F32),
    wo=pltpu.VMEM((6, 768), F32),
    wu=pltpu.VMEM((6, 3072), F32),
    wd=pltpu.VMEM((24, 768), F32),
    pa=pltpu.VMEM((ROWS_A, 256), BF),
    pu=pltpu.VMEM((ROWS_U, 256), BF),
    pw=pltpu.VMEM((ROWS_W, 256), BF),
    sm=pltpu.VMEM((256, 768), BF),
    se=pltpu.VMEM((4, 128, 768), BF),
    ge=pltpu.VMEM((768, 1024), BF),
    f=pltpu.VMEM((96, 768), F32),
    fl=pltpu.VMEM((32, 128), F32),
    ka=pltpu.VMEM((8, 32, 128), BF),
    k=pltpu.VMEM((2, 32, 768), BF),
    xa=pltpu.VMEM((8, 32, 128), BF),
    xu=pltpu.VMEM((8, 32, 768), BF),
    xw=pltpu.VMEM((8, 32, 768), BF),
    ga=pltpu.VMEM((16, ROWS_A, 128), BF),
    gu=pltpu.VMEM((16, ROWS_U, 768), BF),
    gw=pltpu.VMEM((16, ROWS_W, 768), BF),
    lnp=pltpu.VMEM((8, 768), F32),
    wt=pltpu.VMEM((288, 768), BF),
    dwt=pltpu.VMEM((3, 128, 768), F32),
    xhat=pltpu.VMEM((256, 768), F32),
    inv=pltpu.VMEM((256, 1), F32),
    heads=pltpu.VMEM((2, 8, 3, 96, 128), BF),
    p=pltpu.VMEM((6, 2560, 256), BF),
    l=pltpu.VMEM((6, 4, 256), F32),
    os=pltpu.VMEM((2, 8, 96, 128), BF),
    ot=pltpu.VMEM((2, 8, 96, 128), BF),
    h2=pltpu.VMEM((256, 768), BF),
    xh2=pltpu.VMEM((256, 768), F32),
    y=pltpu.VMEM((256, 768), F32),
    dh=pltpu.VMEM((256, 768), F32),
    dot=pltpu.VMEM((2, 8, 96, 128), BF),
    do=pltpu.VMEM((2, 8, 96, 128), BF),
    acc=pltpu.VMEM((2, 32, 1024), F32),
    dq=pltpu.VMEM((8, 3, 96, 128), BF),
    lng=pltpu.VMEM((8, 768), F32),
    xsa=pltpu.VMEM((8, 32, 128), BF),
    xs=pltpu.VMEM((2, 8, 32, 768), BF),
)
SMALL = dict(
    len=pltpu.SMEM((2,), jnp.int32),
    g1=pltpu.SMEM((6,), F32),
    b1=pltpu.SMEM((6,), F32),
    g2=pltpu.SMEM((6,), F32),
    b2=pltpu.SMEM((6,), F32),
)
INPUTS = ("x", "wq", "g1", "b1", "g2", "b2", "ge", "wu", "wo", "wd", "pa", "pu", "pw", "sm", "se", "dy", "len")


def feature_major(ref, b):
    return ref[b].reshape(768, 128)


def layer_kernel(*refs):
    inputs = dict(zip(INPUTS, refs))
    refs = refs[len(INPUTS) :]
    out_ref, ig_ref, sum_ref = refs[:3]
    names = [*SCRATCH, *SMALL]
    v = dict(zip(names, refs[3 : 3 + len(names)]))
    rest = refs[3 + len(names) :]
    scr_a, scr_u1, scr_u2, scr_w = rest[:2], rest[2:7], rest[7:12], rest[12:17]
    scr_x = (rest[17:21], rest[21:25])
    ss, rs, ls = rest[25:]
    at, _ = plan()
    me = Place()
    seq = me.along_seq()
    barrier_signal(me)
    xl = v["xl"]
    loads = {}
    for b in range(2):
        loads[b] = pltpu.make_async_copy(inputs["x"].at[b], xl.at[b, me.s], ls.at[21 + b])
        loads[b].start()
    for i, name in enumerate(INPUTS):
        if name != "x":
            loads[name] = pltpu.make_async_copy(inputs[name], v[name], ls.at[i])
            loads[name].start()

    def loaded(*which):
        for name in which:
            loads[name].wait()

    def seq_gather(src, dst, key):
        made = Exchange(me, lambda d: src, lambda d: dst.at[me.s], lambda d: dst.at[me.seq_at(8 - d)], ss, rs, at[key])
        made.start()
        dst[me.s] = src[...]
        return made

    def seq_scatter(src, dst, key):
        made = Exchange(
            me, lambda d: src.at[me.seq_at(d)], lambda d: dst.at[me.s], lambda d: dst.at[me.seq_at(8 - d)], ss, rs, at[key]
        )
        made.start()
        dst[me.s] = src[me.s]
        return made

    def by_row(src, dst, key):
        return [
            Exchange(
                me,
                lambda d, b=b: src.at[b, me.seq_at(d)],
                lambda d, b=b: dst.at[b, me.s],
                lambda d, b=b: dst.at[b, me.seq_at(8 - d)],
                ss,
                rs,
                at[key] + 7 * b,
            )
            for b in range(2)
        ]

    f, fl = v["f"], v["fl"]
    f[...] = jnp.zeros_like(f)
    fl[...] = jnp.zeros_like(fl)
    ga, gu, gw = v["ga"], v["gu"], v["gw"]
    ag_x = [RowsGather(seq, xl.at[b], CUT_X, ss, rs, at[f"gx{b}"], core=False) for b in range(2)]
    ag_a = DirectGather(me, ga, ss, rs, at["ga"])
    ag_u = RowsGather(me, gu, CUT_U, ss, rs, at["gu"])
    ag_w = RowsGather(me, gw, CUT_W, ss, rs, at["gw"])
    loaded("wq", "g1", "b1", "g2", "b2", "ge")
    for c in range(3):
        for i in range(6):
            f[pl.ds(c * 6 + i, 1), :] = v["wq"][i, pl.ds(c, 1), :]
    fl[pl.ds(18, 1), :] = small_vec([v[name] for name in ("g1", "b1", "g2", "b2")])
    wide = nn(f[pl.ds(0, 32), :].astype(BF), v["ge"][...])
    for k in range(8):
        v["ka"][k] = (wide[:, k * 128 : (k + 1) * 128] + fl[...]).astype(BF)
    loaded("wu", "wo", "wd")
    for j in range(4):
        f[pl.ds(32 + j * 6, 6), :] = v["wu"][:, pl.ds(j * 768, 768)]
    f[pl.ds(56, 6), :] = v["wo"][...]
    f[pl.ds(64, 24), :] = v["wd"][...]
    v["k"][0] = f[pl.ds(32, 32), :].astype(BF)
    v["k"][1] = f[pl.ds(64, 32), :].astype(BF)
    loaded(0, 1, "pa", "pu", "pw", "sm", "se", "dy", "len")
    barrier_wait()
    x_a = seq_scatter(v["ka"], v["xa"], "xa")
    x_u = seq_gather(v["k"].at[0], v["xu"], "xu")
    x_w = seq_gather(v["k"].at[1], v["xw"], "xw")
    ag_x[0].step0()
    x_a.wait_recv()
    ga[me.r] = nn(v["pa"][...], v["xa"][...].reshape(256, 128)).astype(BF)
    ag_a.start()
    x_u.wait_recv()
    gu[me.r] = nn(v["pu"][...], v["xu"][...].reshape(256, 768)).astype(BF)
    ag_u.step0()
    ag_a.share()
    x_w.wait_recv()
    gw[me.r] = nn(v["pw"][...], v["xw"][...].reshape(256, 768)).astype(BF)
    ag_w.step0()
    ag_x[0].step1()
    ag_x[0].step2()
    ag_x[1].step0()
    for b in range(2):
        xhat, inverse = normalise(xl[b, me.s].astype(F32))
        v["xhat"][pl.ds(b * 128, 128), :] = xhat
        v["inv"][pl.ds(b * 128, 128), :] = inverse
    ag_a.wait()
    ag_u.step1()

    lnp = v["lnp"]
    ln = ga[:, pl.ds(144, 16), :].reshape(256, 128)
    for p in range(4):
        spread = nn(ln, v["se"][p])
        lnp[pl.ds(p, 1), :] = jnp.sum(spread * v["sm"][...].astype(F32), axis=0, keepdims=True)
    for c in range(3):
        w = ga[:, pl.ds(c * 48, 48), :].reshape(768, 128)
        v["wt"][pl.ds(c * 96, 96), :] = w.T[:96]

    def prepare(b, slot):
        xhat, _ = normalise(xl[b, slot].astype(F32))
        h = (xhat * lnp[pl.ds(0, 1), :] + lnp[pl.ds(1, 1), :]).astype(BF)
        v["h1"][b, slot] = h
        v["heads"][b, slot] = nt(v["wt"][...], h).astype(BF).reshape(3, 96, 128)

    def prepare_pair(b, dx, dy, step_x, step_y):
        def one(i, carry):
            prepare(b, seq.slot(dx + i * step_x, dy + i * step_y, 0))
            return carry

        lax.fori_loop(0, 2, one, 0)

    x_o = by_row(v["os"], v["ot"], "o")

    def forward(b):
        def one(h, carry):
            attend_one(v["heads"], v["len"][b], v["p"], v["l"], v["os"], b, h, b * 3 + h)
            return carry

        lax.fori_loop(0, 3, one, 0)
        x_o[b].start()
        v["ot"][b, me.s] = v["os"][b, me.s]

    prepare_pair(0, 0, 0, 0, 1)
    ag_x[0].step3()
    prepare_pair(0, 1, 0, 2, 0)
    prepare_pair(0, 1, 1, 2, 0)
    ag_w.step1()
    ag_x[1].step1()
    ag_x[0].step4()
    ag_x[0].step5()
    prepare_pair(0, 2, 0, 0, 1)
    ag_x[1].step2()
    ag_u.step2()
    forward(0)
    ag_w.step2()
    ag_x[1].step3()
    prepare_pair(1, 0, 0, 0, 1)
    prepare_pair(1, 1, 0, 2, 0)
    prepare_pair(1, 1, 1, 2, 0)
    ag_u.step3()
    ag_x[1].step4()
    ag_x[1].step5()
    prepare_pair(1, 2, 0, 0, 1)
    ag_w.step3()
    forward(1)
    ag_u.step4()
    ag_u.step5()
    for b in range(2):
        x_o[b].wait_recv()
    ag_u.step6()

    ot = jnp.concatenate([feature_major(v["ot"], b) for b in range(2)], axis=1)
    wo = gu[:, pl.ds(192, 48), :].reshape(768, 768)
    x1 = jnp.concatenate([xl[b, me.s] for b in range(2)], axis=0).astype(F32) + tn(ot, wo)
    xhat2, inverse2 = normalise(x1)
    v["xh2"][...] = xhat2
    v["h2"][...] = (xhat2 * lnp[pl.ds(2, 1), :] + lnp[pl.ds(3, 1), :]).astype(BF)
    v["y"][...] = x1
    v["dh"][...] = jnp.zeros_like(v["dh"])
    ag_w.step4()
    ag_w.step5()
    ag_w.step6()
    ag_u.finish()
    ag_w.finish()
    rs_u1 = RowsScatter(me, gu, *scr_u1, ss, rs, at["ru1"])
    rs_u2 = RowsScatter(me, gu, *scr_u2, ss, rs, at["ru2"], U1)
    rs_w = RowsScatter(me, gw, *scr_w, ss, rs, at["rw"])
    rs_a = DirectScatter(me, ga, *scr_a, ss, rs, at["ra"])
    feed_forward(0, 2, gu, gw, v["h2"], v["dy"], v["y"], v["dh"])
    rs_u1.start_core()
    feed_forward(2, 4, gu, gw, v["h2"], v["dy"], v["y"], v["dh"])
    rs_w.start_core()
    rs_u1.add_far()
    rs_u1.add_near()
    grad_in, gg2, gb2 = norm_parts(v["dh"][...], lnp[pl.ds(2, 1), :], v["xh2"][...], inverse2)
    v["lng"][pl.ds(2, 1), :] = gg2
    v["lng"][pl.ds(3, 1), :] = gb2
    dx = v["dy"][...].reshape(256, 768).astype(F32) + grad_in
    v["xh2"][...] = dx
    low = dx.astype(BF)
    d = nt(wo, low).astype(BF)
    for k in range(8):
        for b in range(2):
            v["dot"][b, k] = d[k * 96 : (k + 1) * 96, b * 128 : (b + 1) * 128]
    x_do = by_row(v["dot"], v["do"], "do")
    for b in range(2):
        x_do[b].start()
        v["do"][b, me.s] = v["dot"][b, me.s]
    rs_w.add_far()
    rs_u1.pass_near()
    gu[:, pl.ds(192, 48), :] = nn(ot, low).astype(BF).reshape(16, 48, 768)
    rs_u2.start_core()
    rs_w.add_near()
    v["h2"][...] = v["y"][...].astype(BF)
    stores = [pltpu.make_async_copy(v["h2"].at[pl.ds(b * 128, 128)], out_ref.at[b], ls.at[17 + b]) for b in range(2)]
    for b in range(2):
        stores[b].start()
    rs_u2.add_far()
    rs_u2.add_near()

    v["dwt"][...] = jnp.zeros_like(v["dwt"])
    v["lng"][pl.ds(0, 2), :] = jnp.zeros((2, 768), F32)
    dq_ref = v["dq"]

    def one_back(b, slot):
        grad = tn(dq_ref[slot].reshape(288, 128), v["wt"][...])
        v["lng"][pl.ds(0, 1), :] += jnp.sum(grad * v["h1"][b, slot].astype(F32), axis=0, keepdims=True)
        v["lng"][pl.ds(1, 1), :] += jnp.sum(grad, axis=0, keepdims=True)
        xl[b, slot] = grad.astype(BF)

    rs_x = [RowsScatter(seq, xl.at[b], None, *scr_x[b], ss, rs, at[f"rx{b}"]) for b in range(2)]

    def backward(b, between):
        x_do[b].wait_recv()
        ag_x[b].finish()

        def one(h, carry):
            attend_one_back(v["heads"], v["p"], v["l"], v["os"], v["do"], dq_ref, v["acc"], b, h, b * 3 + h)
            return carry

        lax.fori_loop(0, 3, one, 0)
        between()

        def far(i, carry):
            one_back(b, seq.slot(2, i, 0))
            return carry

        def near(i, carry):
            one_back(b, seq.slot((1 + 2 * (i // 2)) % 5, i, 0))
            return carry

        lax.fori_loop(0, 2, far, 0)
        rs_x[b].add_far()
        lax.fori_loop(0, 6, near, 0)
        grad = jnp.concatenate([dq_ref[i].reshape(288, 128) for i in range(8)], axis=1)
        dw = nn(grad, v["h1"][b].reshape(1024, 768))
        for c in range(3):
            v["dwt"][c, pl.ds(0, 96), :] += dw[c * 96 : (c + 1) * 96]

    def between():
        rs_u2.pass_near()
        rs_x[0].pass_near()
        rs_w.own_core()

    backward(0, rs_w.pass_near)
    rs_u1.own_core()
    rs_u1.cross()
    backward(1, between)

    def norm1_back(b):
        rows = pl.ds(b * 128, 128)
        grad = rs_x[b].last()
        grad_in, _, _ = norm_parts(grad, lnp[pl.ds(0, 1), :], v["xhat"][rows, :], v["inv"][rows, :])
        v["xhat"][rows, :] = v["xh2"][rows, :] + grad_in
        stores.append(pltpu.make_async_copy(v["xhat"].at[rows], ig_ref.at[b], ls.at[19 + b]))
        stores[2 + b].start()

    ag_a.finish()
    for c in range(3):
        ga[:, pl.ds(c * 48, 48), :] = v["dwt"][c].T.astype(BF).reshape(16, 48, 128)
    lng = v["lng"]
    lng[pl.ds(0, 1), :] = (lng[pl.ds(0, 1), :] - lnp[pl.ds(1, 1), :] * lng[pl.ds(1, 1), :]) / lnp[pl.ds(0, 1), :]
    parts = jnp.zeros((256, 128), F32)
    for p in range(4):
        parts += nt((v["sm"][...].astype(F32) * lng[pl.ds(p, 1), :]).astype(BF), v["se"][p])
    ga[:, pl.ds(144, 16), :] = parts.astype(BF).reshape(16, 16, 128)
    rs_a.start_core()
    def scatter_rows(ref, perm, rows):
        ref[...] = tn(perm[...], rows.astype(BF)).astype(BF).reshape(ref.shape)

    rs_a.send()
    rs_w.cross()
    rs_x[1].pass_near()
    rs_u2.own_core()
    rs_x[0].cross()
    rs_u2.cross()
    scatter_rows(v["xw"], v["pw"], rs_w.last())
    s_w = seq_scatter(v["xw"], v["xs"].at[1], "sw")
    rs_x[1].cross()
    scatter_rows(v["xa"], v["pa"], rs_a.last())
    s_a = seq_scatter(v["xa"], v["xsa"], "sa")
    norm1_back(0)
    total = jnp.concatenate([rs_u1.last(), rs_u2.last()], axis=0)
    scatter_rows(v["xu"], v["pu"], total)
    s_u = seq_scatter(v["xu"], v["xs"].at[0], "su")
    norm1_back(1)
    s_w.wait_recv()
    f[pl.ds(64, 32), :] = jnp.sum(v["xs"][1].astype(F32), axis=0)
    s_a.wait_recv()
    packets = jnp.concatenate([v["xsa"][k] for k in range(8)], axis=1)
    f[pl.ds(0, 32), :] = nt(packets, v["ge"][...])
    fl[...] = jnp.sum(v["xsa"][...].astype(F32), axis=0)
    f[pl.ds(24, 1), pl.ds(0, 128)] = fl[pl.ds(18, 1), :]
    s_u.wait_recv()
    f[pl.ds(32, 32), :] = jnp.sum(v["xs"][0].astype(F32), axis=0)
    stores.append(pltpu.make_async_copy(f, sum_ref, ls.at[0]))
    stores[4].start()
    for each in (x_a, x_u, x_w, *x_o, *x_do, s_a, s_u, s_w):
        each.wait_send()
    for each in (rs_a, rs_u1, rs_u2, rs_w, *rs_x):
        each.finish()
    for store in stores:
        store.wait()


def final_kernel(out_in, ig_in, f_in, out_ref, ig_ref, dwq_ref, dwo_ref, dwu_ref, dwd_ref, ln_ref, out_v, ig_v, f_ref, sem):
    loads = [
        pltpu.make_async_copy(src, dst, sem.at[i])
        for i, (src, dst) in enumerate(((f_in, f_ref), (ig_in, ig_v), (out_in, out_v)))
    ]
    for load in loads:
        load.start()
    a = pltpu.make_async_copy(out_v, out_ref, sem.at[3])
    b = pltpu.make_async_copy(ig_v, ig_ref, sem.at[4])
    loads[1].wait()
    b.start()
    loads[2].wait()
    a.start()
    loads[0].wait()
    for c in range(3):
        for i in range(6):
            dwq_ref[i, pl.ds(c, 1), :] = f_ref[pl.ds(c * 6 + i, 1), :]
    ln_ref[...] = f_ref[pl.ds(24, 8), :]
    for j in range(4):
        dwu_ref[:, pl.ds(j * 768, 768)] = f_ref[pl.ds(32 + j * 6, 6), :]
    dwo_ref[...] = f_ref[pl.ds(56, 6), :]
    dwd_ref[...] = f_ref[pl.ds(64, 24), :]
    a.wait()
    b.wait()


def on_device(inputs, lengths, qkv_weight, out_weight, up_weight, down_weight, ln1_gain, ln1_bias, ln2_gain, ln2_bias, cotangent):
    sds = jax.ShapeDtypeStruct
    n = plan()[1]
    given = dict(
        x=inputs, dy=cotangent, wq=qkv_weight, wo=out_weight, wu=up_weight, wd=down_weight,
        g1=ln1_gain, b1=ln1_bias, g2=ln2_gain, b2=ln2_bias, len=lengths,
        pa=const(perm_a()), pu=const(perm_u()), pw=const(perm_w()), sm=const(spread_m()), se=const(spread_e()), ge=const(groups_e()),
    )
    out, ig, sums = pl.pallas_call(
        layer_kernel,
        out_shape=(sds((2, 128, 768), BF), sds((2, 128, 768), F32), sds((96, 768), F32)),
        in_specs=[HBM] * len(INPUTS),
        out_specs=[HBM] * 3,
        scratch_shapes=[
            *SCRATCH.values(),
            *SMALL.values(),
            pltpu.VMEM((8, ROWS_A, 128), BF),
            pltpu.VMEM((7, ROWS_A, 128), BF),
            *scatter_scratch(U1, 48, 768),
            *scatter_scratch(U2, 80, 768),
            *scatter_scratch(ROWS_W, CUT_W, 768),
            *scatter_scratch(128, CUT_X, 768, core=False),
            *scatter_scratch(128, CUT_X, 768, core=False),
            pltpu.SemaphoreType.DMA((n,)),
            pltpu.SemaphoreType.DMA((n,)),
            pltpu.SemaphoreType.DMA((23,)),
        ],
        compiler_params=pltpu.CompilerParams(collective_id=0, has_side_effects=True, vmem_limit_bytes=63_000_000),
        name="layer",
    )(*[given[name] for name in INPUTS])
    res = pl.pallas_call(
        final_kernel,
        out_shape=(
            sds((2, 128, 768), BF), sds((2, 128, 768), F32), sds((6, 3, 768), F32), sds((6, 768), F32),
            sds((6, 3072), F32), sds((24, 768), F32), sds((8, 768), F32),
        ),
        in_specs=[HBM] * 3,
        out_specs=[HBM, HBM] + [VM] * 5,
        scratch_shapes=[
            pltpu.VMEM((2, 128, 768), BF),
            pltpu.VMEM((2, 128, 768), F32),
            pltpu.VMEM((96, 768), F32),
            pltpu.SemaphoreType.DMA((5,)),
        ],
        name="final",
    )(out, ig, sums)
    return (*res[:6], *[res[6][0, p * 32 : p * 32 + 6] for p in range(4)])


def solution(mesh):
    both = ("rows", "seq")
    return jax.shard_map(
        on_device,
        mesh=mesh,
        in_specs=(P("rows", "seq", None), P("rows"), P(both, None, None), P(both, None), P(both, None), P(both, None),
                  P(both), P(both), P(both), P(both), P("rows", "seq", None)),
        out_specs=(P("rows", "seq", None), P("rows", "seq", None), P(both, None, None), P(both, None), P(both, None),
                   P(both, None), P(both), P(both), P(both), P(both)),
        check_vma=False,
    )
```

```python
import functools
import math

import jax
import jax.numpy as jnp
import numpy as np
from jax import lax
from jax.experimental import pallas as pl
from jax.experimental.pallas import tpu as pltpu
from jax.sharding import PartitionSpec as P

MESH = pl.DeviceIdType.MESH
BF = jnp.bfloat16
F32 = jnp.float32
HEAD_DIM = 32
EPS = 1e-05
ROWS_A = 160
ROWS_U = 240
ROWS_W = 192
VM = pl.BlockSpec(memory_space=pltpu.VMEM)
SM = pl.BlockSpec(memory_space=pltpu.SMEM)


def perm_a():
    m = np.zeros((ROWS_A, 256), np.float32)
    for s in range(8):
        for c in range(3):
            for i in range(6):
                m[c * 48 + s * 6 + i, s * 32 + c * 6 + i] = 1
        m[144 + s, s * 32 + 18] = 1
    return m


def perm_u():
    m = np.zeros((ROWS_U, 256), np.float32)
    for s in range(8):
        for j in range(5):
            for i in range(6):
                m[j * 48 + s * 6 + i, s * 32 + j * 6 + i] = 1
    return m


def perm_w():
    m = np.zeros((ROWS_W, 256), np.float32)
    for s in range(8):
        for i in range(24):
            m[s * 24 + i, s * 32 + i] = 1
    return m


def spread_m():
    m = np.zeros((256, 768), np.float32)
    for r in range(16):
        for s in range(8):
            m[r * 16 + s, (r * 8 + s) * 6 : (r * 8 + s) * 6 + 6] = 1
    return m


def spread_e():
    m = np.zeros((4, 128, 768), np.float32)
    for p in range(4):
        for j in range(768):
            m[p, p * 32 + j % 6, j] = 1
    return m


def groups_e():
    m = np.zeros((768, 1024), np.float32)
    for j in range(768):
        m[j, j // 96 * 128 + j % 96] = 1
    return m


def const(m):
    return jnp.asarray(m, BF)


def nn(a, b):
    return lax.dot_general(a, b, (((1,), (0,)), ((), ())), preferred_element_type=F32)


def nt(a, b):
    return lax.dot_general(a, b, (((1,), (1,)), ((), ())), preferred_element_type=F32)


def tn(a, b):
    return lax.dot_general(a, b, (((0,), (0,)), ((), ())), preferred_element_type=F32)


class Place:
    def __init__(self):
        self.r = lax.axis_index("rows")
        self.s = lax.axis_index("seq")
        self.z = self.r // 4
        self.y = (self.r // 2) % 2
        self.c = self.r % 2

    def slot(self, dz, dy, dc):
        z = (self.z + dz) % 4
        y = (self.y + dy) % 2
        c = (self.c + dc) % 2
        return z * 4 + y * 2 + c

    def row_dev(self, dz, dy, dc):
        return {"rows": self.slot(dz, dy, dc)}

    def along_seq(self):
        return SeqPlace(self.s)

    def seq_at(self, d):
        return (self.s + d) % 8

    def seq_dev(self, d):
        return {"seq": self.seq_at(d)}


class SeqPlace:
    def __init__(self, s):
        self.s = s

    def slot(self, dx, dy, dc):
        return (self.s // 4 + dy) % 2 * 4 + (self.s + dx) % 4

    def row_dev(self, dx, dy, dc):
        return {"seq": self.slot(dx, dy, dc)}


NEAR = ((1, 0), (3, 0), (0, 1), (1, 1), (3, 1), (2, 0), (2, 1))
ROW_PEERS = ((0, 0, 1), *[(dz, dy, 0) for dz, dy in NEAR])


def barrier_signal(me):
    sem = pltpu.get_barrier_semaphore()
    for p in ROW_PEERS:
        pl.semaphore_signal(sem, inc=1, device_id=me.row_dev(*p), device_id_type=MESH)
    for d in range(1, 8):
        pl.semaphore_signal(sem, inc=1, device_id=me.seq_dev(d), device_id_type=MESH)


def barrier_wait():
    pl.semaphore_wait(pltpu.get_barrier_semaphore(), len(ROW_PEERS) + 7)


def remote(src, dst, ss, rs, dev):
    return pltpu.make_async_remote_copy(
        src_ref=src, dst_ref=dst, send_sem=ss, recv_sem=rs, device_id=dev, device_id_type=MESH
    )


class Exchange:
    def __init__(self, me, src, dst, land, ss, rs, base):
        self.me, self.src, self.dst, self.land = me, src, dst, land
        self.ss, self.rs, self.base = ss, rs, base

    def _copy(self, d):
        return remote(
            self.src(d),
            self.dst(d),
            self.ss.at[self.base + d - 1],
            self.rs.at[self.base + d - 1],
            self.me.seq_dev(d),
        )

    def start(self):
        for d in range(1, 8):
            self._copy(d).start()

    def wait_recv(self):
        for d in range(1, 8):
            here = self.land(d)
            remote(
                here, here, self.ss.at[self.base + d - 1], self.rs.at[self.base + d - 1], self.me.seq_dev(d)
            ).wait_recv()

    def wait_send(self):
        for d in range(1, 8):
            self._copy(d).wait_send()


GATHER_SEMS = 17


class RowsGather:
    def __init__(self, me, buf, cut, ss, rs, base, core=True):
        self.me, self.buf, self.cut, self.core = me, buf, cut, core
        self.ss, self.rs, self.base = ss, rs, base
        self.sent = []

    def _part(self, rel, part):
        slot = self.me.slot(*rel)
        full = self.buf.shape[1]
        if part == 0:
            return self.buf.at[slot]
        if part == 1:
            return self.buf.at[slot, pl.ds(0, self.cut)]
        return self.buf.at[slot, pl.ds(self.cut, full - self.cut)]

    PLAN = {
        "y": (0, (0, 1, 0), (0, 0, 0), 0),
        "p0": (1, (1, 0, 0), (0, 0, 0), 0),
        "m0": (2, (3, 0, 0), (0, 0, 0), 0),
        "p1": (3, (1, 0, 0), (0, 1, 0), 0),
        "m1": (4, (3, 0, 0), (0, 1, 0), 0),
        "fp0": (5, (1, 0, 0), (3, 0, 0), 1),
        "fm0": (6, (3, 0, 0), (1, 0, 0), 2),
        "fp1": (7, (1, 0, 0), (3, 1, 0), 1),
        "fm1": (8, (3, 0, 0), (1, 1, 0), 2),
        "c00": (9, (0, 0, 1), (0, 0, 0), 0),
        "c01": (10, (0, 0, 1), (0, 1, 0), 0),
        "c10": (11, (0, 0, 1), (1, 0, 0), 0),
        "c11": (12, (0, 0, 1), (1, 1, 0), 0),
        "c20": (13, (0, 0, 1), (2, 0, 0), 0),
        "c21": (14, (0, 0, 1), (2, 1, 0), 0),
        "c30": (15, (0, 0, 1), (3, 0, 0), 0),
        "c31": (16, (0, 0, 1), (3, 1, 0), 0),
    }

    def _send(self, name):
        i, to, block, part = self.PLAN[name]
        ref = self._part(block, part)
        return remote(ref, ref, self.ss.at[self.base + i], self.rs.at[self.base + i], self.me.row_dev(*to))

    def send(self, *names):
        for name in names:
            if self.core or name[0] != "c":
                self._send(name).start()
                self.sent.append(name)

    def recv(self, *names):
        for name in names:
            i, to, block, part = self.PLAN[name]
            rel = ((block[0] - to[0]) % 4, (block[1] - to[1]) % 2, (block[2] - to[2]) % 2)
            ref = self._part(rel, part)
            remote(ref, ref, self.ss.at[self.base + i], self.rs.at[self.base + i], self.me.row_dev(*to)).wait_recv()

    def step0(self):
        self.send("p0", "m0", "y", "c00")

    def step1(self):
        self.recv("y")
        self.send("p1", "m1", "c01")

    def step2(self):
        self.recv("p0")
        self.send("fp0", "c30")
        self.recv("m0")
        self.send("fm0", "c10")

    def step3(self):
        self.recv("p1")
        self.send("fp1", "c31")
        self.recv("m1")
        self.send("fm1", "c11")

    def step4(self):
        self.recv("fp0", "fm0")
        self.send("c20")

    def step5(self):
        self.recv("fp1", "fm1")
        self.send("c21")

    def step6(self):
        self.recv("c00", "c01", "c10", "c11", "c20", "c21", "c30", "c31")

    def finish(self):
        for name in self.sent:
            self._send(name).wait_send()


class RowsScatter:
    def __init__(self, me, g, cr, zlo, zhi, zr, yr, ss, rs, base, first=0):
        self.me, self.g, self.cr, self.zlo, self.zhi, self.zr, self.yr = me, g, cr, zlo, zhi, zr, yr
        self.ss, self.rs, self.base = ss, rs, base
        cut, rows = zlo.shape[1], yr.shape[0]
        self.all, self.lo, self.hi = pl.ds(first, rows), pl.ds(first, cut), pl.ds(first + cut, rows - cut)
        self.open = []

    def _copy(self, i, src, dst, to):
        return remote(src, dst, self.ss.at[self.base + i], self.rs.at[self.base + i], self.me.row_dev(*to))

    def _start(self, i, src, dst, to):
        copy = self._copy(i, src, dst, to)
        copy.start()
        self.open.append(copy)

    def _landed(self, i, dst, to):
        self._copy(i, dst, dst, to).wait_recv()

    ORDER = ((2, 0), (2, 1), (1, 0), (1, 1), (3, 0), (3, 1), (0, 1), (0, 0))

    def start_core(self):
        for k, (dz, dy) in enumerate(self.ORDER):
            self._start(k, self.g.at[self.me.slot(dz, dy, 1), self.all], self.cr.at[k], (0, 0, 1))

    def _add(self, k):
        if self.cr is None:
            return
        dz, dy = self.ORDER[k]
        self._landed(k, self.cr.at[k], (0, 0, 1))
        slot = self.me.slot(dz, dy, 0)
        self.g[slot, self.all] = (self.g[slot, self.all].astype(F32) + self.cr[k].astype(F32)).astype(BF)

    def add_far(self):
        for dy in (0, 1):
            self._add(dy)
            slot = self.me.slot(2, dy, 0)
            self._start(8 + dy, self.g.at[slot, self.lo], self.zlo.at[dy], (1, 0, 0))
            self._start(10 + dy, self.g.at[slot, self.hi], self.zhi.at[dy], (3, 0, 0))

    def add_near(self):
        for k in (2, 3, 4, 5):
            self._add(k)

    def pass_near(self):
        for dy in (1, 0):
            self._landed(8 + dy, self.zlo.at[dy], (1, 0, 0))
            slot = self.me.slot(1, dy, 0)
            self.g[slot, self.lo] = (self.g[slot, self.lo].astype(F32) + self.zlo[dy].astype(F32)).astype(BF)
            self._start(12 + 2 * dy, self.g.at[slot, self.all], self.zr.at[0, dy], (1, 0, 0))
            self._landed(10 + dy, self.zhi.at[dy], (3, 0, 0))
            slot = self.me.slot(3, dy, 0)
            self.g[slot, self.hi] = (self.g[slot, self.hi].astype(F32) + self.zhi[dy].astype(F32)).astype(BF)
            self._start(13 + 2 * dy, self.g.at[slot, self.all], self.zr.at[1, dy], (3, 0, 0))

    def own_core(self):
        self._add(6)
        self._add(7)

    def cross(self):
        self._landed(14, self.zr.at[0, 1], (1, 0, 0))
        self._landed(15, self.zr.at[1, 1], (3, 0, 0))
        slot = self.me.slot(0, 1, 0)
        total = self.g[slot, self.all].astype(F32) + self.zr[0, 1].astype(F32) + self.zr[1, 1].astype(F32)
        self.g[slot, self.all] = total.astype(BF)
        self._start(16, self.g.at[slot, self.all], self.yr, (0, 1, 0))

    def last(self):
        self._landed(12, self.zr.at[0, 0], (1, 0, 0))
        self._landed(13, self.zr.at[1, 0], (3, 0, 0))
        self._landed(16, self.yr, (0, 1, 0))
        slot = self.me.slot(0, 0, 0)
        return (
            self.g[slot, self.all].astype(F32)
            + self.zr[0, 0].astype(F32)
            + self.zr[1, 0].astype(F32)
            + self.yr[...].astype(F32)
        )

    def finish(self):
        for copy in self.open:
            copy.wait_send()


SCATTER_SEMS = 17


class DirectGather:
    SEMS = 15

    def __init__(self, me, buf, ss, rs, base):
        self.me, self.buf, self.ss, self.rs, self.base = me, buf, ss, rs, base
        self.open = []

    def _copy(self, i, rel, to):
        block = self.buf.at[self.me.slot(*rel)]
        return remote(block, block, self.ss.at[self.base + i], self.rs.at[self.base + i], self.me.row_dev(*to))

    def _start(self, i, rel, to):
        copy = self._copy(i, rel, to)
        copy.start()
        self.open.append(copy)

    def start(self):
        for k, (dz, dy) in enumerate(NEAR):
            self._start(k, (0, 0, 0), (dz, dy, 0))
        self._start(7, (0, 0, 0), (0, 0, 1))

    def share(self):
        for k, (dz, dy) in enumerate(NEAR):
            self._copy(k, (4 - dz, dy, 0), (dz, dy, 0)).wait_recv()
            self._start(8 + k, (4 - dz, dy, 0), (0, 0, 1))

    def wait(self):
        self._copy(7, (0, 0, 1), (0, 0, 1)).wait_recv()
        for k, (dz, dy) in enumerate(NEAR):
            self._copy(8 + k, (4 - dz, dy, 1), (0, 0, 1)).wait_recv()

    def finish(self):
        for copy in self.open:
            copy.wait_send()


class DirectScatter:
    SEMS = 15

    def __init__(self, me, g, cr, dr, ss, rs, base):
        self.me, self.g, self.cr, self.dr, self.ss, self.rs, self.base = me, g, cr, dr, ss, rs, base
        self.open = []

    def _copy(self, i, src, dst, to):
        return remote(src, dst, self.ss.at[self.base + i], self.rs.at[self.base + i], self.me.row_dev(*to))

    def _start(self, i, src, dst, to):
        copy = self._copy(i, src, dst, to)
        copy.start()
        self.open.append(copy)

    def start_core(self):
        for k, (dz, dy) in enumerate((*NEAR, (0, 0))):
            self._start(k, self.g.at[self.me.slot(dz, dy, 1)], self.cr.at[k], (0, 0, 1))

    def send(self):
        for k, (dz, dy) in enumerate((*NEAR, (0, 0))):
            self._copy(k, self.cr.at[k], self.cr.at[k], (0, 0, 1)).wait_recv()
            slot = self.me.slot(dz, dy, 0)
            self.g[slot] = (self.g[slot].astype(F32) + self.cr[k].astype(F32)).astype(BF)
            if k < 7:
                self._start(8 + k, self.g.at[slot], self.dr.at[k], (dz, dy, 0))

    def last(self):
        total = self.g[self.me.slot(0, 0, 0)].astype(F32)
        for k, (dz, dy) in enumerate(NEAR):
            self._copy(8 + k, self.dr.at[k], self.dr.at[k], (dz, dy, 0)).wait_recv()
            total += self.dr[k].astype(F32)
        return total

    def finish(self):
        for copy in self.open:
            copy.wait_send()


def small_vec(refs):
    lane = lax.broadcasted_iota(jnp.int32, (1, 128), 1)
    out = jnp.zeros((1, 128), F32)
    for p, ref in enumerate(refs):
        for i in range(6):
            out = jnp.where(lane == p * 32 + i, ref[i], out)
    return out


def normalise(v):
    mean = jnp.mean(v, axis=-1, keepdims=True)
    centred = v - mean
    var = jnp.mean(centred * centred, axis=-1, keepdims=True)
    inverse = lax.rsqrt(var + EPS)
    return centred * inverse, inverse


SCALE = HEAD_DIM**-0.5
LOG2E = 1.4426950408889634
BASE = (0, 256, 768, 1536)


def lanes(ref, b, c, h, first, count):
    rows = pl.ds(pl.multiple_of(h * 32, 32), 32)
    if c is None:
        parts = [ref[b, first + i, rows, :] for i in range(count)]
    else:
        parts = [ref[b, first + i, c, rows, :] for i in range(count)]
    return parts[0] if count == 1 else jnp.concatenate(parts, axis=1)


def allowed(nk, length):
    key = lax.broadcasted_iota(jnp.int32, (nk, 256), 0)
    query = lax.broadcasted_iota(jnp.int32, (nk, 256), 1) + (nk - 256)
    return (key <= query) & (key < length)


def attend_one(heads_ref, length, p_ref, l_ref, os_ref, b, h, i):
    rows = pl.ds(pl.multiple_of(h * 32, 32), 32)
    kt = lanes(heads_ref, b, 1, h, 0, 8)
    vt = lanes(heads_ref, b, 2, h, 0, 8)
    for qb in range(4):
        nk = (qb + 1) * 256
        qt = lanes(heads_ref, b, 0, h, 2 * qb, 2)
        s = tn(kt[:, :nk], qt)
        s = jnp.where(allowed(nk, length), s, -1e30)
        top = jnp.max(s, axis=0, keepdims=True)
        p = jnp.exp2((s - top) * (SCALE * LOG2E))
        inverse = 1.0 / jnp.sum(p, axis=0, keepdims=True)
        low = p.astype(BF)
        p_ref[i, pl.ds(BASE[qb], nk), :] = low
        l_ref[i, pl.ds(qb, 1), :] = inverse
        o = (nn(vt[:, :nk], low) * inverse).astype(BF)
        os_ref[b, 2 * qb, rows, :] = o[:, :128]
        os_ref[b, 2 * qb + 1, rows, :] = o[:, 128:]


def attend_one_back(heads_ref, p_ref, l_ref, os_ref, do_ref, dq_ref, acc_ref, b, h, i):
    rows = pl.ds(pl.multiple_of(h * 32, 32), 32)
    kt = lanes(heads_ref, b, 1, h, 0, 8)
    vt = lanes(heads_ref, b, 2, h, 0, 8)
    for qb in range(4):
        nk = (qb + 1) * 256
        qt = lanes(heads_ref, b, 0, h, 2 * qb, 2)
        do = lanes(do_ref, b, None, h, 2 * qb, 2).astype(F32) * l_ref[i, pl.ds(qb, 1), :]
        o = lanes(os_ref, b, None, h, 2 * qb, 2).astype(F32)
        delta = jnp.sum(do * o, axis=0, keepdims=True)
        low = do.astype(BF)
        p = p_ref[i, pl.ds(BASE[qb], nk), :]
        ds = (p.astype(F32) * (tn(vt[:, :nk], low) - delta)).astype(BF)
        dv = nt(low, p)
        dk = nt(qt, ds)
        if nk > 256:
            acc_ref[0, :, : nk - 256] += dk[:, : nk - 256]
            acc_ref[1, :, : nk - 256] += dv[:, : nk - 256]
        acc_ref[0, :, nk - 256 : nk] = dk[:, nk - 256 :]
        acc_ref[1, :, nk - 256 : nk] = dv[:, nk - 256 :]
        dq = (nn(kt[:, :nk], ds) * SCALE).astype(BF)
        dq_ref[2 * qb, 0, rows, :] = dq[:, :128]
        dq_ref[2 * qb + 1, 0, rows, :] = dq[:, 128:]
    for j in range(8):
        dq_ref[j, 1, rows, :] = (acc_ref[0, :, j * 128 : (j + 1) * 128] * SCALE).astype(BF)
        dq_ref[j, 2, rows, :] = acc_ref[1, :, j * 128 : (j + 1) * 128].astype(BF)


def feed_forward(first, end, gu_ref, gw_ref, h2_ref, dy_ref, y_ref, dh_ref):
    def block(j, carry):
        up = pl.ds(pl.multiple_of(j * 48, 16), 48)
        deep = pl.ds(j * 4, 4)
        wu = gu_ref[:, up, :].reshape(768, 768)
        h2 = h2_ref[...]
        u = nn(h2, wu)
        phi = 0.5 + 0.5 * lax.erf(u * (1.0 / math.sqrt(2.0)))
        act = (u * phi).astype(BF)
        slope = phi + u * jnp.exp(-0.5 * u * u) * (1.0 / math.sqrt(2.0 * math.pi))
        wd = gw_ref[deep].reshape(768, 768)
        dy = dy_ref[...].reshape(256, 768)
        y_ref[...] += nn(act, wd)
        du = (nt(dy, wd) * slope).astype(BF)
        gw_ref[deep] = tn(act, dy).astype(BF).reshape(4, 192, 768)
        dh_ref[...] += nt(du, wu)
        gu_ref[:, up, :] = tn(h2, du).astype(BF).reshape(16, 48, 768)
        return carry

    lax.fori_loop(first, end, block, 0)


def norm_parts(grad, gain, scaled, inverse):
    weighted = grad * gain
    first = jnp.mean(weighted, axis=-1, keepdims=True)
    second = jnp.mean(weighted * scaled, axis=-1, keepdims=True)
    grad_in = inverse * (weighted - first - scaled * second)
    return grad_in, jnp.sum(grad * scaled, axis=0, keepdims=True), jnp.sum(grad, axis=0, keepdims=True)


HBM = pl.BlockSpec(memory_space=pl.ANY)


class Counter:
    def __init__(self):
        self.n = 0

    def take(self, k):
        first = self.n
        self.n += k
        return first


def plan():
    c = Counter()
    at = {}
    for name in ("xa", "xu", "xw", "sa", "su", "sw"):
        at[name] = c.take(7)
    for name in ("ga", "gu", "gw", "gx0", "gx1"):
        at[name] = c.take(GATHER_SEMS)
    for name in ("o", "do"):
        at[name] = c.take(14)
    for name in ("ra", "ru1", "ru2", "rw", "rx0", "rx1"):
        at[name] = c.take(SCATTER_SEMS)
    return at, c.n


def scatter_scratch(rows, cut, wide, core=True):
    made = [
        pltpu.VMEM((2, cut, wide), BF),
        pltpu.VMEM((2, rows - cut, wide), BF),
        pltpu.VMEM((2, 2, rows, wide), BF),
        pltpu.VMEM((rows, wide), BF),
    ]
    return ([pltpu.VMEM((8, rows, wide), BF)] if core else []) + made


CUT_U, CUT_W, CUT_X = 128, 96, 64
U1, U2 = 96, 144
SCRATCH = dict(
    xl=pltpu.VMEM((2, 8, 128, 768), BF),
    h1=pltpu.VMEM((2, 8, 128, 768), BF),
    dy=pltpu.VMEM((2, 128, 768), BF),
    wq=pltpu.VMEM((6, 3, 768), F32),
    wo=pltpu.VMEM((6, 768), F32),
    wu=pltpu.VMEM((6, 3072), F32),
    wd=pltpu.VMEM((24, 768), F32),
    pa=pltpu.VMEM((ROWS_A, 256), BF),
    pu=pltpu.VMEM((ROWS_U, 256), BF),
    pw=pltpu.VMEM((ROWS_W, 256), BF),
    sm=pltpu.VMEM((256, 768), BF),
    se=pltpu.VMEM((4, 128, 768), BF),
    ge=pltpu.VMEM((768, 1024), BF),
    f=pltpu.VMEM((96, 768), F32),
    fl=pltpu.VMEM((32, 128), F32),
    ka=pltpu.VMEM((8, 32, 128), BF),
    k=pltpu.VMEM((2, 32, 768), BF),
    xa=pltpu.VMEM((8, 32, 128), BF),
    xu=pltpu.VMEM((8, 32, 768), BF),
    xw=pltpu.VMEM((8, 32, 768), BF),
    ga=pltpu.VMEM((16, ROWS_A, 128), BF),
    gu=pltpu.VMEM((16, ROWS_U, 768), BF),
    gw=pltpu.VMEM((16, ROWS_W, 768), BF),
    lnp=pltpu.VMEM((8, 768), F32),
    wt=pltpu.VMEM((288, 768), BF),
    dwt=pltpu.VMEM((3, 128, 768), F32),
    xhat=pltpu.VMEM((256, 768), F32),
    inv=pltpu.VMEM((256, 1), F32),
    heads=pltpu.VMEM((2, 8, 3, 96, 128), BF),
    p=pltpu.VMEM((6, 2560, 256), BF),
    l=pltpu.VMEM((6, 4, 256), F32),
    os=pltpu.VMEM((2, 8, 96, 128), BF),
    ot=pltpu.VMEM((2, 8, 96, 128), BF),
    h2=pltpu.VMEM((256, 768), BF),
    xh2=pltpu.VMEM((256, 768), F32),
    y=pltpu.VMEM((256, 768), F32),
    dh=pltpu.VMEM((256, 768), F32),
    dot=pltpu.VMEM((2, 8, 96, 128), BF),
    do=pltpu.VMEM((2, 8, 96, 128), BF),
    acc=pltpu.VMEM((2, 32, 1024), F32),
    dq=pltpu.VMEM((8, 3, 96, 128), BF),
    lng=pltpu.VMEM((8, 768), F32),
    xsa=pltpu.VMEM((8, 32, 128), BF),
    xs=pltpu.VMEM((2, 8, 32, 768), BF),
)
SMALL = dict(
    len=pltpu.SMEM((2,), jnp.int32),
    g1=pltpu.SMEM((6,), F32),
    b1=pltpu.SMEM((6,), F32),
    g2=pltpu.SMEM((6,), F32),
    b2=pltpu.SMEM((6,), F32),
)
INPUTS = ("x", "wq", "g1", "b1", "g2", "b2", "ge", "wu", "wo", "wd", "pa", "pu", "pw", "sm", "se", "dy", "len")


def feature_major(ref, b):
    return ref[b].reshape(768, 128)


def layer_kernel(*refs):
    inputs = dict(zip(INPUTS, refs))
    refs = refs[len(INPUTS) :]
    out_ref, ig_ref, sum_ref = refs[:3]
    names = [*SCRATCH, *SMALL]
    v = dict(zip(names, refs[3 : 3 + len(names)]))
    rest = refs[3 + len(names) :]
    scr_a, scr_u1, scr_u2, scr_w = rest[:2], rest[2:7], rest[7:12], rest[12:17]
    scr_x = (rest[17:21], rest[21:25])
    ss, rs, ls = rest[25:]
    at, _ = plan()
    me = Place()
    seq = me.along_seq()
    barrier_signal(me)
    xl = v["xl"]
    loads = {}
    for b in range(2):
        loads[b] = pltpu.make_async_copy(inputs["x"].at[b], xl.at[b, me.s], ls.at[21 + b])
        loads[b].start()
    for i, name in enumerate(INPUTS):
        if name != "x":
            loads[name] = pltpu.make_async_copy(inputs[name], v[name], ls.at[i])
            loads[name].start()

    def loaded(*which):
        for name in which:
            loads[name].wait()

    def seq_gather(src, dst, key):
        made = Exchange(me, lambda d: src, lambda d: dst.at[me.s], lambda d: dst.at[me.seq_at(8 - d)], ss, rs, at[key])
        made.start()
        dst[me.s] = src[...]
        return made

    def seq_scatter(src, dst, key):
        made = Exchange(
            me, lambda d: src.at[me.seq_at(d)], lambda d: dst.at[me.s], lambda d: dst.at[me.seq_at(8 - d)], ss, rs, at[key]
        )
        made.start()
        dst[me.s] = src[me.s]
        return made

    def by_row(src, dst, key):
        return [
            Exchange(
                me,
                lambda d, b=b: src.at[b, me.seq_at(d)],
                lambda d, b=b: dst.at[b, me.s],
                lambda d, b=b: dst.at[b, me.seq_at(8 - d)],
                ss,
                rs,
                at[key] + 7 * b,
            )
            for b in range(2)
        ]

    f, fl = v["f"], v["fl"]
    f[...] = jnp.zeros_like(f)
    fl[...] = jnp.zeros_like(fl)
    ga, gu, gw = v["ga"], v["gu"], v["gw"]
    ag_x = [RowsGather(seq, xl.at[b], CUT_X, ss, rs, at[f"gx{b}"], core=False) for b in range(2)]
    ag_a = DirectGather(me, ga, ss, rs, at["ga"])
    ag_u = RowsGather(me, gu, CUT_U, ss, rs, at["gu"])
    ag_w = RowsGather(me, gw, CUT_W, ss, rs, at["gw"])
    loaded("wq", "g1", "b1", "g2", "b2", "ge")
    for c in range(3):
        for i in range(6):
            f[pl.ds(c * 6 + i, 1), :] = v["wq"][i, pl.ds(c, 1), :]
    fl[pl.ds(18, 1), :] = small_vec([v[name] for name in ("g1", "b1", "g2", "b2")])
    wide = nn(f[pl.ds(0, 32), :].astype(BF), v["ge"][...])
    for k in range(8):
        v["ka"][k] = (wide[:, k * 128 : (k + 1) * 128] + fl[...]).astype(BF)
    loaded("wu", "wo", "wd")
    for j in range(4):
        f[pl.ds(32 + j * 6, 6), :] = v["wu"][:, pl.ds(j * 768, 768)]
    f[pl.ds(56, 6), :] = v["wo"][...]
    f[pl.ds(64, 24), :] = v["wd"][...]
    v["k"][0] = f[pl.ds(32, 32), :].astype(BF)
    v["k"][1] = f[pl.ds(64, 32), :].astype(BF)
    loaded(0, 1, "pa", "pu", "pw", "sm", "se", "dy", "len")
    barrier_wait()
    x_a = seq_scatter(v["ka"], v["xa"], "xa")
    x_u = seq_gather(v["k"].at[0], v["xu"], "xu")
    x_w = seq_gather(v["k"].at[1], v["xw"], "xw")
    ag_x[0].step0()
    x_a.wait_recv()
    ga[me.r] = nn(v["pa"][...], v["xa"][...].reshape(256, 128)).astype(BF)
    ag_a.start()
    x_u.wait_recv()
    gu[me.r] = nn(v["pu"][...], v["xu"][...].reshape(256, 768)).astype(BF)
    ag_u.step0()
    ag_a.share()
    x_w.wait_recv()
    gw[me.r] = nn(v["pw"][...], v["xw"][...].reshape(256, 768)).astype(BF)
    ag_w.step0()
    ag_x[0].step1()
    ag_x[0].step2()
    ag_x[1].step0()
    for b in range(2):
        xhat, inverse = normalise(xl[b, me.s].astype(F32))
        v["xhat"][pl.ds(b * 128, 128), :] = xhat
        v["inv"][pl.ds(b * 128, 128), :] = inverse
    ag_a.wait()
    ag_u.step1()

    lnp = v["lnp"]
    ln = ga[:, pl.ds(144, 16), :].reshape(256, 128)
    for p in range(4):
        spread = nn(ln, v["se"][p])
        lnp[pl.ds(p, 1), :] = jnp.sum(spread * v["sm"][...].astype(F32), axis=0, keepdims=True)
    for c in range(3):
        w = ga[:, pl.ds(c * 48, 48), :].reshape(768, 128)
        v["wt"][pl.ds(c * 96, 96), :] = w.T[:96]

    def prepare(b, slot):
        xhat, _ = normalise(xl[b, slot].astype(F32))
        h = (xhat * lnp[pl.ds(0, 1), :] + lnp[pl.ds(1, 1), :]).astype(BF)
        v["h1"][b, slot] = h
        v["heads"][b, slot] = nt(v["wt"][...], h).astype(BF).reshape(3, 96, 128)

    def prepare_pair(b, dx, dy, step_x, step_y):
        def one(i, carry):
            prepare(b, seq.slot(dx + i * step_x, dy + i * step_y, 0))
            return carry

        lax.fori_loop(0, 2, one, 0)

    x_o = by_row(v["os"], v["ot"], "o")

    def forward(b):
        def one(h, carry):
            attend_one(v["heads"], v["len"][b], v["p"], v["l"], v["os"], b, h, b * 3 + h)
            return carry

        lax.fori_loop(0, 3, one, 0)
        x_o[b].start()
        v["ot"][b, me.s] = v["os"][b, me.s]

    prepare_pair(0, 0, 0, 0, 1)
    ag_x[0].step3()
    prepare_pair(0, 1, 0, 2, 0)
    prepare_pair(0, 1, 1, 2, 0)
    ag_w.step1()
    ag_x[1].step1()
    ag_x[0].step4()
    ag_x[0].step5()
    prepare_pair(0, 2, 0, 0, 1)
    ag_x[1].step2()
    ag_u.step2()
    forward(0)
    ag_w.step2()
    ag_x[1].step3()
    prepare_pair(1, 0, 0, 0, 1)
    prepare_pair(1, 1, 0, 2, 0)
    prepare_pair(1, 1, 1, 2, 0)
    ag_u.step3()
    ag_x[1].step4()
    ag_x[1].step5()
    prepare_pair(1, 2, 0, 0, 1)
    ag_w.step3()
    forward(1)
    ag_u.step4()
    ag_u.step5()
    for b in range(2):
        x_o[b].wait_recv()
    ag_u.step6()

    ot = jnp.concatenate([feature_major(v["ot"], b) for b in range(2)], axis=1)
    wo = gu[:, pl.ds(192, 48), :].reshape(768, 768)
    x1 = jnp.concatenate([xl[b, me.s] for b in range(2)], axis=0).astype(F32) + tn(ot, wo)
    xhat2, inverse2 = normalise(x1)
    v["xh2"][...] = xhat2
    v["h2"][...] = (xhat2 * lnp[pl.ds(2, 1), :] + lnp[pl.ds(3, 1), :]).astype(BF)
    v["y"][...] = x1
    v["dh"][...] = jnp.zeros_like(v["dh"])
    ag_w.step4()
    ag_w.step5()
    ag_w.step6()
    ag_u.finish()
    ag_w.finish()
    rs_u1 = RowsScatter(me, gu, *scr_u1, ss, rs, at["ru1"])
    rs_u2 = RowsScatter(me, gu, *scr_u2, ss, rs, at["ru2"], U1)
    rs_w = RowsScatter(me, gw, *scr_w, ss, rs, at["rw"])
    rs_a = DirectScatter(me, ga, *scr_a, ss, rs, at["ra"])
    feed_forward(0, 2, gu, gw, v["h2"], v["dy"], v["y"], v["dh"])
    rs_u1.start_core()
    feed_forward(2, 4, gu, gw, v["h2"], v["dy"], v["y"], v["dh"])
    rs_w.start_core()
    rs_u1.add_far()
    rs_u1.add_near()
    grad_in, gg2, gb2 = norm_parts(v["dh"][...], lnp[pl.ds(2, 1), :], v["xh2"][...], inverse2)
    v["lng"][pl.ds(2, 1), :] = gg2
    v["lng"][pl.ds(3, 1), :] = gb2
    dx = v["dy"][...].reshape(256, 768).astype(F32) + grad_in
    v["xh2"][...] = dx
    low = dx.astype(BF)
    d = nt(wo, low).astype(BF)
    for k in range(8):
        for b in range(2):
            v["dot"][b, k] = d[k * 96 : (k + 1) * 96, b * 128 : (b + 1) * 128]
    x_do = by_row(v["dot"], v["do"], "do")
    for b in range(2):
        x_do[b].start()
        v["do"][b, me.s] = v["dot"][b, me.s]
    rs_w.add_far()
    rs_u1.pass_near()
    gu[:, pl.ds(192, 48), :] = nn(ot, low).astype(BF).reshape(16, 48, 768)
    rs_u2.start_core()
    rs_w.add_near()
    v["h2"][...] = v["y"][...].astype(BF)
    stores = [pltpu.make_async_copy(v["h2"].at[pl.ds(b * 128, 128)], out_ref.at[b], ls.at[17 + b]) for b in range(2)]
    for b in range(2):
        stores[b].start()
    rs_u2.add_far()
    rs_u2.add_near()

    v["dwt"][...] = jnp.zeros_like(v["dwt"])
    v["lng"][pl.ds(0, 2), :] = jnp.zeros((2, 768), F32)
    dq_ref = v["dq"]

    def one_back(b, slot):
        grad = tn(dq_ref[slot].reshape(288, 128), v["wt"][...])
        v["lng"][pl.ds(0, 1), :] += jnp.sum(grad * v["h1"][b, slot].astype(F32), axis=0, keepdims=True)
        v["lng"][pl.ds(1, 1), :] += jnp.sum(grad, axis=0, keepdims=True)
        xl[b, slot] = grad.astype(BF)

    rs_x = [RowsScatter(seq, xl.at[b], None, *scr_x[b], ss, rs, at[f"rx{b}"]) for b in range(2)]

    def backward(b, between):
        x_do[b].wait_recv()
        ag_x[b].finish()

        def one(h, carry):
            attend_one_back(v["heads"], v["p"], v["l"], v["os"], v["do"], dq_ref, v["acc"], b, h, b * 3 + h)
            return carry

        lax.fori_loop(0, 3, one, 0)
        between()

        def far(i, carry):
            one_back(b, seq.slot(2, i, 0))
            return carry

        def near(i, carry):
            one_back(b, seq.slot((1 + 2 * (i // 2)) % 5, i, 0))
            return carry

        lax.fori_loop(0, 2, far, 0)
        rs_x[b].add_far()
        lax.fori_loop(0, 6, near, 0)
        grad = jnp.concatenate([dq_ref[i].reshape(288, 128) for i in range(8)], axis=1)
        dw = nn(grad, v["h1"][b].reshape(1024, 768))
        for c in range(3):
            v["dwt"][c, pl.ds(0, 96), :] += dw[c * 96 : (c + 1) * 96]

    def between():
        rs_u2.pass_near()
        rs_x[0].pass_near()
        rs_w.own_core()

    backward(0, rs_w.pass_near)
    rs_u1.own_core()
    rs_u1.cross()
    backward(1, between)

    def norm1_back(b):
        rows = pl.ds(b * 128, 128)
        grad = rs_x[b].last()
        grad_in, _, _ = norm_parts(grad, lnp[pl.ds(0, 1), :], v["xhat"][rows, :], v["inv"][rows, :])
        v["xhat"][rows, :] = v["xh2"][rows, :] + grad_in
        stores.append(pltpu.make_async_copy(v["xhat"].at[rows], ig_ref.at[b], ls.at[19 + b]))
        stores[2 + b].start()

    ag_a.finish()
    for c in range(3):
        ga[:, pl.ds(c * 48, 48), :] = v["dwt"][c].T.astype(BF).reshape(16, 48, 128)
    lng = v["lng"]
    lng[pl.ds(0, 1), :] = (lng[pl.ds(0, 1), :] - lnp[pl.ds(1, 1), :] * lng[pl.ds(1, 1), :]) / lnp[pl.ds(0, 1), :]
    parts = jnp.zeros((256, 128), F32)
    for p in range(4):
        parts += nt((v["sm"][...].astype(F32) * lng[pl.ds(p, 1), :]).astype(BF), v["se"][p])
    ga[:, pl.ds(144, 16), :] = parts.astype(BF).reshape(16, 16, 128)
    rs_a.start_core()
    def scatter_rows(ref, perm, rows):
        ref[...] = tn(perm[...], rows.astype(BF)).astype(BF).reshape(ref.shape)

    rs_a.send()
    rs_w.cross()
    rs_x[1].pass_near()
    rs_u2.own_core()
    rs_x[0].cross()
    rs_u2.cross()
    scatter_rows(v["xw"], v["pw"], rs_w.last())
    s_w = seq_scatter(v["xw"], v["xs"].at[1], "sw")
    rs_x[1].cross()
    scatter_rows(v["xa"], v["pa"], rs_a.last())
    s_a = seq_scatter(v["xa"], v["xsa"], "sa")
    norm1_back(0)
    total = jnp.concatenate([rs_u1.last(), rs_u2.last()], axis=0)
    scatter_rows(v["xu"], v["pu"], total)
    s_u = seq_scatter(v["xu"], v["xs"].at[0], "su")
    norm1_back(1)
    s_w.wait_recv()
    f[pl.ds(64, 32), :] = jnp.sum(v["xs"][1].astype(F32), axis=0)
    s_a.wait_recv()
    packets = jnp.concatenate([v["xsa"][k] for k in range(8)], axis=1)
    f[pl.ds(0, 32), :] = nt(packets, v["ge"][...])
    fl[...] = jnp.sum(v["xsa"][...].astype(F32), axis=0)
    f[pl.ds(24, 1), pl.ds(0, 128)] = fl[pl.ds(18, 1), :]
    s_u.wait_recv()
    f[pl.ds(32, 32), :] = jnp.sum(v["xs"][0].astype(F32), axis=0)
    stores.append(pltpu.make_async_copy(f, sum_ref, ls.at[0]))
    stores[4].start()
    for each in (x_a, x_u, x_w, *x_o, *x_do, s_a, s_u, s_w):
        each.wait_send()
    for each in (rs_a, rs_u1, rs_u2, rs_w, *rs_x):
        each.finish()
    for store in stores:
        store.wait()


def final_kernel(out_in, ig_in, f_in, out_ref, ig_ref, dwq_ref, dwo_ref, dwu_ref, dwd_ref, g1_ref, b1_ref, g2_ref, b2_ref, out_v, ig_v, f_ref, sem):
    loads = [
        pltpu.make_async_copy(src, dst, sem.at[i])
        for i, (src, dst) in enumerate(((f_in, f_ref), (ig_in, ig_v), (out_in, out_v)))
    ]
    for load in loads:
        load.start()
    a = pltpu.make_async_copy(out_v, out_ref, sem.at[3])
    b = pltpu.make_async_copy(ig_v, ig_ref, sem.at[4])
    loads[1].wait()
    b.start()
    loads[2].wait()
    a.start()
    loads[0].wait()
    for c in range(3):
        for i in range(6):
            dwq_ref[i, pl.ds(c, 1), :] = f_ref[pl.ds(c * 6 + i, 1), :]
    for p, ref in enumerate((g1_ref, b1_ref, g2_ref, b2_ref)):
        ref[...] = f_ref[24, pl.ds(0, 128)][p * 32 : p * 32 + 6]
    for j in range(4):
        dwu_ref[:, pl.ds(j * 768, 768)] = f_ref[pl.ds(32 + j * 6, 6), :]
    dwo_ref[...] = f_ref[pl.ds(56, 6), :]
    dwd_ref[...] = f_ref[pl.ds(64, 24), :]
    a.wait()
    b.wait()


def on_device(inputs, lengths, qkv_weight, out_weight, up_weight, down_weight, ln1_gain, ln1_bias, ln2_gain, ln2_bias, cotangent):
    sds = jax.ShapeDtypeStruct
    n = plan()[1]
    given = dict(
        x=inputs, dy=cotangent, wq=qkv_weight, wo=out_weight, wu=up_weight, wd=down_weight,
        g1=ln1_gain, b1=ln1_bias, g2=ln2_gain, b2=ln2_bias, len=lengths,
        pa=const(perm_a()), pu=const(perm_u()), pw=const(perm_w()), sm=const(spread_m()), se=const(spread_e()), ge=const(groups_e()),
    )
    out, ig, sums = pl.pallas_call(
        layer_kernel,
        out_shape=(sds((2, 128, 768), BF), sds((2, 128, 768), F32), sds((96, 768), F32)),
        in_specs=[HBM] * len(INPUTS),
        out_specs=[HBM] * 3,
        scratch_shapes=[
            *SCRATCH.values(),
            *SMALL.values(),
            pltpu.VMEM((8, ROWS_A, 128), BF),
            pltpu.VMEM((7, ROWS_A, 128), BF),
            *scatter_scratch(U1, 48, 768),
            *scatter_scratch(U2, 80, 768),
            *scatter_scratch(ROWS_W, CUT_W, 768),
            *scatter_scratch(128, CUT_X, 768, core=False),
            *scatter_scratch(128, CUT_X, 768, core=False),
            pltpu.SemaphoreType.DMA((n,)),
            pltpu.SemaphoreType.DMA((n,)),
            pltpu.SemaphoreType.DMA((23,)),
        ],
        compiler_params=pltpu.CompilerParams(collective_id=0, has_side_effects=True, vmem_limit_bytes=63_000_000),
        name="layer",
    )(*[given[name] for name in INPUTS])
    res = pl.pallas_call(
        final_kernel,
        out_shape=(
            sds((2, 128, 768), BF), sds((2, 128, 768), F32), sds((6, 3, 768), F32), sds((6, 768), F32),
            sds((6, 3072), F32), sds((24, 768), F32), *[sds((6,), F32)] * 4,
        ),
        in_specs=[HBM] * 3,
        out_specs=[HBM, HBM] + [VM] * 8,
        scratch_shapes=[
            pltpu.VMEM((2, 128, 768), BF),
            pltpu.VMEM((2, 128, 768), F32),
            pltpu.VMEM((96, 768), F32),
            pltpu.SemaphoreType.DMA((5,)),
        ],
        name="final",
    )(out, ig, sums)
    return res


def solution(mesh):
    both = ("rows", "seq")
    return jax.shard_map(
        on_device,
        mesh=mesh,
        in_specs=(P("rows", "seq", None), P("rows"), P(both, None, None), P(both, None), P(both, None), P(both, None),
                  P(both), P(both), P(both), P(both), P("rows", "seq", None)),
        out_specs=(P("rows", "seq", None), P("rows", "seq", None), P(both, None, None), P(both, None), P(both, None),
                   P(both, None), P(both), P(both), P(both), P(both)),
        check_vma=False,
    )
```
